32 devices in a mesh: ctx: 16 (over z, y, x), dp: 2 (over core).
Axes of the slice: x: 2, y: 2, z: 4, core: 2. Of those that a mesh axis runs over, the one named last changes fastest.
Arguments:
- queries: bfloat16 [2048, 2048], P('ctx', 'dp'), may hold values from -192 to 192
- keys: bfloat16 [2048, 128], P('ctx'), may hold values from -32 to 32
- values: bfloat16 [2048, 128], P('ctx'), may hold values from -6 to 6
- out_grads: bfloat16 [2048, 2048], P('ctx', 'dp'), may hold values from -6 to 6
- doc_lengths: int32 [8], replicated, may hold values from 1 to 1152, 2048 in all
Outputs:
- query_grads: bfloat16 [2048, 2048], P('ctx', 'dp')
- key_grads: bfloat16 [2048, 128], P(('ctx', 'dp'))
- value_grads: bfloat16 [2048, 128], P(('ctx', 'dp'))
The draws below stay inside these ranges and needn't reach their ends.
Inputs may be any that keep to these rules, and one draw needn't show every extreme that they name: `doc_lengths`: document lengths in order of position; they sum to 2048 and the longest document has exactly 1152 tokens.
All inputs are finite; a program needn't handle non-finite values.
Results may differ from the reference program's by a relative error of at most 0.023.
Values may be sent and summed in bfloat16 or wider, within the bound.
No kernel may reach another device: no remote copies, remote signals or barrier semaphores. Data moves between devices by JAX's collectives and lax.ppermute only.
A program may use at most 64 MiB of HBM per device.

```python
import math
import jax
import jax.numpy as jnp
import numpy as np
from jax import lax

HD = 128
GROUP = 16
TOK_DEV = 128
SPAN = 64
NCHUNK = 32
SEQ = 2048
MAXDOC = 1152
NDOCS = 8


def key_table(key):
    noise_rows = jnp.clip(jax.random.normal(jax.random.fold_in(key, 101), (SEQ, HD), jnp.float32), -6.0, 6.0)
    return noise_rows


def draw_keys(key, part):
    return key_table(key).astype(jnp.bfloat16)


def draw_queries(key, part):
    base_rows = jnp.clip(jax.random.normal(jax.random.fold_in(key, 201), (SEQ, GROUP, HD), jnp.float32), -6.0, 6.0)
    return base_rows.reshape(SEQ, GROUP * HD).astype(jnp.bfloat16)


def steps_of(stream_key, extent, shards, low, top_value):
    def one(dim, parts):
        steps = jax.random.uniform(jax.random.fold_in(jax.random.fold_in(stream_key, 6), dim), (parts,), jnp.float32, low / len(shards), top_value / len(shards))
        return jnp.repeat(jnp.exp(steps), extent[dim] // parts).reshape((-1,) + (1,) * (len(extent) - dim - 1))

    factor_of = one(*shards[0])
    for cut in shards[1:]:
        factor_of = factor_of * one(*cut)
    return factor_of


def profile(number_of, total, limit, lean):
    loads = [(1 << 20) // math.isqrt(rank ** lean) + 1 for rank in range(2, number_of + 1)]
    rest, holding = total - limit - (number_of - 1), [1] * (number_of - 1)
    while rest > 0:
        free = [i for i in range(number_of - 1) if holding[i] < limit]
        pool, remaining = sum([loads[i] for i in free]), rest
        for i in free:
            extra = min(limit - holding[i], max(1, remaining * loads[i] // pool), rest)
            holding[i] = holding[i] + extra
            rest = rest - extra
    return np.array([limit] + holding)


def ragged_sizes(stream_key, count, total, bound, slope):
    if count == 2:
        one = jax.random.randint(stream_key, (), max(1, total - bound), min(bound, total - 1) + 1)
        return jnp.stack([one, total - one])
    lengths = jnp.asarray(profile(count, total, bound, slope), jnp.int32)
    pairs = (count - 1) // 2
    source_of, taker = lengths[1:1 + 2 * pairs:2], lengths[2:2 + 2 * pairs:2]
    margin = jnp.minimum(source_of - 1, bound - taker)
    shifted = jax.random.randint(jax.random.fold_in(stream_key, 1), (pairs,), 0, 1 << 20) % (margin + 1)
    lengths = lengths.at[1:1 + 2 * pairs:2].set(source_of - shifted).at[2:2 + 2 * pairs:2].set(taker + shifted)
    return lengths[jax.random.permutation(jax.random.fold_in(stream_key, 2), count)]


def gaussian(key, extent, deviation, limit, cuts=(), held_as=jnp.bfloat16):
    entries = deviation * jax.random.normal(key, extent, jnp.float32)
    if cuts:
        entries = entries * steps_of(key, extent, cuts, -0.22, 0.18)
    return jnp.clip(entries, -limit, limit).astype(held_as)


def setup_inputs(seed: int = 0) -> dict:
    arg_keys = jax.random.split(jax.random.key(seed), 6)
    queries = draw_queries(jax.random.fold_in(arg_keys[5], 71), 0)
    keys = draw_keys(jax.random.fold_in(arg_keys[5], 71), 0)
    values = gaussian(arg_keys[2], (SEQ, HD), 1.0, 6.0, ((0, 16),))
    out_grads = gaussian(arg_keys[3], (SEQ, GROUP * HD), 1.0, 6.0, ((0, 16), (1, 2)))
    doc_lengths = ragged_sizes(arg_keys[4], NDOCS, SEQ, MAXDOC, 1).astype(jnp.int32)
    return dict(queries=queries, keys=keys, values=values, out_grads=out_grads, doc_lengths=doc_lengths)


masked_value = -1.0e30


def token_positions():
    row_ids = jnp.arange(SEQ, dtype=jnp.int32)
    device_ids = row_ids // TOK_DEV
    offsets = row_ids % TOK_DEV
    low_pos = device_ids * SPAN + offsets
    high_pos = (NCHUNK - 1 - device_ids) * SPAN + offsets - SPAN
    return jnp.where(offsets < SPAN, low_pos, high_pos)


def reference(queries, keys, values, out_grads, doc_lengths):
    positions = token_positions()
    doc_ends = jnp.cumsum(doc_lengths)
    doc_index = jnp.sum((positions[:, None] >= doc_ends[None, :]).astype(jnp.int32), axis=1)
    live_mask = (positions[None, :] <= positions[:, None]) & (doc_index[None, :] == doc_index[:, None])
    score_scale = HD ** -0.5

    def one_head(head_id):
        start = (head_id * HD).astype(jnp.int32)
        query_head = lax.dynamic_slice_in_dim(queries, start, HD, 1)
        grad_head = lax.dynamic_slice_in_dim(out_grads, start, HD, 1)
        logits = score_scale * jnp.dot(query_head, keys.T, preferred_element_type=jnp.float32)
        row_top = jnp.max(jnp.where(live_mask, logits, masked_value), axis=1, keepdims=True)
        row_total = jnp.sum(jnp.where(live_mask, jnp.exp(logits - row_top), 0.0), axis=1, keepdims=True)
        row_lse = row_top + jnp.log(row_total)
        weights_f = jnp.where(live_mask, jnp.exp(logits - row_lse), 0.0)
        weights_low = weights_f.astype(jnp.bfloat16)
        output = jnp.dot(weights_low, values, preferred_element_type=jnp.float32)
        delta = jnp.sum(grad_head.astype(jnp.float32) * output, axis=1, keepdims=True)
        dweights = jnp.dot(grad_head, values.T, preferred_element_type=jnp.float32)
        dlogits = (weights_f * (dweights - delta)).astype(jnp.bfloat16)
        query_grad = (score_scale * jnp.dot(dlogits, keys, preferred_element_type=jnp.float32)).astype(jnp.bfloat16)
        key_part = jnp.dot(dlogits.T, query_head, preferred_element_type=jnp.float32)
        value_part = jnp.dot(weights_low.T, grad_head, preferred_element_type=jnp.float32)
        return query_grad, key_part, value_part

    query_parts, key_parts, value_parts = lax.map(one_head, jnp.arange(GROUP, dtype=jnp.int32))
    query_grads = jnp.transpose(query_parts, (1, 0, 2)).reshape(SEQ, GROUP * HD)
    key_grads = (score_scale * jnp.sum(key_parts, axis=0)).astype(jnp.bfloat16)
    value_grads = jnp.sum(value_parts, axis=0).astype(jnp.bfloat16)
    return (query_grads, key_grads, value_grads)
```

```python
import functools
import math

import jax
import jax.numpy as jnp
from jax import lax
from jax.experimental import pallas as pl
from jax.experimental.pallas import tpu as pltpu
from jax.sharding import PartitionSpec as P

masked_value = -1e30


def span_row(span, ctx_count, span_rows):
    low = span < ctx_count
    return (span if low else 2 * ctx_count - 1 - span) * 2 * span_rows + (0 if low else span_rows)


def attend_kernel(
    ctx_count,
    tile,
    lengths_ref,
    q_ref,
    g_ref,
    kv_ref,
    dq_ref,
    dkv_ref,
    ordered_ref,
    kt_ref,
    acc_ref,
    stack_ref,
    flip_ref,
    s_ref,
    dp_ref,
    dqt_ref,
):
    tok_rows, width = q_ref.shape
    head_width = kv_ref.shape[1] // 2
    head_count = width // head_width
    span_rows = tok_rows // 2
    span_count = 2 * ctx_count
    seq = span_count * span_rows
    cols = head_count * span_rows
    scale = head_width ** (-0.5)
    ctx_index = lax.axis_index("ctx")

    for span in range(span_count):
        ordered_ref[pl.ds(span * span_rows, span_rows), :] = kv_ref[
            pl.ds(span_row(span, ctx_count, span_rows), span_rows), :
        ]
    for part in range(seq // tile):
        rows = pl.ds(part * tile, tile)
        kt_ref[:, rows] = ordered_ref[rows, :head_width].T
    acc_ref[...] = jnp.zeros_like(acc_ref)

    for half in range(2):
        rows = pl.ds(half * span_rows, span_rows)
        for head in range(head_count):
            lanes = pl.ds(head * head_width, head_width)
            out_rows = pl.ds(head * span_rows, span_rows)
            stack_ref[0, out_rows, :] = q_ref[rows, lanes]
            stack_ref[1, out_rows, :] = g_ref[rows, lanes]
        flip_ref[0] = stack_ref[0].T
        flip_ref[1] = stack_ref[1].T
        span = ctx_index if half == 0 else span_count - 1 - ctx_index
        first = span * span_rows
        query_pos = first + lax.rem(
            lax.broadcasted_iota(jnp.int32, (1, cols), 1), jnp.int32(span_rows)
        )
        doc_start = jnp.zeros((1, cols), jnp.int32)
        first_key = jnp.int32(0)
        end = jnp.int32(0)
        for doc in range(lengths_ref.shape[0]):
            end = end + lengths_ref[doc]
            doc_start = jnp.where(query_pos >= end, end, doc_start)
            first_key = jnp.where(first >= end, end, first_key)
        tile_low = first_key // tile
        tile_high = (first + span_rows + tile - 1) // tile

        def logits_step(index, top):
            rows = pl.ds(pl.multiple_of(index * tile, tile), tile)
            logits = jnp.dot(
                ordered_ref[rows, :head_width], flip_ref[0], preferred_element_type=jnp.float32
            )
            key_pos = index * tile + lax.broadcasted_iota(jnp.int32, (tile, cols), 0)
            live = (key_pos >= doc_start) & (key_pos <= query_pos)
            logits = jnp.where(live, logits * scale, masked_value)
            s_ref[rows, :] = logits
            return jnp.maximum(top, jnp.max(logits, axis=0, keepdims=True))

        top = lax.fori_loop(
            tile_low, tile_high, logits_step, jnp.full((1, cols), masked_value, jnp.float32)
        )

        def sums_step(index, state):
            total, mixed = state
            rows = pl.ds(pl.multiple_of(index * tile, tile), tile)
            terms = jnp.exp(s_ref[rows, :] - top)
            dweights = jnp.dot(
                ordered_ref[rows, head_width:], flip_ref[1], preferred_element_type=jnp.float32
            )
            s_ref[rows, :] = terms
            dp_ref[rows, :] = dweights
            return (
                total + jnp.sum(terms, axis=0, keepdims=True),
                mixed + jnp.sum(terms * dweights, axis=0, keepdims=True),
            )

        zero = jnp.zeros((1, cols), jnp.float32)
        total, mixed = lax.fori_loop(tile_low, tile_high, sums_step, (zero, zero))
        inverse = 1.0 / total
        delta = mixed * inverse
        dqt_ref[...] = jnp.zeros_like(dqt_ref)

        def grads_step(index, carry):
            rows = pl.ds(pl.multiple_of(index * tile, tile), tile)
            weights = s_ref[rows, :] * inverse
            dlogits = (weights * (dp_ref[rows, :] - delta)).astype(jnp.bfloat16)
            acc_ref[rows, head_width:] += jnp.dot(
                weights.astype(jnp.bfloat16), stack_ref[1], preferred_element_type=jnp.float32
            )
            acc_ref[rows, :head_width] += jnp.dot(
                dlogits, stack_ref[0], preferred_element_type=jnp.float32
            )
            dqt_ref[...] += jnp.dot(kt_ref[:, rows], dlogits, preferred_element_type=jnp.float32)
            return carry

        lax.fori_loop(tile_low, tile_high, grads_step, 0)
        dq = (scale * dqt_ref[...]).T.astype(jnp.bfloat16)
        for head in range(head_count):
            dq_ref[rows, pl.ds(head * head_width, head_width)] = dq[
                head * span_rows : (head + 1) * span_rows
            ]

    for span in range(span_count):
        rows = pl.ds(span * span_rows, span_rows)
        out_rows = pl.ds(span_row(span, ctx_count, span_rows), span_rows)
        dkv_ref[out_rows, :head_width] = (scale * acc_ref[rows, :head_width]).astype(jnp.bfloat16)
        dkv_ref[out_rows, head_width:] = acc_ref[rows, head_width:].astype(jnp.bfloat16)


def attend(ctx_count, doc_lengths, queries, out_grads, kv_all):
    tok_rows, width = queries.shape
    seq, kv_width = kv_all.shape
    head_width = kv_width // 2
    span_rows = tok_rows // 2
    cols = width // head_width * span_rows
    tile = min(256, seq)
    vmem = pl.BlockSpec(memory_space=pltpu.VMEM)
    return pl.pallas_call(
        functools.partial(attend_kernel, ctx_count, tile),
        out_shape=(
            jax.ShapeDtypeStruct((tok_rows, width), jnp.bfloat16),
            jax.ShapeDtypeStruct((seq, kv_width), jnp.bfloat16),
        ),
        in_specs=[pl.BlockSpec(memory_space=pltpu.SMEM), vmem, vmem, vmem],
        out_specs=(vmem, vmem),
        scratch_shapes=[
            pltpu.VMEM((seq, kv_width), jnp.bfloat16),
            pltpu.VMEM((head_width, seq), jnp.bfloat16),
            pltpu.VMEM((seq, kv_width), jnp.float32),
            pltpu.VMEM((2, cols, head_width), jnp.bfloat16),
            pltpu.VMEM((2, head_width, cols), jnp.bfloat16),
            pltpu.VMEM((seq, cols), jnp.float32),
            pltpu.VMEM((seq, cols), jnp.float32),
            pltpu.VMEM((head_width, cols), jnp.float32),
        ],
        compiler_params=pltpu.CompilerParams(vmem_limit_bytes=40 * 1024 * 1024),
    )(doc_lengths, queries, out_grads, kv_all)


def body(queries, keys, values, out_grads, doc_lengths):
    ctx_count = lax.axis_size("ctx")
    dp_count = lax.axis_size("dp")
    tok_rows, head_width = keys.shape
    kv_all = lax.all_gather(
        jnp.concatenate([keys, values], axis=1), "ctx", axis=0, tiled=True
    )
    query_grads, kv_parts = attend(ctx_count, doc_lengths, queries, out_grads, kv_all)
    received = lax.all_to_all(kv_parts, ("ctx", "dp"), split_axis=0, concat_axis=0, tiled=True)
    shares = received.reshape(ctx_count * dp_count, tok_rows // dp_count, 2 * head_width)
    kv_grads = jnp.sum(shares.astype(jnp.float32), axis=0).astype(jnp.bfloat16)
    return (query_grads, kv_grads[:, :head_width], kv_grads[:, head_width:])


def solution(mesh):
    return jax.shard_map(
        body,
        mesh=mesh,
        in_specs=(P("ctx", "dp"), P("ctx", None), P("ctx", None), P("ctx", "dp"), P()),
        out_specs=(P("ctx", "dp"), P(("ctx", "dp"), None), P(("ctx", "dp"), None)),
        check_vma=False,
    )
```

```python
import functools
import math

import jax
import jax.numpy as jnp
from jax import lax
from jax.experimental import pallas as pl
from jax.experimental.pallas import tpu as pltpu
from jax.sharding import PartitionSpec as P

masked_value = -1e30


def part_position(ctx_index, dp_index, ctx_count, part_rows, span_rows):
    start = dp_index * part_rows
    low = ctx_index * span_rows + start
    high = (2 * ctx_count - 1 - ctx_index) * span_rows + start - span_rows
    return pl.multiple_of(jnp.where(start < span_rows, low, high), part_rows)


def attend_kernel(
    ctx_count,
    dp_count,
    inner,
    tile,
    lengths_ref,
    q_ref,
    g_ref,
    *refs,
):
    outer = ctx_count // inner
    piece_count = dp_count * inner
    kv_refs = refs[:piece_count]
    dq_ref = refs[piece_count]
    dkv_refs = refs[piece_count + 1 : 2 * piece_count + 1]
    ordered_ref, kt_ref, acc_ref, stack_ref, flip_ref, s_ref, dp_ref, dqt_ref = refs[
        2 * piece_count + 1 :
    ]
    tok_rows, width = q_ref.shape
    part_rows = tok_rows // dp_count
    head_width = kv_refs[0].shape[1] // 2
    head_count = width // head_width
    span_rows = tok_rows // 2
    span_count = 2 * ctx_count
    seq = span_count * span_rows
    cols = head_count * span_rows
    scale = head_width ** (-0.5)
    ctx_index = lax.axis_index("ctx")

    dp_index = lax.axis_index("dp")

    def blocks():
        for piece in range(piece_count):
            for block in range(outer):
                owner = ctx_index ^ (piece % inner) ^ (block * inner)
                position = part_position(
                    owner, dp_index ^ (piece // inner), ctx_count, part_rows, span_rows
                )
                yield piece, pl.ds(block * part_rows, part_rows), pl.ds(position, part_rows)

    for piece, here, ordered in blocks():
        ordered_ref[ordered, :] = kv_refs[piece][here, :]
    for part in range(seq // tile):
        rows = pl.ds(part * tile, tile)
        kt_ref[:, rows] = ordered_ref[rows, :head_width].T
    acc_ref[...] = jnp.zeros_like(acc_ref)

    for half in range(2):
        rows = pl.ds(half * span_rows, span_rows)
        for head in range(head_count):
            lanes = pl.ds(head * head_width, head_width)
            out_rows = pl.ds(head * span_rows, span_rows)
            stack_ref[0, out_rows, :] = q_ref[rows, lanes]
            stack_ref[1, out_rows, :] = g_ref[rows, lanes]
        flip_ref[0] = stack_ref[0].T
        flip_ref[1] = stack_ref[1].T
        span = ctx_index if half == 0 else span_count - 1 - ctx_index
        first = span * span_rows
        query_pos = first + lax.rem(
            lax.broadcasted_iota(jnp.int32, (1, cols), 1), jnp.int32(span_rows)
        )
        doc_start = jnp.zeros((1, cols), jnp.int32)
        first_key = jnp.int32(0)
        end = jnp.int32(0)
        for doc in range(lengths_ref.shape[0]):
            end = end + lengths_ref[doc]
            doc_start = jnp.where(query_pos >= end, end, doc_start)
            first_key = jnp.where(first >= end, end, first_key)
        tile_low = first_key // tile
        tile_high = (first + span_rows + tile - 1) // tile

        def logits_step(index, top):
            rows = pl.ds(pl.multiple_of(index * tile, tile), tile)
            logits = jnp.dot(
                ordered_ref[rows, :head_width], flip_ref[0], preferred_element_type=jnp.float32
            )
            key_pos = index * tile + lax.broadcasted_iota(jnp.int32, (tile, cols), 0)
            live = (key_pos >= doc_start) & (key_pos <= query_pos)
            logits = jnp.where(live, logits * scale, masked_value)
            s_ref[rows, :] = logits
            return jnp.maximum(top, jnp.max(logits, axis=0, keepdims=True))

        top = lax.fori_loop(
            tile_low, tile_high, logits_step, jnp.full((1, cols), masked_value, jnp.float32)
        )

        def sums_step(index, state):
            total, mixed = state
            rows = pl.ds(pl.multiple_of(index * tile, tile), tile)
            terms = jnp.exp(s_ref[rows, :] - top)
            dweights = jnp.dot(
                ordered_ref[rows, head_width:], flip_ref[1], preferred_element_type=jnp.float32
            )
            s_ref[rows, :] = terms
            dp_ref[rows, :] = dweights
            return (
                total + jnp.sum(terms, axis=0, keepdims=True),
                mixed + jnp.sum(terms * dweights, axis=0, keepdims=True),
            )

        zero = jnp.zeros((1, cols), jnp.float32)
        total, mixed = lax.fori_loop(tile_low, tile_high, sums_step, (zero, zero))
        inverse = 1.0 / total
        delta = mixed * inverse
        dqt_ref[...] = jnp.zeros_like(dqt_ref)

        def grads_step(index, carry):
            rows = pl.ds(pl.multiple_of(index * tile, tile), tile)
            weights = s_ref[rows, :] * inverse
            dlogits = (weights * (dp_ref[rows, :] - delta)).astype(jnp.bfloat16)
            acc_ref[rows, head_width:] += jnp.dot(
                weights.astype(jnp.bfloat16), stack_ref[1], preferred_element_type=jnp.float32
            )
            acc_ref[rows, :head_width] += jnp.dot(
                dlogits, stack_ref[0], preferred_element_type=jnp.float32
            )
            dqt_ref[...] += jnp.dot(kt_ref[:, rows], dlogits, preferred_element_type=jnp.float32)
            return carry

        lax.fori_loop(tile_low, tile_high, grads_step, 0)
        dq = (scale * dqt_ref[...]).T.astype(jnp.bfloat16)
        for head in range(head_count):
            dq_ref[rows, pl.ds(head * head_width, head_width)] = dq[
                head * span_rows : (head + 1) * span_rows
            ]

    for piece, here, ordered in blocks():
        dkv_refs[piece][here, :head_width] = (scale * acc_ref[ordered, :head_width]).astype(
            jnp.bfloat16
        )
        dkv_refs[piece][here, head_width:] = acc_ref[ordered, head_width:].astype(jnp.bfloat16)


def attend(ctx_count, dp_count, inner, doc_lengths, queries, out_grads, pieces):
    tok_rows, width = queries.shape
    kv_width = pieces[0].shape[1]
    head_width = kv_width // 2
    span_rows = tok_rows // 2
    seq = ctx_count * tok_rows
    cols = width // head_width * span_rows
    tile = min(256, seq)
    vmem = pl.BlockSpec(memory_space=pltpu.VMEM)
    results = pl.pallas_call(
        functools.partial(attend_kernel, ctx_count, dp_count, inner, tile),
        out_shape=[jax.ShapeDtypeStruct((tok_rows, width), jnp.bfloat16)]
        + [jax.ShapeDtypeStruct(piece.shape, jnp.bfloat16) for piece in pieces],
        in_specs=[pl.BlockSpec(memory_space=pltpu.SMEM)] + [vmem] * (2 + len(pieces)),
        out_specs=[vmem] * (1 + len(pieces)),
        scratch_shapes=[
            pltpu.VMEM((seq, kv_width), jnp.bfloat16),
            pltpu.VMEM((head_width, seq), jnp.bfloat16),
            pltpu.VMEM((seq, kv_width), jnp.float32),
            pltpu.VMEM((2, cols, head_width), jnp.bfloat16),
            pltpu.VMEM((2, head_width, cols), jnp.bfloat16),
            pltpu.VMEM((seq, cols), jnp.float32),
            pltpu.VMEM((seq, cols), jnp.float32),
            pltpu.VMEM((head_width, cols), jnp.float32),
        ],
        compiler_params=pltpu.CompilerParams(vmem_limit_bytes=40 * 1024 * 1024),
    )(doc_lengths, queries, out_grads, *pieces)
    return results[0], results[1:]


def swap(value, axis, offset):
    pairs = [(index, index ^ offset) for index in range(lax.axis_size(axis))]
    return lax.ppermute(value, axis, pairs)


def total_of(terms):
    return sum(term.astype(jnp.float32) for term in terms)


def body(queries, keys, values, out_grads, doc_lengths):
    ctx_count = lax.axis_size("ctx")
    dp_count = lax.axis_size("dp")
    inner = math.gcd(4, ctx_count)
    outer = ctx_count // inner
    tok_rows, head_width = keys.shape
    part_rows = tok_rows // dp_count
    own = lax.dynamic_slice_in_dim(
        jnp.concatenate([keys, values], axis=1), lax.axis_index("dp") * part_rows, part_rows, 0
    )
    line = jnp.concatenate(
        [own] + [swap(own, "ctx", block * inner) for block in range(1, outer)], axis=0
    )
    plane = [line] + [swap(line, "ctx", offset) for offset in range(1, inner)]
    pieces = plane + [
        swap(piece, "dp", offset) for offset in range(1, dp_count) for piece in plane
    ]
    query_grads, parts = attend(
        ctx_count, dp_count, inner, doc_lengths, queries, out_grads, pieces
    )
    plane_sums = [
        total_of(
            [parts[offset]]
            + [swap(parts[far * inner + offset], "dp", far) for far in range(1, dp_count)]
        ).astype(jnp.bfloat16)
        for offset in range(inner)
    ]
    line_sum = total_of(
        [plane_sums[0]] + [swap(plane_sums[offset], "ctx", offset) for offset in range(1, inner)]
    ).astype(jnp.bfloat16)
    blocks = [line_sum[block * part_rows : (block + 1) * part_rows] for block in range(outer)]
    kv_grads = total_of(
        [blocks[0]] + [swap(blocks[block], "ctx", block * inner) for block in range(1, outer)]
    ).astype(jnp.bfloat16)
    return (query_grads, kv_grads[:, :head_width], kv_grads[:, head_width:])


def solution(mesh):
    return jax.shard_map(
        body,
        mesh=mesh,
        in_specs=(P("ctx", "dp"), P("ctx", None), P("ctx", None), P("ctx", "dp"), P()),
        out_specs=(P("ctx", "dp"), P(("ctx", "dp"), None), P(("ctx", "dp"), None)),
        check_vma=False,
    )
```

```python
import functools
import math

import jax
import jax.numpy as jnp
from jax import lax
from jax.experimental import pallas as pl
from jax.experimental.pallas import tpu as pltpu
from jax.sharding import PartitionSpec as P

masked_value = -1e30


def part_position(ctx_index, dp_index, ctx_count, part_rows, span_rows):
    start = dp_index * part_rows
    low = ctx_index * span_rows + start
    high = (2 * ctx_count - 1 - ctx_index) * span_rows + start - span_rows
    return pl.multiple_of(jnp.where(start < span_rows, low, high), part_rows)


def attend_kernel(
    ctx_count,
    dp_count,
    inner,
    tile,
    lengths_ref,
    q_ref,
    g_ref,
    *refs,
):
    outer = ctx_count // inner
    piece_count = dp_count * inner
    kv_refs = refs[:piece_count]
    dq_ref = refs[piece_count]
    dkv_refs = refs[piece_count + 1 : piece_count + 1 + dp_count]
    ordered_ref, kt_ref, acc_ref, stack_ref, flip_ref, s_ref, dp_ref, dqt_ref = refs[
        piece_count + 1 + dp_count :
    ]
    tok_rows, width = q_ref.shape
    part_rows = tok_rows // dp_count
    head_width = kv_refs[0].shape[1] // 2
    head_count = width // head_width
    span_rows = tok_rows // 2
    span_count = 2 * ctx_count
    seq = span_count * span_rows
    cols = head_count * span_rows
    scale = head_width ** (-0.5)
    ctx_index = lax.axis_index("ctx")

    dp_index = lax.axis_index("dp")

    def blocks():
        for piece in range(piece_count):
            for block in range(outer):
                owner = ((ctx_index & (inner - 1)) ^ (piece % inner)) + block * inner
                position = part_position(
                    owner, dp_index ^ (piece // inner), ctx_count, part_rows, span_rows
                )
                yield piece, pl.ds(block * part_rows, part_rows), pl.ds(position, part_rows)

    for piece, here, ordered in blocks():
        ordered_ref[ordered, :] = kv_refs[piece][here, :]
    for part in range(seq // tile):
        rows = pl.ds(part * tile, tile)
        kt_ref[:, rows] = ordered_ref[rows, :head_width].T
    acc_ref[...] = jnp.zeros_like(acc_ref)

    for half in range(2):
        rows = pl.ds(half * span_rows, span_rows)
        for head in range(head_count):
            lanes = pl.ds(head * head_width, head_width)
            out_rows = pl.ds(head * span_rows, span_rows)
            stack_ref[0, out_rows, :] = q_ref[rows, lanes]
            stack_ref[1, out_rows, :] = g_ref[rows, lanes]
        flip_ref[0] = stack_ref[0].T
        flip_ref[1] = stack_ref[1].T
        span = ctx_index if half == 0 else span_count - 1 - ctx_index
        first = span * span_rows
        query_pos = first + lax.rem(
            lax.broadcasted_iota(jnp.int32, (1, cols), 1), jnp.int32(span_rows)
        )
        doc_start = jnp.zeros((1, cols), jnp.int32)
        first_key = jnp.int32(0)
        end = jnp.int32(0)
        for doc in range(lengths_ref.shape[0]):
            end = end + lengths_ref[doc]
            doc_start = jnp.where(query_pos >= end, end, doc_start)
            first_key = jnp.where(first >= end, end, first_key)
        tile_low = first_key // tile
        tile_high = (first + span_rows + tile - 1) // tile

        def logits_step(index, top):
            rows = pl.ds(pl.multiple_of(index * tile, tile), tile)
            logits = jnp.dot(
                ordered_ref[rows, :head_width], flip_ref[0], preferred_element_type=jnp.float32
            )
            key_pos = index * tile + lax.broadcasted_iota(jnp.int32, (tile, cols), 0)
            live = (key_pos >= doc_start) & (key_pos <= query_pos)
            logits = jnp.where(live, logits * scale, masked_value)
            s_ref[rows, :] = logits
            return jnp.maximum(top, jnp.max(logits, axis=0, keepdims=True))

        top = lax.fori_loop(
            tile_low, tile_high, logits_step, jnp.full((1, cols), masked_value, jnp.float32)
        )

        def sums_step(index, state):
            total, mixed = state
            rows = pl.ds(pl.multiple_of(index * tile, tile), tile)
            terms = jnp.exp(s_ref[rows, :] - top)
            dweights = jnp.dot(
                ordered_ref[rows, head_width:], flip_ref[1], preferred_element_type=jnp.float32
            )
            s_ref[rows, :] = terms
            dp_ref[rows, :] = dweights
            return (
                total + jnp.sum(terms, axis=0, keepdims=True),
                mixed + jnp.sum(terms * dweights, axis=0, keepdims=True),
            )

        zero = jnp.zeros((1, cols), jnp.float32)
        total, mixed = lax.fori_loop(tile_low, tile_high, sums_step, (zero, zero))
        inverse = 1.0 / total
        delta = mixed * inverse
        dqt_ref[...] = jnp.zeros_like(dqt_ref)

        def grads_step(index, carry):
            rows = pl.ds(pl.multiple_of(index * tile, tile), tile)
            weights = s_ref[rows, :] * inverse
            dlogits = (weights * (dp_ref[rows, :] - delta)).astype(jnp.bfloat16)
            acc_ref[rows, head_width:] += jnp.dot(
                weights.astype(jnp.bfloat16), stack_ref[1], preferred_element_type=jnp.float32
            )
            acc_ref[rows, :head_width] += jnp.dot(
                dlogits, stack_ref[0], preferred_element_type=jnp.float32
            )
            dqt_ref[...] += jnp.dot(kt_ref[:, rows], dlogits, preferred_element_type=jnp.float32)
            return carry

        lax.fori_loop(tile_low, tile_high, grads_step, 0)
        dq = (scale * dqt_ref[...]).T.astype(jnp.bfloat16)
        for head in range(head_count):
            dq_ref[rows, pl.ds(head * head_width, head_width)] = dq[
                head * span_rows : (head + 1) * span_rows
            ]

    for far in range(dp_count):
        for owner in range(ctx_count):
            here = pl.ds(owner * part_rows, part_rows)
            position = part_position(owner, dp_index ^ far, ctx_count, part_rows, span_rows)
            ordered = pl.ds(position, part_rows)
            dkv_refs[far][here, :head_width] = (scale * acc_ref[ordered, :head_width]).astype(
                jnp.bfloat16
            )
            dkv_refs[far][here, head_width:] = acc_ref[ordered, head_width:].astype(jnp.bfloat16)


def attend(ctx_count, dp_count, inner, doc_lengths, queries, out_grads, pieces):
    tok_rows, width = queries.shape
    kv_width = pieces[0].shape[1]
    head_width = kv_width // 2
    span_rows = tok_rows // 2
    seq = ctx_count * tok_rows
    cols = width // head_width * span_rows
    tile = min(256, seq)
    vmem = pl.BlockSpec(memory_space=pltpu.VMEM)
    results = pl.pallas_call(
        functools.partial(attend_kernel, ctx_count, dp_count, inner, tile),
        out_shape=[jax.ShapeDtypeStruct((tok_rows, width), jnp.bfloat16)]
        + [jax.ShapeDtypeStruct((seq // dp_count, kv_width), jnp.bfloat16)] * dp_count,
        in_specs=[pl.BlockSpec(memory_space=pltpu.SMEM)] + [vmem] * (2 + len(pieces)),
        out_specs=[vmem] * (1 + dp_count),
        scratch_shapes=[
            pltpu.VMEM((seq, kv_width), jnp.bfloat16),
            pltpu.VMEM((head_width, seq), jnp.bfloat16),
            pltpu.VMEM((seq, kv_width), jnp.float32),
            pltpu.VMEM((2, cols, head_width), jnp.bfloat16),
            pltpu.VMEM((2, head_width, cols), jnp.bfloat16),
            pltpu.VMEM((seq, cols), jnp.float32),
            pltpu.VMEM((seq, cols), jnp.float32),
            pltpu.VMEM((head_width, cols), jnp.float32),
        ],
        compiler_params=pltpu.CompilerParams(vmem_limit_bytes=40 * 1024 * 1024),
    )(doc_lengths, queries, out_grads, *pieces)
    return results[0], results[1:]


def swap(value, axis, offset):
    pairs = [(index, index ^ offset) for index in range(lax.axis_size(axis))]
    return lax.ppermute(value, axis, pairs)


def total_of(terms):
    return sum(term.astype(jnp.float32) for term in terms)


def body(queries, keys, values, out_grads, doc_lengths):
    ctx_count = lax.axis_size("ctx")
    dp_count = lax.axis_size("dp")
    inner = math.gcd(4, ctx_count)
    outer = ctx_count // inner
    tok_rows, head_width = keys.shape
    part_rows = tok_rows // dp_count
    own = lax.dynamic_slice_in_dim(
        jnp.concatenate([keys, values], axis=1), lax.axis_index("dp") * part_rows, part_rows, 0
    )
    lines = [
        [block * inner + offset for block in range(outer)] for offset in range(inner)
    ]
    line = lax.all_to_all(
        jnp.tile(own, (outer, 1)),
        "ctx",
        split_axis=0,
        concat_axis=0,
        axis_index_groups=lines,
        tiled=True,
    )
    plane = [line] + [swap(line, "ctx", offset) for offset in range(1, inner)]
    pieces = plane + [
        swap(piece, "dp", offset) for offset in range(1, dp_count) for piece in plane
    ]
    query_grads, parts = attend(
        ctx_count, dp_count, inner, doc_lengths, queries, out_grads, pieces
    )
    chip_sum = total_of(
        [parts[0]] + [swap(parts[far], "dp", far) for far in range(1, dp_count)]
    ).astype(jnp.bfloat16)
    received = lax.all_to_all(chip_sum, "ctx", split_axis=0, concat_axis=0, tiled=True)
    kv_grads = total_of(jnp.split(received, ctx_count, axis=0)).astype(jnp.bfloat16)
    return (query_grads, kv_grads[:, :head_width], kv_grads[:, head_width:])


def solution(mesh):
    return jax.shard_map(
        body,
        mesh=mesh,
        in_specs=(P("ctx", "dp"), P("ctx", None), P("ctx", None), P("ctx", "dp"), P()),
        out_specs=(P("ctx", "dp"), P(("ctx", "dp"), None), P(("ctx", "dp"), None)),
        check_vma=False,
    )
```

```python
import functools
import math

import jax
import jax.numpy as jnp
from jax import lax
from jax.experimental import pallas as pl
from jax.experimental.pallas import tpu as pltpu
from jax.sharding import PartitionSpec as P

masked_value = -1e30


def part_position(ctx_index, dp_index, ctx_count, part_rows, span_rows):
    start = dp_index * part_rows
    low = ctx_index * span_rows + start
    high = (2 * ctx_count - 1 - ctx_index) * span_rows + start - span_rows
    return pl.multiple_of(jnp.where(start < span_rows, low, high), part_rows)


def attend_kernel(
    ctx_count,
    dp_count,
    inner,
    tile,
    lengths_ref,
    q_ref,
    g_ref,
    *refs,
):
    outer = ctx_count // inner
    kv_refs = refs[:dp_count]
    dq_ref = refs[dp_count]
    dkv_refs = refs[dp_count + 1 : 2 * dp_count + 1]
    ordered_ref, kt_ref, acc_ref, stack_ref, flip_ref, s_ref, dp_ref, dqt_ref = refs[
        2 * dp_count + 1 :
    ]
    tok_rows, width = q_ref.shape
    part_rows = tok_rows // dp_count
    head_width = kv_refs[0].shape[1] // 2
    head_count = width // head_width
    span_rows = tok_rows // 2
    span_count = 2 * ctx_count
    seq = span_count * span_rows
    cols = head_count * span_rows
    scale = head_width ** (-0.5)
    ctx_index = lax.axis_index("ctx")

    dp_index = lax.axis_index("dp")

    for far in range(dp_count):
        for owner in range(ctx_count):
            position = part_position(owner, dp_index ^ far, ctx_count, part_rows, span_rows)
            ordered_ref[pl.ds(position, part_rows), :] = kv_refs[far][
                pl.ds(owner * part_rows, part_rows), :
            ]
    for part in range(seq // tile):
        rows = pl.ds(part * tile, tile)
        kt_ref[:, rows] = ordered_ref[rows, :head_width].T
    acc_ref[...] = jnp.zeros_like(acc_ref)

    for half in range(2):
        rows = pl.ds(half * span_rows, span_rows)
        for head in range(head_count):
            lanes = pl.ds(head * head_width, head_width)
            out_rows = pl.ds(head * span_rows, span_rows)
            stack_ref[0, out_rows, :] = q_ref[rows, lanes]
            stack_ref[1, out_rows, :] = g_ref[rows, lanes]
        flip_ref[0] = stack_ref[0].T
        flip_ref[1] = stack_ref[1].T
        span = ctx_index if half == 0 else span_count - 1 - ctx_index
        first = span * span_rows
        query_pos = first + lax.rem(
            lax.broadcasted_iota(jnp.int32, (1, cols), 1), jnp.int32(span_rows)
        )
        doc_start = jnp.zeros((1, cols), jnp.int32)
        first_key = jnp.int32(0)
        end = jnp.int32(0)
        for doc in range(lengths_ref.shape[0]):
            end = end + lengths_ref[doc]
            doc_start = jnp.where(query_pos >= end, end, doc_start)
            first_key = jnp.where(first >= end, end, first_key)
        tile_low = first_key // tile
        tile_high = (first + span_rows + tile - 1) // tile

        def logits_step(index, top):
            rows = pl.ds(pl.multiple_of(index * tile, tile), tile)
            logits = jnp.dot(
                ordered_ref[rows, :head_width], flip_ref[0], preferred_element_type=jnp.float32
            )
            key_pos = index * tile + lax.broadcasted_iota(jnp.int32, (tile, cols), 0)
            live = (key_pos >= doc_start) & (key_pos <= query_pos)
            logits = jnp.where(live, logits * scale, masked_value)
            s_ref[rows, :] = logits
            return jnp.maximum(top, jnp.max(logits, axis=0, keepdims=True))

        top = lax.fori_loop(
            tile_low, tile_high, logits_step, jnp.full((1, cols), masked_value, jnp.float32)
        )

        def sums_step(index, state):
            total, mixed = state
            rows = pl.ds(pl.multiple_of(index * tile, tile), tile)
            terms = jnp.exp(s_ref[rows, :] - top)
            dweights = jnp.dot(
                ordered_ref[rows, head_width:], flip_ref[1], preferred_element_type=jnp.float32
            )
            s_ref[rows, :] = terms
            dp_ref[rows, :] = dweights
            return (
                total + jnp.sum(terms, axis=0, keepdims=True),
                mixed + jnp.sum(terms * dweights, axis=0, keepdims=True),
            )

        zero = jnp.zeros((1, cols), jnp.float32)
        total, mixed = lax.fori_loop(tile_low, tile_high, sums_step, (zero, zero))
        inverse = 1.0 / total
        delta = mixed * inverse
        dqt_ref[...] = jnp.zeros_like(dqt_ref)

        def grads_step(index, carry):
            rows = pl.ds(pl.multiple_of(index * tile, tile), tile)
            weights = s_ref[rows, :] * inverse
            dlogits = (weights * (dp_ref[rows, :] - delta)).astype(jnp.bfloat16)
            acc_ref[rows, head_width:] += jnp.dot(
                weights.astype(jnp.bfloat16), stack_ref[1], preferred_element_type=jnp.float32
            )
            acc_ref[rows, :head_width] += jnp.dot(
                dlogits, stack_ref[0], preferred_element_type=jnp.float32
            )
            dqt_ref[...] += jnp.dot(kt_ref[:, rows], dlogits, preferred_element_type=jnp.float32)
            return carry

        lax.fori_loop(tile_low, tile_high, grads_step, 0)
        dq = (scale * dqt_ref[...]).T.astype(jnp.bfloat16)
        for head in range(head_count):
            dq_ref[rows, pl.ds(head * head_width, head_width)] = dq[
                head * span_rows : (head + 1) * span_rows
            ]

    for far in range(dp_count):
        for offset in range(inner):
            for block in range(outer):
                here = pl.ds((offset * outer + block) * part_rows, part_rows)
                owner = ctx_index ^ offset ^ (block * inner)
                position = part_position(owner, dp_index ^ far, ctx_count, part_rows, span_rows)
                ordered = pl.ds(position, part_rows)
                dkv_refs[far][here, :head_width] = (scale * acc_ref[ordered, :head_width]).astype(
                    jnp.bfloat16
                )
                dkv_refs[far][here, head_width:] = acc_ref[ordered, head_width:].astype(
                    jnp.bfloat16
                )


def attend(ctx_count, dp_count, inner, doc_lengths, queries, out_grads, pieces):
    tok_rows, width = queries.shape
    kv_width = pieces[0].shape[1]
    head_width = kv_width // 2
    span_rows = tok_rows // 2
    seq = ctx_count * tok_rows
    cols = width // head_width * span_rows
    tile = min(256, seq)
    vmem = pl.BlockSpec(memory_space=pltpu.VMEM)
    results = pl.pallas_call(
        functools.partial(attend_kernel, ctx_count, dp_count, inner, tile),
        out_shape=[jax.ShapeDtypeStruct((tok_rows, width), jnp.bfloat16)]
        + [jax.ShapeDtypeStruct((seq // dp_count, kv_width), jnp.bfloat16)] * dp_count,
        in_specs=[pl.BlockSpec(memory_space=pltpu.SMEM)] + [vmem] * (2 + len(pieces)),
        out_specs=[vmem] * (1 + dp_count),
        scratch_shapes=[
            pltpu.VMEM((seq, kv_width), jnp.bfloat16),
            pltpu.VMEM((head_width, seq), jnp.bfloat16),
            pltpu.VMEM((seq, kv_width), jnp.float32),
            pltpu.VMEM((2, cols, head_width), jnp.bfloat16),
            pltpu.VMEM((2, head_width, cols), jnp.bfloat16),
            pltpu.VMEM((seq, cols), jnp.float32),
            pltpu.VMEM((seq, cols), jnp.float32),
            pltpu.VMEM((head_width, cols), jnp.float32),
        ],
        compiler_params=pltpu.CompilerParams(vmem_limit_bytes=40 * 1024 * 1024),
    )(doc_lengths, queries, out_grads, *pieces)
    return results[0], results[1:]


def swap(value, axis, offset):
    pairs = [(index, index ^ offset) for index in range(lax.axis_size(axis))]
    return lax.ppermute(value, axis, pairs)


def total_of(terms):
    return sum(term.astype(jnp.float32) for term in terms)


def body(queries, keys, values, out_grads, doc_lengths):
    ctx_count = lax.axis_size("ctx")
    dp_count = lax.axis_size("dp")
    inner = math.gcd(4, ctx_count)
    outer = ctx_count // inner
    tok_rows, head_width = keys.shape
    part_rows = tok_rows // dp_count
    own = lax.dynamic_slice_in_dim(
        jnp.concatenate([keys, values], axis=1), lax.axis_index("dp") * part_rows, part_rows, 0
    )
    half = lax.all_gather(own, "ctx", axis=0, tiled=True)
    pieces = [half] + [swap(half, "dp", offset) for offset in range(1, dp_count)]
    query_grads, parts = attend(
        ctx_count, dp_count, inner, doc_lengths, queries, out_grads, pieces
    )
    chip_sum = total_of(
        [parts[0]] + [swap(parts[far], "dp", far) for far in range(1, dp_count)]
    ).astype(jnp.bfloat16)
    rows = ctx_count * part_rows // inner
    plane_sums = [chip_sum[offset * rows : (offset + 1) * rows] for offset in range(inner)]
    line_sum = total_of(
        [plane_sums[0]] + [swap(plane_sums[offset], "ctx", offset) for offset in range(1, inner)]
    ).astype(jnp.bfloat16)
    blocks = [line_sum[block * part_rows : (block + 1) * part_rows] for block in range(outer)]
    kv_grads = total_of(
        [blocks[0]] + [swap(blocks[block], "ctx", block * inner) for block in range(1, outer)]
    ).astype(jnp.bfloat16)
    return (query_grads, kv_grads[:, :head_width], kv_grads[:, head_width:])


def solution(mesh):
    return jax.shard_map(
        body,
        mesh=mesh,
        in_specs=(P("ctx", "dp"), P("ctx", None), P("ctx", None), P("ctx", "dp"), P()),
        out_specs=(P("ctx", "dp"), P(("ctx", "dp"), None), P(("ctx", "dp"), None)),
        check_vma=False,
    )
```

```python
import functools
import math

import jax
import jax.numpy as jnp
from jax import lax
from jax.experimental import pallas as pl
from jax.experimental.pallas import tpu as pltpu
from jax.sharding import PartitionSpec as P

masked_value = -1e30


def part_position(ctx_index, dp_index, ctx_count, part_rows, span_rows):
    start = dp_index * part_rows
    low = ctx_index * span_rows + start
    high = (2 * ctx_count - 1 - ctx_index) * span_rows + start - span_rows
    return pl.multiple_of(jnp.where(start < span_rows, low, high), part_rows)


def tile_range(half, ctx_index, ctx_count, span_rows, tile, lengths_ref):
    span = ctx_index if half == 0 else 2 * ctx_count - 1 - ctx_index
    first = span * span_rows
    first_key = jnp.int32(0)
    end = jnp.int32(0)
    for doc in range(lengths_ref.shape[0]):
        end = end + lengths_ref[doc]
        first_key = jnp.where(first >= end, end, first_key)
    return first, first_key // tile, (first + span_rows + tile - 1) // tile


def prepare_kernel(q_hbm, g_hbm, line_ref, stack_ref, flip_ref, same_ref, raw_ref, sems):
    tok_rows = q_hbm.shape[0]
    head_width = stack_ref.shape[3]
    span_rows = tok_rows // 2
    copies = [
        pltpu.make_async_copy(source, raw_ref.at[slot], sems.at[slot])
        for slot, source in enumerate((q_hbm, g_hbm))
    ]
    for copy in copies:
        copy.start()
    same_ref[...] = line_ref[...]
    for slot, copy in enumerate(copies):
        copy.wait()
        for half in range(2):
            for head in range(q_hbm.shape[1] // head_width):
                stack_ref[half, slot, pl.ds(head * span_rows, span_rows), :] = raw_ref[
                    slot,
                    pl.ds(half * span_rows, span_rows),
                    pl.ds(head * head_width, head_width),
                ]
            flip_ref[half, slot] = stack_ref[half, slot].T


def attend_kernel(ctx_count, dp_count, inner, tile, lengths_ref, stack_ref, flip_ref, *refs):
    outer = ctx_count // inner
    piece_count = dp_count * inner
    kv_refs = refs[:piece_count]
    keys_ref, dlogits_ref = refs[piece_count : piece_count + 2]
    dkv_refs = refs[piece_count + 2 : 2 * piece_count + 2]
    values_ref, acc_ref, terms_ref, dweights_ref, tops_ref = refs[2 * piece_count + 2 :]
    cols, head_width = stack_ref.shape[2:]
    seq = keys_ref.shape[0]
    tok_rows = seq // ctx_count
    part_rows = tok_rows // dp_count
    span_rows = tok_rows // 2
    scale = head_width ** (-0.5)
    ctx_index = lax.axis_index("ctx")
    dp_index = lax.axis_index("dp")

    def blocks():
        for piece in range(piece_count):
            for block in range(outer):
                owner = ctx_index ^ (piece % inner) ^ (block * inner)
                position = part_position(
                    owner, dp_index ^ (piece // inner), ctx_count, part_rows, span_rows
                )
                yield piece, pl.ds(block * part_rows, part_rows), pl.ds(position, part_rows)

    for piece, here, ordered in blocks():
        keys_ref[ordered, :] = kv_refs[piece][here, :head_width]
        values_ref[ordered, :] = kv_refs[piece][here, head_width:]
    acc_ref[...] = jnp.zeros_like(acc_ref)

    for half in range(2):
        first, tile_low, tile_high = tile_range(
            half, ctx_index, ctx_count, span_rows, tile, lengths_ref
        )
        query_pos = first + lax.rem(
            lax.broadcasted_iota(jnp.int32, (1, cols), 1), jnp.int32(span_rows)
        )
        doc_start = jnp.zeros((1, cols), jnp.int32)
        end = jnp.int32(0)
        for doc in range(lengths_ref.shape[0]):
            end = end + lengths_ref[doc]
            doc_start = jnp.where(query_pos >= end, end, doc_start)

        def sums_step(index, state):
            top, total, mixed = state
            rows = pl.ds(pl.multiple_of(index * tile, tile), tile)
            logits = jnp.dot(
                keys_ref[rows, :], flip_ref[half, 0], preferred_element_type=jnp.float32
            )
            key_pos = lax.broadcasted_iota(jnp.int32, (tile, cols), 0)
            live = (key_pos >= doc_start - index * tile) & (key_pos <= query_pos - index * tile)
            logits = jnp.where(live, logits * (scale * math.log2(math.e)), masked_value)
            new_top = jnp.maximum(top, jnp.max(logits, axis=0, keepdims=True))
            terms = jnp.exp2(logits - new_top)
            dweights = jnp.dot(
                values_ref[rows, :], flip_ref[half, 1], preferred_element_type=jnp.float32
            )
            terms_ref[rows, :] = terms
            dweights_ref[rows, :] = dweights
            tops_ref[pl.ds(index, 1), :] = new_top
            decay = jnp.exp2(top - new_top)
            return (
                new_top,
                total * decay + jnp.sum(terms, axis=0, keepdims=True),
                mixed * decay + jnp.sum(terms * dweights, axis=0, keepdims=True),
            )

        zero = jnp.zeros((1, cols), jnp.float32)
        top, total, mixed = lax.fori_loop(
            tile_low, tile_high, sums_step, (jnp.full_like(zero, masked_value), zero, zero)
        )
        inverse = 1.0 / total
        delta = mixed * inverse

        def grads_step(index, carry):
            rows = pl.ds(pl.multiple_of(index * tile, tile), tile)
            factor = jnp.exp2(tops_ref[pl.ds(index, 1), :] - top) * inverse
            weights = terms_ref[rows, :] * factor
            dlogits = (weights * (dweights_ref[rows, :] - delta)).astype(jnp.bfloat16)
            dlogits_ref[half, rows, :] = dlogits
            acc_ref[rows, head_width:] += jnp.dot(
                weights.astype(jnp.bfloat16),
                stack_ref[half, 1],
                preferred_element_type=jnp.float32,
            )
            acc_ref[rows, :head_width] += jnp.dot(
                dlogits, stack_ref[half, 0], preferred_element_type=jnp.float32
            )
            return carry

        lax.fori_loop(tile_low, tile_high, grads_step, 0)

    for piece, here, ordered in blocks():
        dkv_refs[piece][here, :head_width] = (scale * acc_ref[ordered, :head_width]).astype(
            jnp.bfloat16
        )
        dkv_refs[piece][here, head_width:] = acc_ref[ordered, head_width:].astype(jnp.bfloat16)


def query_kernel(ctx_count, tile, lengths_ref, keys_ref, dlogits_ref, order_ref, dq_ref, sum_ref):
    tok_rows = dq_ref.shape[0]
    head_width = keys_ref.shape[1]
    span_rows = tok_rows // 2
    scale = head_width ** (-0.5)
    ctx_index = lax.axis_index("ctx")
    for half in range(2):
        _, tile_low, tile_high = tile_range(
            half, ctx_index, ctx_count, span_rows, tile, lengths_ref
        )
        sum_ref[...] = jnp.zeros_like(sum_ref)

        def query_step(index, carry):
            rows = pl.ds(pl.multiple_of(index * tile, tile), tile)
            sum_ref[...] += jnp.dot(
                keys_ref[rows, :].T, dlogits_ref[half, rows, :], preferred_element_type=jnp.float32
            )
            return carry

        lax.fori_loop(tile_low, tile_high, query_step, 0)
        grads = (scale * sum_ref[...]).T.astype(jnp.bfloat16)
        for head in range(dq_ref.shape[1] // head_width):
            dq_ref[
                pl.ds(half * span_rows, span_rows), pl.ds(head * head_width, head_width)
            ] = grads[head * span_rows : (head + 1) * span_rows]


vmem = pl.BlockSpec(memory_space=pltpu.VMEM)
smem = pl.BlockSpec(memory_space=pltpu.SMEM)


def prepare(queries, out_grads, head_width, line):
    tok_rows, width = queries.shape
    cols = width // head_width * (tok_rows // 2)
    hbm = pl.BlockSpec(memory_space=pltpu.HBM)
    return pl.pallas_call(
        prepare_kernel,
        out_shape=(
            jax.ShapeDtypeStruct((2, 2, cols, head_width), jnp.bfloat16),
            jax.ShapeDtypeStruct((2, 2, head_width, cols), jnp.bfloat16),
            jax.ShapeDtypeStruct(line.shape, line.dtype),
        ),
        in_specs=[hbm, hbm, vmem],
        out_specs=(vmem, vmem, vmem),
        scratch_shapes=[
            pltpu.VMEM((2, tok_rows, width), jnp.bfloat16),
            pltpu.SemaphoreType.DMA((2,)),
        ],
        compiler_params=pltpu.CompilerParams(vmem_limit_bytes=4 * 1024 * 1024),
    )(queries, out_grads, line)


def attend(ctx_count, dp_count, inner, tile, doc_lengths, stacked, flipped, pieces):
    cols, head_width = stacked.shape[2:]
    seq = ctx_count * dp_count * pieces[0].shape[0] // (ctx_count // inner)
    results = pl.pallas_call(
        functools.partial(attend_kernel, ctx_count, dp_count, inner, tile),
        out_shape=[
            jax.ShapeDtypeStruct((seq, head_width), jnp.bfloat16),
            jax.ShapeDtypeStruct((2, seq, cols), jnp.bfloat16),
        ]
        + [jax.ShapeDtypeStruct(piece.shape, jnp.bfloat16) for piece in pieces],
        in_specs=[smem] + [vmem] * (2 + len(pieces)),
        out_specs=[vmem] * (2 + len(pieces)),
        scratch_shapes=[
            pltpu.VMEM((seq, head_width), jnp.bfloat16),
            pltpu.VMEM((seq, 2 * head_width), jnp.float32),
            pltpu.VMEM((seq, cols), jnp.float32),
            pltpu.VMEM((seq, cols), jnp.float32),
            pltpu.VMEM((seq // tile, cols), jnp.float32),
        ],
        compiler_params=pltpu.CompilerParams(vmem_limit_bytes=32 * 1024 * 1024),
    )(doc_lengths, stacked, flipped, *pieces)
    return results[0], results[1], results[2:]


def query_side(ctx_count, tile, doc_lengths, keys_ordered, dlogits, order, tok_rows):
    cols = dlogits.shape[2]
    head_width = keys_ordered.shape[1]
    return pl.pallas_call(
        functools.partial(query_kernel, ctx_count, tile),
        out_shape=jax.ShapeDtypeStruct(
            (tok_rows, cols // (tok_rows // 2) * head_width), jnp.bfloat16
        ),
        in_specs=[smem, vmem, vmem, pl.BlockSpec(memory_space=pl.ANY)],
        out_specs=vmem,
        scratch_shapes=[pltpu.VMEM((head_width, cols), jnp.float32)],
        compiler_params=pltpu.CompilerParams(vmem_limit_bytes=8 * 1024 * 1024),
    )(doc_lengths, keys_ordered, dlogits, order)


def swap(value, axis, offset):
    pairs = [(index, index ^ offset) for index in range(lax.axis_size(axis))]
    return lax.ppermute(value, axis, pairs)


def total_of(terms):
    return sum(term.astype(jnp.float32) for term in terms)


def body(queries, keys, values, out_grads, doc_lengths):
    ctx_count = lax.axis_size("ctx")
    dp_count = lax.axis_size("dp")
    inner = math.gcd(4, ctx_count)
    outer = ctx_count // inner
    tok_rows, head_width = keys.shape
    part_rows = tok_rows // dp_count
    own = lax.dynamic_slice_in_dim(
        jnp.concatenate([keys, values], axis=1), lax.axis_index("dp") * part_rows, part_rows, 0
    )
    line = jnp.concatenate(
        [own] + [swap(own, "ctx", block * inner) for block in range(1, outer)], axis=0
    )
    plane = [line] + [swap(line, "ctx", offset) for offset in range(1, inner)]
    stacked, flipped, line = prepare(queries, out_grads, head_width, line)
    plane[0] = line
    pieces = plane + [
        swap(piece, "dp", offset) for offset in range(1, dp_count) for piece in plane
    ]
    tile = math.gcd(256, ctx_count * tok_rows)
    keys_ordered, dlogits, parts = attend(
        ctx_count, dp_count, inner, tile, doc_lengths, stacked, flipped, pieces
    )
    plane_sums = [
        total_of(
            [parts[offset]]
            + [swap(parts[far * inner + offset], "dp", far) for far in range(1, dp_count)]
        ).astype(jnp.bfloat16)
        for offset in range(inner)
    ]
    query_grads = query_side(
        ctx_count, tile, doc_lengths, keys_ordered, dlogits, plane_sums[-1], tok_rows
    )
    line_sum = total_of(
        [plane_sums[0]] + [swap(plane_sums[offset], "ctx", offset) for offset in range(1, inner)]
    ).astype(jnp.bfloat16)
    blocks = [line_sum[block * part_rows : (block + 1) * part_rows] for block in range(outer)]
    kv_grads = total_of(
        [blocks[0]] + [swap(blocks[block], "ctx", block * inner) for block in range(1, outer)]
    ).astype(jnp.bfloat16)
    return (query_grads, kv_grads[:, :head_width], kv_grads[:, head_width:])


def solution(mesh):
    return jax.shard_map(
        body,
        mesh=mesh,
        in_specs=(P("ctx", "dp"), P("ctx", None), P("ctx", None), P("ctx", "dp"), P()),
        out_specs=(P("ctx", "dp"), P(("ctx", "dp"), None), P(("ctx", "dp"), None)),
        check_vma=False,
    )
```

```python
import functools
import math

import jax
import jax.numpy as jnp
from jax import lax
from jax.experimental import pallas as pl
from jax.experimental.pallas import tpu as pltpu
from jax.sharding import PartitionSpec as P

masked_value = -1e30

vmem = pl.BlockSpec(memory_space=pltpu.VMEM)
smem = pl.BlockSpec(memory_space=pltpu.SMEM)
hbm = pl.BlockSpec(memory_space=pltpu.HBM)


def row_position(ctx_index, start, ctx_count, rows, span_rows):
    low = ctx_index * span_rows + start
    high = (2 * ctx_count - 1 - ctx_index) * span_rows + start - span_rows
    return pl.multiple_of(jnp.where(start < span_rows, low, high), rows)


def span_first(half, ctx_count, span_rows):
    ctx_index = lax.axis_index("ctx")
    return (ctx_index if half == 0 else 2 * ctx_count - 1 - ctx_index) * span_rows


def prepare_kernel(
    ctx_count,
    tile,
    lengths_ref,
    q_hbm,
    g_hbm,
    line_ref,
    stack_ref,
    flip_ref,
    starts_ref,
    tiles_ref,
    same_ref,
    raw_ref,
    sems,
):
    tok_rows = q_hbm.shape[0]
    head_width = stack_ref.shape[3]
    cols = stack_ref.shape[2]
    span_rows = tok_rows // 2
    copies = [
        pltpu.make_async_copy(source, raw_ref.at[slot], sems.at[slot])
        for slot, source in enumerate((q_hbm, g_hbm))
    ]
    for copy in copies:
        copy.start()
    same_ref[...] = line_ref[...]
    lane = lax.broadcasted_iota(jnp.int32, tiles_ref.shape, 1)
    tiles = jnp.zeros(tiles_ref.shape, jnp.int32)
    for half in range(2):
        first = span_first(half, ctx_count, span_rows)
        query_pos = first + lax.rem(
            lax.broadcasted_iota(jnp.int32, (1, cols), 1), jnp.int32(span_rows)
        )
        doc_start = jnp.zeros((1, cols), jnp.int32)
        first_key = jnp.int32(0)
        end = jnp.int32(0)
        for doc in range(lengths_ref.shape[0]):
            end = end + lengths_ref[doc]
            doc_start = jnp.where(query_pos >= end, end, doc_start)
            first_key = jnp.where(first >= end, end, first_key)
        starts_ref[half] = doc_start
        count = (first + span_rows - first_key + tile - 1) // tile
        tiles = jnp.where(lane == half, count, tiles)
    tiles_ref[...] = tiles
    for slot, copy in enumerate(copies):
        copy.wait()
        for half in range(2):
            for head in range(q_hbm.shape[1] // head_width):
                stack_ref[half, slot, pl.ds(head * span_rows, span_rows), :] = raw_ref[
                    slot,
                    pl.ds(half * span_rows, span_rows),
                    pl.ds(head * head_width, head_width),
                ]
            flip_ref[half, slot] = stack_ref[half, slot].T


def attend_kernel(
    ctx_count, pairs, inner, tile, tiles_ref, starts_ref, stack_ref, flip_ref, *refs
):
    outer = ctx_count // inner
    piece_count = pairs * inner
    odd_refs = refs[:piece_count]
    even_refs = refs[piece_count : 2 * piece_count]
    refs = refs[2 * piece_count :]
    keys_ref, dlogits_ref = refs[:2]
    dkv_refs = refs[2 : piece_count + 2]
    values_ref, acc_ref, terms_ref, dweights_ref, tops_ref, counts_ref, sem = refs[
        piece_count + 2 :
    ]
    cols, head_width = stack_ref.shape[2:]
    tok_rows = (keys_ref.shape[0] - tile) // ctx_count
    part_rows = tok_rows // pairs
    half_rows = part_rows // 2
    span_rows = tok_rows // 2
    scale = head_width ** (-0.5)
    ctx_index = lax.axis_index("ctx")
    dp_index = lax.axis_index("dp")
    count_copy = pltpu.make_async_copy(tiles_ref, counts_ref, sem)
    count_copy.start()

    def blocks():
        for piece in range(piece_count):
            for block in range(outer):
                owner = ctx_index ^ (piece % inner) ^ (block * inner)
                first = ((dp_index // 2) ^ (piece // inner)) * part_rows
                for part in range(2):
                    position = row_position(
                        owner, first + part * half_rows, ctx_count, half_rows, span_rows
                    )
                    yield piece, block * 2 * part_rows, part, pl.ds(tile + position, half_rows)

    dead = jnp.zeros((tile, head_width), jnp.bfloat16)
    keys_ref[:tile, :] = dead
    values_ref[:tile, :] = dead
    for parity, kv_refs in enumerate((even_refs, odd_refs)):

        @pl.when(lax.rem(dp_index, 2) == parity)
        def _():
            for piece, base, part, ordered in blocks():
                here = base + part * half_rows
                keys_ref[ordered, :] = kv_refs[piece][pl.ds(here, half_rows), :]
                values_ref[ordered, :] = kv_refs[piece][pl.ds(part_rows + here, half_rows), :]

    acc_ref[...] = jnp.zeros_like(acc_ref)
    count_copy.wait()

    for half in range(2):
        first = span_first(half, ctx_count, span_rows)
        query_pos = first + lax.rem(
            lax.broadcasted_iota(jnp.int32, (1, cols), 1), jnp.int32(span_rows)
        )
        doc_start = starts_ref[half]
        count = counts_ref[0, half]

        def tile_rows(index):
            position = first + span_rows - (index + 1) * tile
            rows = pl.ds(pl.multiple_of(tile + position, span_rows), tile)
            return position, rows, pl.ds(pl.multiple_of(index * tile, tile), tile)

        def sums_step(index, state):
            top, total, mixed = state
            position, rows, slot = tile_rows(index)
            logits = jnp.dot(
                keys_ref[rows, :], flip_ref[half, 0], preferred_element_type=jnp.float32
            )
            key_pos = lax.broadcasted_iota(jnp.int32, (tile, cols), 0)
            live = (key_pos >= doc_start - position) & (key_pos <= query_pos - position)
            logits = jnp.where(live, logits * (scale * math.log2(math.e)), masked_value)
            new_top = jnp.maximum(top, jnp.max(logits, axis=0, keepdims=True))
            terms = jnp.exp2(logits - new_top)
            dweights = jnp.dot(
                values_ref[rows, :], flip_ref[half, 1], preferred_element_type=jnp.float32
            )
            terms_ref[slot, :] = terms
            dweights_ref[slot, :] = dweights
            tops_ref[pl.ds(index, 1), :] = new_top
            decay = jnp.exp2(top - new_top)
            return (
                new_top,
                total * decay + jnp.sum(terms, axis=0, keepdims=True),
                mixed * decay + jnp.sum(terms * dweights, axis=0, keepdims=True),
            )

        zero = jnp.zeros((1, cols), jnp.float32)
        top, total, mixed = lax.fori_loop(
            0, count, sums_step, (jnp.full_like(zero, masked_value), zero, zero)
        )
        inverse = 1.0 / total
        delta = mixed * inverse

        def grads_step(index, carry):
            _, rows, slot = tile_rows(index)
            factor = jnp.exp2(tops_ref[pl.ds(index, 1), :] - top) * inverse
            weights = terms_ref[slot, :] * factor
            dlogits = (weights * (dweights_ref[slot, :] - delta)).astype(jnp.bfloat16)
            dlogits_ref[half, slot, :] = dlogits
            acc_ref[1, rows, :] += jnp.dot(
                weights.astype(jnp.bfloat16),
                stack_ref[half, 1],
                preferred_element_type=jnp.float32,
            )
            acc_ref[0, rows, :] += jnp.dot(
                dlogits, stack_ref[half, 0], preferred_element_type=jnp.float32
            )
            return carry

        lax.fori_loop(0, count, grads_step, 0)

    for piece, base, part, ordered in blocks():
        here = base + part * part_rows
        dkv_refs[piece][pl.ds(here, half_rows), :] = (scale * acc_ref[0, ordered, :]).astype(
            jnp.bfloat16
        )
        dkv_refs[piece][pl.ds(here + half_rows, half_rows), :] = acc_ref[1, ordered, :].astype(
            jnp.bfloat16
        )


def query_kernel(
    ctx_count,
    tile,
    tiles_ref,
    keys_ref,
    dlogits_ref,
    passed_ref,
    dq_ref,
    same_ref,
    sum_ref,
    counts_ref,
    sem,
):
    tok_rows = dq_ref.shape[0]
    head_width = keys_ref.shape[1]
    span_rows = tok_rows // 2
    scale = head_width ** (-0.5)
    count_copy = pltpu.make_async_copy(tiles_ref, counts_ref, sem)
    count_copy.start()
    same_ref[...] = passed_ref[...]
    count_copy.wait()
    for half in range(2):
        end = span_first(half, ctx_count, span_rows) + span_rows
        sum_ref[...] = jnp.zeros_like(sum_ref)

        def query_step(index, carry):
            rows = pl.ds(pl.multiple_of(end - index * tile, span_rows), tile)
            slot = pl.ds(pl.multiple_of(index * tile, tile), tile)
            sum_ref[...] += jnp.dot(
                keys_ref[rows, :].T, dlogits_ref[half, slot, :], preferred_element_type=jnp.float32
            )
            return carry

        lax.fori_loop(0, counts_ref[0, half], query_step, 0)
        grads = (scale * sum_ref[...]).T.astype(jnp.bfloat16)
        for head in range(dq_ref.shape[1] // head_width):
            dq_ref[
                pl.ds(half * span_rows, span_rows), pl.ds(head * head_width, head_width)
            ] = grads[head * span_rows : (head + 1) * span_rows]


def prepare(ctx_count, tile, doc_lengths, queries, out_grads, head_width, line):
    tok_rows, width = queries.shape
    cols = width // head_width * (tok_rows // 2)
    return pl.pallas_call(
        functools.partial(prepare_kernel, ctx_count, tile),
        out_shape=(
            jax.ShapeDtypeStruct((2, 2, cols, head_width), jnp.bfloat16),
            jax.ShapeDtypeStruct((2, 2, head_width, cols), jnp.bfloat16),
            jax.ShapeDtypeStruct((2, 1, cols), jnp.int32),
            jax.ShapeDtypeStruct((8, 128), jnp.int32),
            jax.ShapeDtypeStruct(line.shape, line.dtype),
        ),
        in_specs=[smem, hbm, hbm, vmem],
        out_specs=[vmem] * 5,
        scratch_shapes=[
            pltpu.VMEM((2, tok_rows, width), jnp.bfloat16),
            pltpu.SemaphoreType.DMA((2,)),
        ],
        compiler_params=pltpu.CompilerParams(vmem_limit_bytes=4 * 1024 * 1024),
    )(doc_lengths, queries, out_grads, line)


def attend(ctx_count, pairs, inner, tile, tiles, starts, stacked, flipped, odd_pieces, even_pieces):
    cols, head_width = stacked.shape[2:]
    seq = inner * pairs * odd_pieces[0].shape[0] // 2
    slots = -(-seq // tile)
    results = pl.pallas_call(
        functools.partial(attend_kernel, ctx_count, pairs, inner, tile),
        out_shape=[
            jax.ShapeDtypeStruct((tile + seq, head_width), jnp.bfloat16),
            jax.ShapeDtypeStruct((2, slots * tile, cols), jnp.bfloat16),
        ]
        + [jax.ShapeDtypeStruct(piece.shape, jnp.bfloat16) for piece in odd_pieces],
        in_specs=[vmem] * (4 + 2 * len(odd_pieces)),
        out_specs=[vmem] * (2 + len(odd_pieces)),
        scratch_shapes=[
            pltpu.VMEM((tile + seq, head_width), jnp.bfloat16),
            pltpu.VMEM((2, tile + seq, head_width), jnp.float32),
            pltpu.VMEM((slots * tile, cols), jnp.float32),
            pltpu.VMEM((slots * tile, cols), jnp.float32),
            pltpu.VMEM((slots, cols), jnp.float32),
            pltpu.SMEM((8, 128), jnp.int32),
            pltpu.SemaphoreType.DMA,
        ],
        compiler_params=pltpu.CompilerParams(vmem_limit_bytes=32 * 1024 * 1024),
    )(tiles, starts, stacked, flipped, *odd_pieces, *even_pieces)
    return results[0], results[1], results[2:]


def query_side(ctx_count, tile, tiles, keys_ordered, dlogits, passed, tok_rows):
    cols = dlogits.shape[2]
    head_width = keys_ordered.shape[1]
    return pl.pallas_call(
        functools.partial(query_kernel, ctx_count, tile),
        out_shape=(
            jax.ShapeDtypeStruct(
                (tok_rows, cols // (tok_rows // 2) * head_width), jnp.bfloat16
            ),
            jax.ShapeDtypeStruct(passed.shape, passed.dtype),
        ),
        in_specs=[vmem] * 4,
        out_specs=(vmem, vmem),
        scratch_shapes=[
            pltpu.VMEM((head_width, cols), jnp.float32),
            pltpu.SMEM((8, 128), jnp.int32),
            pltpu.SemaphoreType.DMA,
        ],
        compiler_params=pltpu.CompilerParams(vmem_limit_bytes=8 * 1024 * 1024),
    )(tiles, keys_ordered, dlogits, passed)


def swap_odd(value, axis, offset):
    ctx_count, dp_count = lax.axis_size("ctx"), lax.axis_size("dp")
    ctx_offset, dp_offset = (offset, 0) if axis == "ctx" else (0, offset)
    pairs = [
        (ctx * dp_count + dp, (ctx ^ ctx_offset) * dp_count + (dp ^ dp_offset))
        for ctx in range(ctx_count)
        for dp in range(1, dp_count, 2)
    ]
    return lax.ppermute(value, ("ctx", "dp"), pairs)


def across(value, from_odd):
    odds = range(1, lax.axis_size("dp"), 2)
    return lax.ppermute(
        value, "dp", [(dp, dp - 1) if from_odd else (dp - 1, dp) for dp in odds]
    )


def total_of(terms):
    return sum(term.astype(jnp.float32) for term in terms).astype(jnp.bfloat16)


def body(queries, keys, values, out_grads, doc_lengths):
    ctx_count = lax.axis_size("ctx")
    pairs = lax.axis_size("dp") // 2
    inner = math.gcd(4, ctx_count)
    outer = ctx_count // inner
    tok_rows, head_width = keys.shape
    part_rows = tok_rows // pairs
    tile = math.gcd(256, ctx_count * tok_rows)
    is_odd = lax.rem(lax.axis_index("dp"), 2) == 1
    if pairs > 1:
        start = lax.axis_index("dp") // 2 * part_rows
        keys = lax.dynamic_slice_in_dim(keys, start, part_rows, 0)
        values = lax.dynamic_slice_in_dim(values, start, part_rows, 0)
    own = jnp.concatenate([keys, values], axis=0)
    line = jnp.concatenate(
        [own] + [swap_odd(own, "ctx", block * inner) for block in range(1, outer)], axis=0
    )
    plane = [line] + [swap_odd(line, "ctx", offset) for offset in range(1, inner)]
    stacked, flipped, starts, tiles, plane[0] = prepare(
        ctx_count, tile, doc_lengths, queries, out_grads, head_width, line
    )
    pieces = plane + [
        swap_odd(piece, "dp", 2 * far) for far in range(1, pairs) for piece in plane
    ]
    keys_ordered, dlogits, parts = attend(
        ctx_count,
        pairs,
        inner,
        tile,
        tiles,
        starts,
        stacked,
        flipped,
        pieces,
        [across(piece, True) for piece in pieces],
    )
    chip_sums = [total_of([part, across(part, False)]) for part in parts]
    plane_sums = [
        total_of(
            [chip_sums[offset]]
            + [swap_odd(chip_sums[far * inner + offset], "dp", 2 * far) for far in range(1, pairs)]
        )
        for offset in range(inner)
    ]
    query_grads, plane_sums[0] = query_side(
        ctx_count, tile, tiles, keys_ordered, dlogits, plane_sums[0], tok_rows
    )
    line_sum = total_of(
        [plane_sums[0]]
        + [swap_odd(plane_sums[offset], "ctx", offset) for offset in range(1, inner)]
    )
    blocks = jnp.split(line_sum, outer, axis=0)
    kv_grads = total_of(
        [blocks[0]] + [swap_odd(blocks[block], "ctx", block * inner) for block in range(1, outer)]
    )
    kv_grads = jnp.where(is_odd, kv_grads[part_rows:], across(kv_grads[:part_rows], True))
    return (query_grads, kv_grads[: part_rows // 2], kv_grads[part_rows // 2 :])


def solution(mesh):
    return jax.shard_map(
        body,
        mesh=mesh,
        in_specs=(P("ctx", "dp"), P("ctx", None), P("ctx", None), P("ctx", "dp"), P()),
        out_specs=(P("ctx", "dp"), P(("ctx", "dp"), None), P(("ctx", "dp"), None)),
        check_vma=False,
    )
```

```python
import functools
import math

import jax
import jax.numpy as jnp
from jax import lax
from jax.experimental import pallas as pl
from jax.experimental.pallas import tpu as pltpu
from jax.sharding import PartitionSpec as P

masked_value = -1e30

vmem = pl.BlockSpec(memory_space=pltpu.VMEM)
smem = pl.BlockSpec(memory_space=pltpu.SMEM)
hbm = pl.BlockSpec(memory_space=pltpu.HBM)


def row_position(ctx_index, start, ctx_count, rows, span_rows):
    low = ctx_index * span_rows + start
    high = (2 * ctx_count - 1 - ctx_index) * span_rows + start - span_rows
    return pl.multiple_of(jnp.where(start < span_rows, low, high), rows)


def span_first(half, ctx_count, span_rows):
    ctx_index = lax.axis_index("ctx")
    return (ctx_index if half == 0 else 2 * ctx_count - 1 - ctx_index) * span_rows


def prepare_kernel(
    ctx_count,
    tile,
    lengths_ref,
    q_hbm,
    g_hbm,
    line_ref,
    stack_ref,
    flip_ref,
    starts_ref,
    tiles_ref,
    same_ref,
    raw_ref,
    sems,
):
    tok_rows = q_hbm.shape[0]
    head_width = stack_ref.shape[3]
    cols = stack_ref.shape[2]
    span_rows = tok_rows // 2
    copies = [
        pltpu.make_async_copy(source, raw_ref.at[slot], sems.at[slot])
        for slot, source in enumerate((q_hbm, g_hbm))
    ]
    for copy in copies:
        copy.start()
    same_ref[...] = line_ref[...]
    lane = lax.broadcasted_iota(jnp.int32, tiles_ref.shape, 1)
    tiles = jnp.zeros(tiles_ref.shape, jnp.int32)
    for half in range(2):
        first = span_first(half, ctx_count, span_rows)
        query_pos = first + lax.rem(
            lax.broadcasted_iota(jnp.int32, (1, cols), 1), jnp.int32(span_rows)
        )
        doc_start = jnp.zeros((1, cols), jnp.int32)
        first_key = jnp.int32(0)
        end = jnp.int32(0)
        for doc in range(lengths_ref.shape[0]):
            end = end + lengths_ref[doc]
            doc_start = jnp.where(query_pos >= end, end, doc_start)
            first_key = jnp.where(first >= end, end, first_key)
        starts_ref[half] = doc_start
        count = (first + span_rows - first_key + tile - 1) // tile
        tiles = jnp.where(lane == half, count, tiles)
    tiles_ref[...] = tiles
    for slot, copy in enumerate(copies):
        copy.wait()
        for half in range(2):
            for head in range(q_hbm.shape[1] // head_width):
                stack_ref[half, slot, pl.ds(head * span_rows, span_rows), :] = raw_ref[
                    slot,
                    pl.ds(half * span_rows, span_rows),
                    pl.ds(head * head_width, head_width),
                ]
            flip_ref[half, slot] = stack_ref[half, slot].T


def attend_kernel(
    ctx_count, dp_count, inner, tile, tiles_ref, starts_ref, stack_ref, flip_ref, *refs
):
    outer = ctx_count // inner
    piece_count = dp_count * inner
    kv_refs = refs[:piece_count]
    refs = refs[piece_count:]
    keys_ref, dlogits_ref = refs[:2]
    dkv_refs = refs[2 : piece_count + 2]
    values_ref, acc_ref, terms_ref, dweights_ref, tops_ref, counts_ref, sem = refs[
        piece_count + 2 :
    ]
    cols, head_width = stack_ref.shape[2:]
    tok_rows = (keys_ref.shape[0] - tile) // ctx_count
    part_rows = tok_rows // dp_count
    span_rows = tok_rows // 2
    scale = head_width ** (-0.5)
    ctx_index = lax.axis_index("ctx")
    dp_index = lax.axis_index("dp")
    count_copy = pltpu.make_async_copy(tiles_ref, counts_ref, sem)
    count_copy.start()

    def blocks():
        for piece in range(piece_count):
            for block in range(outer):
                owner = ctx_index ^ (piece % inner) ^ (block * inner)
                first = (dp_index ^ (piece // inner)) * part_rows
                position = row_position(owner, first, ctx_count, part_rows, span_rows)
                yield (
                    piece,
                    pl.ds(block * part_rows, part_rows),
                    pl.ds(tile + position, part_rows),
                )

    dead = jnp.zeros((tile, head_width), jnp.bfloat16)
    keys_ref[:tile, :] = dead
    values_ref[:tile, :] = dead
    for piece, here, ordered in blocks():
        keys_ref[ordered, :] = kv_refs[piece][here, :head_width]
        values_ref[ordered, :] = kv_refs[piece][here, head_width:]
    acc_ref[...] = jnp.zeros_like(acc_ref)
    count_copy.wait()

    for half in range(2):
        first = span_first(half, ctx_count, span_rows)
        query_pos = first + lax.rem(
            lax.broadcasted_iota(jnp.int32, (1, cols), 1), jnp.int32(span_rows)
        )
        doc_start = starts_ref[half]
        count = counts_ref[0, half]

        def tile_rows(index):
            position = first + span_rows - (index + 1) * tile
            rows = pl.ds(pl.multiple_of(tile + position, span_rows), tile)
            return position, rows, pl.ds(pl.multiple_of(index * tile, tile), tile)

        def sums_step(index, state):
            top, total, mixed = state
            position, rows, slot = tile_rows(index)
            logits = jnp.dot(
                keys_ref[rows, :], flip_ref[half, 0], preferred_element_type=jnp.float32
            )
            key_pos = lax.broadcasted_iota(jnp.int32, (tile, cols), 0)
            live = (key_pos >= doc_start - position) & (key_pos <= query_pos - position)
            logits = jnp.where(live, logits * (scale * math.log2(math.e)), masked_value)
            new_top = jnp.maximum(top, jnp.max(logits, axis=0, keepdims=True))
            terms = jnp.exp2(logits - new_top)
            dweights = jnp.dot(
                values_ref[rows, :], flip_ref[half, 1], preferred_element_type=jnp.float32
            )
            terms_ref[slot, :] = terms
            dweights_ref[slot, :] = dweights
            tops_ref[pl.ds(index, 1), :] = new_top
            decay = jnp.exp2(top - new_top)
            return (
                new_top,
                total * decay + jnp.sum(terms, axis=0, keepdims=True),
                mixed * decay + jnp.sum(terms * dweights, axis=0, keepdims=True),
            )

        zero = jnp.zeros((1, cols), jnp.float32)
        top, total, mixed = lax.fori_loop(
            0, count, sums_step, (jnp.full_like(zero, masked_value), zero, zero)
        )
        inverse = 1.0 / total
        delta = mixed * inverse

        def grads_step(index, carry):
            _, rows, slot = tile_rows(index)
            factor = jnp.exp2(tops_ref[pl.ds(index, 1), :] - top) * inverse
            weights = terms_ref[slot, :] * factor
            dlogits = (weights * (dweights_ref[slot, :] - delta)).astype(jnp.bfloat16)
            dlogits_ref[half, slot, :] = dlogits
            acc_ref[1, rows, :] += jnp.dot(
                weights.astype(jnp.bfloat16),
                stack_ref[half, 1],
                preferred_element_type=jnp.float32,
            )
            acc_ref[0, rows, :] += jnp.dot(
                dlogits, stack_ref[half, 0], preferred_element_type=jnp.float32
            )
            return carry

        lax.fori_loop(0, count, grads_step, 0)

    for piece, here, ordered in blocks():
        dkv_refs[piece][here, :head_width] = (scale * acc_ref[0, ordered, :]).astype(jnp.bfloat16)
        dkv_refs[piece][here, head_width:] = acc_ref[1, ordered, :].astype(jnp.bfloat16)


def query_kernel(
    ctx_count,
    tile,
    tiles_ref,
    keys_ref,
    dlogits_ref,
    passed_ref,
    dq_ref,
    same_ref,
    sum_ref,
    counts_ref,
    sem,
):
    tok_rows = dq_ref.shape[0]
    head_width = keys_ref.shape[1]
    span_rows = tok_rows // 2
    scale = head_width ** (-0.5)
    count_copy = pltpu.make_async_copy(tiles_ref, counts_ref, sem)
    count_copy.start()
    same_ref[...] = passed_ref[...]
    count_copy.wait()
    for half in range(2):
        end = span_first(half, ctx_count, span_rows) + span_rows
        sum_ref[...] = jnp.zeros_like(sum_ref)

        def query_step(index, carry):
            rows = pl.ds(pl.multiple_of(end - index * tile, span_rows), tile)
            slot = pl.ds(pl.multiple_of(index * tile, tile), tile)
            sum_ref[...] += jnp.dot(
                keys_ref[rows, :].T, dlogits_ref[half, slot, :], preferred_element_type=jnp.float32
            )
            return carry

        lax.fori_loop(0, counts_ref[0, half], query_step, 0)
        grads = (scale * sum_ref[...]).T.astype(jnp.bfloat16)
        for head in range(dq_ref.shape[1] // head_width):
            dq_ref[
                pl.ds(half * span_rows, span_rows), pl.ds(head * head_width, head_width)
            ] = grads[head * span_rows : (head + 1) * span_rows]


def prepare(ctx_count, tile, doc_lengths, queries, out_grads, head_width, line):
    tok_rows, width = queries.shape
    cols = width // head_width * (tok_rows // 2)
    return pl.pallas_call(
        functools.partial(prepare_kernel, ctx_count, tile),
        out_shape=(
            jax.ShapeDtypeStruct((2, 2, cols, head_width), jnp.bfloat16),
            jax.ShapeDtypeStruct((2, 2, head_width, cols), jnp.bfloat16),
            jax.ShapeDtypeStruct((2, 1, cols), jnp.int32),
            jax.ShapeDtypeStruct((8, 128), jnp.int32),
            jax.ShapeDtypeStruct(line.shape, line.dtype),
        ),
        in_specs=[smem, hbm, hbm, vmem],
        out_specs=[vmem] * 5,
        scratch_shapes=[
            pltpu.VMEM((2, tok_rows, width), jnp.bfloat16),
            pltpu.SemaphoreType.DMA((2,)),
        ],
        compiler_params=pltpu.CompilerParams(vmem_limit_bytes=4 * 1024 * 1024),
    )(doc_lengths, queries, out_grads, line)


def attend(ctx_count, dp_count, inner, tile, tiles, starts, stacked, flipped, pieces):
    cols, head_width = stacked.shape[2:]
    seq = dp_count * inner * pieces[0].shape[0]
    slots = -(-seq // tile)
    results = pl.pallas_call(
        functools.partial(attend_kernel, ctx_count, dp_count, inner, tile),
        out_shape=[
            jax.ShapeDtypeStruct((tile + seq, head_width), jnp.bfloat16),
            jax.ShapeDtypeStruct((2, slots * tile, cols), jnp.bfloat16),
        ]
        + [jax.ShapeDtypeStruct(piece.shape, jnp.bfloat16) for piece in pieces],
        in_specs=[vmem] * (4 + len(pieces)),
        out_specs=[vmem] * (2 + len(pieces)),
        scratch_shapes=[
            pltpu.VMEM((tile + seq, head_width), jnp.bfloat16),
            pltpu.VMEM((2, tile + seq, head_width), jnp.float32),
            pltpu.VMEM((slots * tile, cols), jnp.float32),
            pltpu.VMEM((slots * tile, cols), jnp.float32),
            pltpu.VMEM((slots, cols), jnp.float32),
            pltpu.SMEM((8, 128), jnp.int32),
            pltpu.SemaphoreType.DMA,
        ],
        compiler_params=pltpu.CompilerParams(vmem_limit_bytes=32 * 1024 * 1024),
    )(tiles, starts, stacked, flipped, *pieces)
    return results[0], results[1], results[2:]


def query_side(ctx_count, tile, tiles, keys_ordered, dlogits, passed, tok_rows):
    cols = dlogits.shape[2]
    head_width = keys_ordered.shape[1]
    return pl.pallas_call(
        functools.partial(query_kernel, ctx_count, tile),
        out_shape=(
            jax.ShapeDtypeStruct(
                (tok_rows, cols // (tok_rows // 2) * head_width), jnp.bfloat16
            ),
            jax.ShapeDtypeStruct(passed.shape, passed.dtype),
        ),
        in_specs=[vmem] * 4,
        out_specs=(vmem, vmem),
        scratch_shapes=[
            pltpu.VMEM((head_width, cols), jnp.float32),
            pltpu.SMEM((8, 128), jnp.int32),
            pltpu.SemaphoreType.DMA,
        ],
        compiler_params=pltpu.CompilerParams(vmem_limit_bytes=8 * 1024 * 1024),
    )(tiles, keys_ordered, dlogits, passed)


def swap(value, axis, offset):
    pairs = [(index, index ^ offset) for index in range(lax.axis_size(axis))]
    return lax.ppermute(value, axis, pairs)


def total_of(terms):
    return sum(term.astype(jnp.float32) for term in terms).astype(jnp.bfloat16)


def body(queries, keys, values, out_grads, doc_lengths):
    ctx_count = lax.axis_size("ctx")
    dp_count = lax.axis_size("dp")
    inner = math.gcd(4, ctx_count)
    outer = ctx_count // inner
    tok_rows, head_width = keys.shape
    part_rows = tok_rows // dp_count
    tile = math.gcd(256, ctx_count * tok_rows)
    own = lax.dynamic_slice_in_dim(
        jnp.concatenate([keys, values], axis=1), lax.axis_index("dp") * part_rows, part_rows, 0
    )
    line = jnp.concatenate(
        [own] + [swap(own, "ctx", block * inner) for block in range(1, outer)], axis=0
    )
    plane = [line] + [swap(line, "ctx", offset) for offset in range(1, inner)]
    stacked, flipped, starts, tiles, plane[0] = prepare(
        ctx_count, tile, doc_lengths, queries, out_grads, head_width, line
    )
    pieces = plane + [
        swap(piece, "dp", offset) for offset in range(1, dp_count) for piece in plane
    ]
    keys_ordered, dlogits, parts = attend(
        ctx_count, dp_count, inner, tile, tiles, starts, stacked, flipped, pieces
    )
    plane_sums = [
        total_of(
            [parts[offset]]
            + [swap(parts[far * inner + offset], "dp", far) for far in range(1, dp_count)]
        )
        for offset in range(inner)
    ]
    query_grads, plane_sums[0] = query_side(
        ctx_count, tile, tiles, keys_ordered, dlogits, plane_sums[0], tok_rows
    )
    line_sum = total_of(
        [plane_sums[0]] + [swap(plane_sums[offset], "ctx", offset) for offset in range(1, inner)]
    )
    blocks = jnp.split(line_sum, outer, axis=0)
    kv_grads = total_of(
        [blocks[0]] + [swap(blocks[block], "ctx", block * inner) for block in range(1, outer)]
    )
    return (query_grads, kv_grads[:, :head_width], kv_grads[:, head_width:])


def solution(mesh):
    return jax.shard_map(
        body,
        mesh=mesh,
        in_specs=(P("ctx", "dp"), P("ctx", None), P("ctx", None), P("ctx", "dp"), P()),
        out_specs=(P("ctx", "dp"), P(("ctx", "dp"), None), P(("ctx", "dp"), None)),
        check_vma=False,
    )
```

```python
import functools
import math

import jax
import jax.numpy as jnp
from jax import lax
from jax.experimental import pallas as pl
from jax.experimental.pallas import tpu as pltpu
from jax.sharding import PartitionSpec as P

masked_value = -1e30

vmem = pl.BlockSpec(memory_space=pltpu.VMEM)
smem = pl.BlockSpec(memory_space=pltpu.SMEM)
hbm = pl.BlockSpec(memory_space=pltpu.HBM)


def row_position(ctx_index, start, ctx_count, rows, span_rows):
    low = ctx_index * span_rows + start
    high = (2 * ctx_count - 1 - ctx_index) * span_rows + start - span_rows
    return pl.multiple_of(jnp.where(start < span_rows, low, high), rows)


def span_first(half, ctx_count, span_rows):
    ctx_index = lax.axis_index("ctx")
    return (ctx_index if half == 0 else 2 * ctx_count - 1 - ctx_index) * span_rows


def prepare_kernel(
    ctx_count,
    tile,
    lengths_ref,
    q_hbm,
    g_hbm,
    line_ref,
    stack_ref,
    flip_ref,
    starts_ref,
    tiles_ref,
    same_ref,
    raw_ref,
    sems,
):
    tok_rows = q_hbm.shape[0]
    head_width = stack_ref.shape[3]
    cols = stack_ref.shape[2]
    span_rows = tok_rows // 2
    copies = [
        pltpu.make_async_copy(source, raw_ref.at[slot], sems.at[slot])
        for slot, source in enumerate((q_hbm, g_hbm))
    ]
    for copy in copies:
        copy.start()
    same_ref[...] = line_ref[...]
    lane = lax.broadcasted_iota(jnp.int32, tiles_ref.shape, 1)
    tiles = jnp.zeros(tiles_ref.shape, jnp.int32)
    for half in range(2):
        first = span_first(half, ctx_count, span_rows)
        query_pos = first + lax.rem(
            lax.broadcasted_iota(jnp.int32, (1, cols), 1), jnp.int32(span_rows)
        )
        doc_start = jnp.zeros((1, cols), jnp.int32)
        first_key = jnp.int32(0)
        end = jnp.int32(0)
        for doc in range(lengths_ref.shape[0]):
            end = end + lengths_ref[doc]
            doc_start = jnp.where(query_pos >= end, end, doc_start)
            first_key = jnp.where(first >= end, end, first_key)
        starts_ref[half] = doc_start
        count = (first + span_rows - first_key + tile - 1) // tile
        tiles = jnp.where(lane == half, count, tiles)
    tiles_ref[...] = tiles
    for slot, copy in enumerate(copies):
        copy.wait()
        for half in range(2):
            for head in range(q_hbm.shape[1] // head_width):
                stack_ref[half, slot, pl.ds(head * span_rows, span_rows), :] = raw_ref[
                    slot,
                    pl.ds(half * span_rows, span_rows),
                    pl.ds(head * head_width, head_width),
                ]
            flip_ref[half, slot] = stack_ref[half, slot].T


def part_moves(ctx_count, dp_count, inner, part_rows, ctx_index, dp_index):
    for piece in range(dp_count * inner):
        for block in range(ctx_count // inner):
            owner = ctx_index ^ (piece % inner) ^ (block * inner)
            yield piece, block * part_rows, owner, (dp_index ^ (piece // inner)) * part_rows


def two_axis_moves(inner, part_rows, ctx_index, dp_index):
    def place(own_side, near, far=0):
        odd_first, even_first = (near * inner) ^ far, near ^ (far * inner)
        if not own_side:
            odd_first, even_first = even_first, odd_first
        return ctx_index ^ jnp.where(dp_index == 1, odd_first, even_first)

    for part in range(2):
        yield 0, part * part_rows, ctx_index, part * part_rows
        for side in range(2):
            for near in range(1, inner):
                row = (2 * (near - 1) + part) * part_rows
                yield 1 + side, row, place(side == 0, near), part * part_rows
    for side in range(2):
        for far in range(1, inner):
            for near in range(1, inner):
                piece = 3 + side * (inner - 1) + far - 1
                owner = place(side == 0, near, far)
                yield piece, (near - 1) * part_rows, owner, (dp_index ^ side) * part_rows


def attend_kernel(
    ctx_count,
    dp_count,
    inner,
    tile,
    moves,
    piece_count,
    tiles_ref,
    starts_ref,
    stack_ref,
    flip_ref,
    *refs,
):
    outer = ctx_count // inner
    part_count = dp_count * inner
    kv_refs = refs[:piece_count]
    refs = refs[piece_count:]
    keys_ref, dlogits_ref = refs[:2]
    dkv_refs = refs[2 : part_count + 2]
    values_ref, acc_ref, terms_ref, dweights_ref, tops_ref, counts_ref, sem = refs[
        part_count + 2 :
    ]
    cols, head_width = stack_ref.shape[2:]
    tok_rows = (keys_ref.shape[0] - tile) // ctx_count
    part_rows = tok_rows // dp_count
    span_rows = tok_rows // 2
    scale = head_width ** (-0.5)
    ctx_index = lax.axis_index("ctx")
    dp_index = lax.axis_index("dp")
    count_copy = pltpu.make_async_copy(tiles_ref, counts_ref, sem)
    count_copy.start()

    def ordered_rows(owner, start):
        position = row_position(owner, start, ctx_count, part_rows, span_rows)
        return pl.ds(tile + position, part_rows)

    dead = jnp.zeros((tile, head_width), jnp.bfloat16)
    keys_ref[:tile, :] = dead
    values_ref[:tile, :] = dead
    for piece, row, owner, start in moves(ctx_index, dp_index):
        here, ordered = pl.ds(row, part_rows), ordered_rows(owner, start)
        keys_ref[ordered, :] = kv_refs[piece][here, :head_width]
        values_ref[ordered, :] = kv_refs[piece][here, head_width:]
    acc_ref[...] = jnp.zeros_like(acc_ref)
    count_copy.wait()

    for half in range(2):
        first = span_first(half, ctx_count, span_rows)
        query_pos = first + lax.rem(
            lax.broadcasted_iota(jnp.int32, (1, cols), 1), jnp.int32(span_rows)
        )
        doc_start = starts_ref[half]
        count = counts_ref[0, half]

        def tile_rows(index):
            position = first + span_rows - (index + 1) * tile
            rows = pl.ds(pl.multiple_of(tile + position, span_rows), tile)
            return position, rows, pl.ds(pl.multiple_of(index * tile, tile), tile)

        def sums_step(index, state):
            top, total, mixed = state
            position, rows, slot = tile_rows(index)
            logits = jnp.dot(
                keys_ref[rows, :], flip_ref[half, 0], preferred_element_type=jnp.float32
            )
            key_pos = lax.broadcasted_iota(jnp.int32, (tile, cols), 0)
            live = (key_pos >= doc_start - position) & (key_pos <= query_pos - position)
            logits = jnp.where(live, logits * (scale * math.log2(math.e)), masked_value)
            new_top = jnp.maximum(top, jnp.max(logits, axis=0, keepdims=True))
            terms = jnp.exp2(logits - new_top)
            dweights = jnp.dot(
                values_ref[rows, :], flip_ref[half, 1], preferred_element_type=jnp.float32
            )
            terms_ref[slot, :] = terms
            dweights_ref[slot, :] = dweights
            tops_ref[pl.ds(index, 1), :] = new_top
            decay = jnp.exp2(top - new_top)
            return (
                new_top,
                total * decay + jnp.sum(terms, axis=0, keepdims=True),
                mixed * decay + jnp.sum(terms * dweights, axis=0, keepdims=True),
            )

        zero = jnp.zeros((1, cols), jnp.float32)
        top, total, mixed = lax.fori_loop(
            0, count, sums_step, (jnp.full_like(zero, masked_value), zero, zero)
        )
        inverse = 1.0 / total
        delta = mixed * inverse

        def grads_step(index, carry):
            _, rows, slot = tile_rows(index)
            factor = jnp.exp2(tops_ref[pl.ds(index, 1), :] - top) * inverse
            weights = terms_ref[slot, :] * factor
            dlogits = (weights * (dweights_ref[slot, :] - delta)).astype(jnp.bfloat16)
            dlogits_ref[half, slot, :] = dlogits
            acc_ref[1, rows, :] += jnp.dot(
                weights.astype(jnp.bfloat16),
                stack_ref[half, 1],
                preferred_element_type=jnp.float32,
            )
            acc_ref[0, rows, :] += jnp.dot(
                dlogits, stack_ref[half, 0], preferred_element_type=jnp.float32
            )
            return carry

        lax.fori_loop(0, count, grads_step, 0)

    for piece, row, owner, start in part_moves(
        ctx_count, dp_count, inner, part_rows, ctx_index, dp_index
    ):
        here, ordered = pl.ds(row, part_rows), ordered_rows(owner, start)
        dkv_refs[piece][here, :head_width] = (scale * acc_ref[0, ordered, :]).astype(jnp.bfloat16)
        dkv_refs[piece][here, head_width:] = acc_ref[1, ordered, :].astype(jnp.bfloat16)


def query_kernel(
    ctx_count,
    tile,
    tiles_ref,
    keys_ref,
    dlogits_ref,
    passed_ref,
    dq_ref,
    same_ref,
    sum_ref,
    counts_ref,
    sem,
):
    tok_rows = dq_ref.shape[0]
    head_width = keys_ref.shape[1]
    span_rows = tok_rows // 2
    scale = head_width ** (-0.5)
    count_copy = pltpu.make_async_copy(tiles_ref, counts_ref, sem)
    count_copy.start()
    same_ref[...] = passed_ref[...]
    count_copy.wait()
    for half in range(2):
        end = span_first(half, ctx_count, span_rows) + span_rows
        sum_ref[...] = jnp.zeros_like(sum_ref)

        def query_step(index, carry):
            rows = pl.ds(pl.multiple_of(end - index * tile, span_rows), tile)
            slot = pl.ds(pl.multiple_of(index * tile, tile), tile)
            sum_ref[...] += jnp.dot(
                keys_ref[rows, :].T, dlogits_ref[half, slot, :], preferred_element_type=jnp.float32
            )
            return carry

        lax.fori_loop(0, counts_ref[0, half], query_step, 0)
        grads = (scale * sum_ref[...]).T.astype(jnp.bfloat16)
        for head in range(dq_ref.shape[1] // head_width):
            dq_ref[
                pl.ds(half * span_rows, span_rows), pl.ds(head * head_width, head_width)
            ] = grads[head * span_rows : (head + 1) * span_rows]


def prepare(ctx_count, tile, doc_lengths, queries, out_grads, head_width, line):
    tok_rows, width = queries.shape
    cols = width // head_width * (tok_rows // 2)
    return pl.pallas_call(
        functools.partial(prepare_kernel, ctx_count, tile),
        out_shape=(
            jax.ShapeDtypeStruct((2, 2, cols, head_width), jnp.bfloat16),
            jax.ShapeDtypeStruct((2, 2, head_width, cols), jnp.bfloat16),
            jax.ShapeDtypeStruct((2, 1, cols), jnp.int32),
            jax.ShapeDtypeStruct((8, 128), jnp.int32),
            jax.ShapeDtypeStruct(line.shape, line.dtype),
        ),
        in_specs=[smem, hbm, hbm, vmem],
        out_specs=[vmem] * 5,
        scratch_shapes=[
            pltpu.VMEM((2, tok_rows, width), jnp.bfloat16),
            pltpu.SemaphoreType.DMA((2,)),
        ],
        compiler_params=pltpu.CompilerParams(vmem_limit_bytes=4 * 1024 * 1024),
    )(doc_lengths, queries, out_grads, line)


def attend(ctx_count, dp_count, inner, tile, moves, tiles, starts, stacked, flipped, pieces, seq):
    cols, head_width = stacked.shape[2:]
    part_count = dp_count * inner
    part = jax.ShapeDtypeStruct((seq // part_count, 2 * head_width), jnp.bfloat16)
    slots = -(-seq // tile)
    results = pl.pallas_call(
        functools.partial(
            attend_kernel, ctx_count, dp_count, inner, tile, moves, len(pieces)
        ),
        out_shape=[
            jax.ShapeDtypeStruct((tile + seq, head_width), jnp.bfloat16),
            jax.ShapeDtypeStruct((2, slots * tile, cols), jnp.bfloat16),
        ]
        + [part] * part_count,
        in_specs=[vmem] * (4 + len(pieces)),
        out_specs=[vmem] * (2 + part_count),
        scratch_shapes=[
            pltpu.VMEM((tile + seq, head_width), jnp.bfloat16),
            pltpu.VMEM((2, tile + seq, head_width), jnp.float32),
            pltpu.VMEM((slots * tile, cols), jnp.float32),
            pltpu.VMEM((slots * tile, cols), jnp.float32),
            pltpu.VMEM((slots, cols), jnp.float32),
            pltpu.SMEM((8, 128), jnp.int32),
            pltpu.SemaphoreType.DMA,
        ],
        compiler_params=pltpu.CompilerParams(vmem_limit_bytes=32 * 1024 * 1024),
    )(tiles, starts, stacked, flipped, *pieces)
    return results[0], results[1], results[2:]


def query_side(ctx_count, tile, tiles, keys_ordered, dlogits, passed, tok_rows):
    cols = dlogits.shape[2]
    head_width = keys_ordered.shape[1]
    return pl.pallas_call(
        functools.partial(query_kernel, ctx_count, tile),
        out_shape=(
            jax.ShapeDtypeStruct(
                (tok_rows, cols // (tok_rows // 2) * head_width), jnp.bfloat16
            ),
            jax.ShapeDtypeStruct(passed.shape, passed.dtype),
        ),
        in_specs=[vmem] * 4,
        out_specs=(vmem, vmem),
        scratch_shapes=[
            pltpu.VMEM((head_width, cols), jnp.float32),
            pltpu.SMEM((8, 128), jnp.int32),
            pltpu.SemaphoreType.DMA,
        ],
        compiler_params=pltpu.CompilerParams(vmem_limit_bytes=8 * 1024 * 1024),
    )(tiles, keys_ordered, dlogits, passed)


def swap(value, axis, offset):
    pairs = [(index, index ^ offset) for index in range(lax.axis_size(axis))]
    return lax.ppermute(value, axis, pairs)


def total_of(terms):
    return sum(term.astype(jnp.float32) for term in terms).astype(jnp.bfloat16)


def swap_axes(value, inner, odd_step, even_step):
    ctx_count = lax.axis_size("ctx")
    pairs = [
        (2 * ctx + dp, 2 * (ctx ^ (odd_step if dp else even_step)) + dp)
        for ctx in range(ctx_count)
        for dp in range(2)
    ]
    return lax.ppermute(value, ("ctx", "dp"), pairs)


def halves(value, part_rows):
    return lax.dynamic_slice_in_dim(value, lax.axis_index("dp") * part_rows, part_rows, 0)


def gather_two_axes(keys, values, inner, part_rows, run_prepare):
    tok_rows, head_width = keys.shape
    lane = lax.broadcasted_iota(jnp.int32, (tok_rows, 2 * head_width), 1)
    zero = jnp.zeros((), keys.dtype)
    own = jnp.where(
        lane < head_width,
        lax.pad(keys, zero, ((0, 0, 0), (0, head_width, 0))),
        lax.pad(values, zero, ((0, 0, 0), (head_width, 0, 0))),
    )
    shards = [swap_axes(own, inner, step * inner, step) for step in range(1, inner)]
    near = jnp.concatenate(shards, axis=0)
    half_near = jnp.concatenate([halves(shard, part_rows) for shard in shards], axis=0)
    others = [swap_axes(half_near, inner, step, step * inner) for step in range(1, inner)]
    prepared, near = run_prepare(near)
    pieces = [own, near, swap(near, "dp", 1)] + others + [swap(piece, "dp", 1) for piece in others]
    return prepared, pieces


def gather_in_stages(keys, values, inner, part_rows, run_prepare):
    outer = lax.axis_size("ctx") // inner
    own = halves(jnp.concatenate([keys, values], axis=1), part_rows)
    line = jnp.concatenate(
        [own] + [swap(own, "ctx", block * inner) for block in range(1, outer)], axis=0
    )
    plane = [line] + [swap(line, "ctx", offset) for offset in range(1, inner)]
    prepared, plane[0] = run_prepare(line)
    pieces = plane + [
        swap(piece, "dp", offset)
        for offset in range(1, lax.axis_size("dp"))
        for piece in plane
    ]
    return prepared, pieces


def body(queries, keys, values, out_grads, doc_lengths):
    ctx_count = lax.axis_size("ctx")
    dp_count = lax.axis_size("dp")
    inner = math.gcd(4, ctx_count)
    outer = ctx_count // inner
    tok_rows, head_width = keys.shape
    part_rows = tok_rows // dp_count
    seq = ctx_count * tok_rows
    tile = math.gcd(256, seq)

    def run_prepare(held):
        *prepared, held = prepare(
            ctx_count, tile, doc_lengths, queries, out_grads, head_width, held
        )
        return prepared, held

    if outer == inner and dp_count == 2:
        gather, moves = gather_two_axes, functools.partial(two_axis_moves, inner, part_rows)
    else:
        gather = gather_in_stages
        moves = functools.partial(part_moves, ctx_count, dp_count, inner, part_rows)
    (stacked, flipped, starts, tiles), pieces = gather(
        keys, values, inner, part_rows, run_prepare
    )
    keys_ordered, dlogits, parts = attend(
        ctx_count, dp_count, inner, tile, moves, tiles, starts, stacked, flipped, pieces, seq
    )
    plane_sums = [
        total_of(
            [parts[offset]]
            + [swap(parts[far * inner + offset], "dp", far) for far in range(1, dp_count)]
        )
        for offset in range(inner)
    ]
    query_grads, plane_sums[0] = query_side(
        ctx_count, tile, tiles, keys_ordered, dlogits, plane_sums[0], tok_rows
    )
    line_sum = total_of(
        [plane_sums[0]] + [swap(plane_sums[offset], "ctx", offset) for offset in range(1, inner)]
    )
    blocks = jnp.split(line_sum, outer, axis=0)
    kv_grads = total_of(
        [blocks[0]] + [swap(blocks[block], "ctx", block * inner) for block in range(1, outer)]
    )
    return (query_grads, kv_grads[:, :head_width], kv_grads[:, head_width:])


def solution(mesh):
    return jax.shard_map(
        body,
        mesh=mesh,
        in_specs=(P("ctx", "dp"), P("ctx", None), P("ctx", None), P("ctx", "dp"), P()),
        out_specs=(P("ctx", "dp"), P(("ctx", "dp"), None), P(("ctx", "dp"), None)),
        check_vma=False,
    )
```

```python
import functools
import math

import jax
import jax.numpy as jnp
from jax import lax
from jax.experimental import pallas as pl
from jax.experimental.pallas import tpu as pltpu
from jax.sharding import PartitionSpec as P

masked_value = -1e30

vmem = pl.BlockSpec(memory_space=pltpu.VMEM)
smem = pl.BlockSpec(memory_space=pltpu.SMEM)
hbm = pl.BlockSpec(memory_space=pltpu.HBM)


def row_position(ctx_index, start, ctx_count, rows, span_rows):
    low = ctx_index * span_rows + start
    high = (2 * ctx_count - 1 - ctx_index) * span_rows + start - span_rows
    return pl.multiple_of(jnp.where(start < span_rows, low, high), rows)


def span_first(half, ctx_count, span_rows):
    ctx_index = lax.axis_index("ctx")
    return (ctx_index if half == 0 else 2 * ctx_count - 1 - ctx_index) * span_rows


def prepare_kernel(
    ctx_count,
    tile,
    lengths_hbm,
    q_hbm,
    g_hbm,
    line_ref,
    stack_ref,
    flip_ref,
    starts_ref,
    tiles_ref,
    same_ref,
    raw_ref,
    lengths_ref,
    sems,
):
    tok_rows = q_hbm.shape[0]
    head_width = stack_ref.shape[3]
    cols = stack_ref.shape[2]
    span_rows = tok_rows // 2
    copies = [
        pltpu.make_async_copy(source, raw_ref.at[slot], sems.at[slot])
        for slot, source in enumerate((q_hbm, g_hbm))
    ]
    for copy in copies:
        copy.start()
    lengths_copy = pltpu.make_async_copy(lengths_hbm, lengths_ref, sems.at[2])
    lengths_copy.start()
    same_ref[...] = line_ref[...]
    lane = lax.broadcasted_iota(jnp.int32, tiles_ref.shape, 1)
    tiles = jnp.zeros(tiles_ref.shape, jnp.int32)
    lengths_copy.wait()
    for half in range(2):
        first = span_first(half, ctx_count, span_rows)
        query_pos = first + lax.rem(
            lax.broadcasted_iota(jnp.int32, (1, cols), 1), jnp.int32(span_rows)
        )
        doc_start = jnp.zeros((1, cols), jnp.int32)
        first_key = jnp.int32(0)
        end = jnp.int32(0)
        for doc in range(lengths_ref.shape[0]):
            end = end + lengths_ref[doc]
            doc_start = jnp.where(query_pos >= end, end, doc_start)
            first_key = jnp.where(first >= end, end, first_key)
        starts_ref[half] = doc_start
        count = (first + span_rows - first_key + tile - 1) // tile
        tiles = jnp.where(lane == half, count, tiles)
    tiles_ref[...] = tiles
    for slot, copy in enumerate(copies):
        copy.wait()
        for half in range(2):
            for head in range(q_hbm.shape[1] // head_width):
                stack_ref[half, slot, pl.ds(head * span_rows, span_rows), :] = raw_ref[
                    slot,
                    pl.ds(half * span_rows, span_rows),
                    pl.ds(head * head_width, head_width),
                ]
            flip_ref[half, slot] = stack_ref[half, slot].T


def part_moves(ctx_count, dp_count, inner, part_rows, ctx_index, dp_index):
    for piece in range(dp_count * inner):
        for block in range(ctx_count // inner):
            owner = ctx_index ^ (piece % inner) ^ (block * inner)
            yield piece, block * part_rows, owner, (dp_index ^ (piece // inner)) * part_rows


def two_axis_moves(inner, part_rows, ctx_index, dp_index):
    def place(own_side, near, far=0):
        odd_first, even_first = (near * inner) ^ far, near ^ (far * inner)
        if not own_side:
            odd_first, even_first = even_first, odd_first
        return ctx_index ^ jnp.where(dp_index == 1, odd_first, even_first)

    for part in range(2):
        yield 0, part * part_rows, ctx_index, part * part_rows
        for side in range(2):
            for near in range(1, inner):
                row = (2 * (near - 1) + part) * part_rows
                yield 1 + side, row, place(side == 0, near), part * part_rows
    for side in range(2):
        for far in range(1, inner):
            for near in range(1, inner):
                piece = 3 + side * (inner - 1) + far - 1
                owner = place(side == 0, near, far)
                yield piece, (near - 1) * part_rows, owner, (dp_index ^ side) * part_rows


def attend_kernel(
    ctx_count,
    dp_count,
    inner,
    tile,
    moves,
    piece_count,
    tiles_ref,
    starts_ref,
    stack_ref,
    flip_ref,
    *refs,
):
    outer = ctx_count // inner
    part_count = dp_count * inner
    kv_refs = refs[:piece_count]
    refs = refs[piece_count:]
    keys_ref, dlogits_ref = refs[:2]
    dkv_refs = refs[2 : part_count + 2]
    values_ref, acc_ref, terms_ref, dweights_ref, tops_ref, counts_ref, sem = refs[
        part_count + 2 :
    ]
    cols, head_width = stack_ref.shape[2:]
    tok_rows = (keys_ref.shape[0] - tile) // ctx_count
    part_rows = tok_rows // dp_count
    span_rows = tok_rows // 2
    scale = head_width ** (-0.5)
    ctx_index = lax.axis_index("ctx")
    dp_index = lax.axis_index("dp")
    count_copy = pltpu.make_async_copy(tiles_ref, counts_ref, sem)
    count_copy.start()

    def ordered_rows(owner, start):
        position = row_position(owner, start, ctx_count, part_rows, span_rows)
        return pl.ds(tile + position, part_rows)

    dead = jnp.zeros((tile, head_width), jnp.bfloat16)
    keys_ref[:tile, :] = dead
    values_ref[:tile, :] = dead
    for piece, row, owner, start in moves(ctx_index, dp_index):
        here, ordered = pl.ds(row, part_rows), ordered_rows(owner, start)
        keys_ref[ordered, :] = kv_refs[piece][here, :head_width]
        values_ref[ordered, :] = kv_refs[piece][here, head_width:]
    acc_ref[...] = jnp.zeros_like(acc_ref)
    count_copy.wait()

    for half in range(2):
        first = span_first(half, ctx_count, span_rows)
        query_pos = first + lax.rem(
            lax.broadcasted_iota(jnp.int32, (1, cols), 1), jnp.int32(span_rows)
        )
        doc_start = starts_ref[half]
        count = counts_ref[0, half]

        def tile_rows(index):
            position = first + span_rows - (index + 1) * tile
            rows = pl.ds(pl.multiple_of(tile + position, span_rows), tile)
            return position, rows, pl.ds(pl.multiple_of(index * tile, tile), tile)

        def sums_step(index, state):
            top, total, mixed = state
            position, rows, slot = tile_rows(index)
            logits = jnp.dot(
                keys_ref[rows, :], flip_ref[half, 0], preferred_element_type=jnp.float32
            )
            key_pos = lax.broadcasted_iota(jnp.int32, (tile, cols), 0)
            live = (key_pos >= doc_start - position) & (key_pos <= query_pos - position)
            logits = jnp.where(live, logits * (scale * math.log2(math.e)), masked_value)
            new_top = jnp.maximum(top, jnp.max(logits, axis=0, keepdims=True))
            terms = jnp.exp2(logits - new_top)
            dweights = jnp.dot(
                values_ref[rows, :], flip_ref[half, 1], preferred_element_type=jnp.float32
            )
            terms_ref[slot, :] = terms
            dweights_ref[slot, :] = dweights
            tops_ref[pl.ds(index, 1), :] = new_top
            decay = jnp.exp2(top - new_top)
            return (
                new_top,
                total * decay + jnp.sum(terms, axis=0, keepdims=True),
                mixed * decay + jnp.sum(terms * dweights, axis=0, keepdims=True),
            )

        zero = jnp.zeros((1, cols), jnp.float32)
        top, total, mixed = lax.fori_loop(
            0, count, sums_step, (jnp.full_like(zero, masked_value), zero, zero)
        )
        inverse = 1.0 / total
        delta = mixed * inverse

        def grads_step(index, carry):
            _, rows, slot = tile_rows(index)
            factor = jnp.exp2(tops_ref[pl.ds(index, 1), :] - top) * inverse
            weights = terms_ref[slot, :] * factor
            dlogits = (weights * (dweights_ref[slot, :] - delta)).astype(jnp.bfloat16)
            dlogits_ref[half, slot, :] = dlogits
            acc_ref[1, rows, :] += jnp.dot(
                weights.astype(jnp.bfloat16),
                stack_ref[half, 1],
                preferred_element_type=jnp.float32,
            )
            acc_ref[0, rows, :] += jnp.dot(
                dlogits, stack_ref[half, 0], preferred_element_type=jnp.float32
            )
            return carry

        lax.fori_loop(0, count, grads_step, 0)

    for piece, row, owner, start in part_moves(
        ctx_count, dp_count, inner, part_rows, ctx_index, dp_index
    ):
        here, ordered = pl.ds(row, part_rows), ordered_rows(owner, start)
        dkv_refs[piece][here, :head_width] = (scale * acc_ref[0, ordered, :]).astype(jnp.bfloat16)
        dkv_refs[piece][here, head_width:] = acc_ref[1, ordered, :].astype(jnp.bfloat16)


def query_kernel(
    ctx_count,
    tile,
    tiles_ref,
    keys_ref,
    dlogits_ref,
    passed_ref,
    dq_ref,
    same_ref,
    sum_ref,
    counts_ref,
    sem,
):
    tok_rows = dq_ref.shape[0]
    head_width = keys_ref.shape[1]
    span_rows = tok_rows // 2
    scale = head_width ** (-0.5)
    count_copy = pltpu.make_async_copy(tiles_ref, counts_ref, sem)
    count_copy.start()
    same_ref[...] = passed_ref[...]
    count_copy.wait()
    for half in range(2):
        end = span_first(half, ctx_count, span_rows) + span_rows
        sum_ref[...] = jnp.zeros_like(sum_ref)

        def query_step(index, carry):
            rows = pl.ds(pl.multiple_of(end - index * tile, span_rows), tile)
            slot = pl.ds(pl.multiple_of(index * tile, tile), tile)
            sum_ref[...] += jnp.dot(
                keys_ref[rows, :].T, dlogits_ref[half, slot, :], preferred_element_type=jnp.float32
            )
            return carry

        lax.fori_loop(0, counts_ref[0, half], query_step, 0)
        grads = (scale * sum_ref[...]).T.astype(jnp.bfloat16)
        for head in range(dq_ref.shape[1] // head_width):
            dq_ref[
                pl.ds(half * span_rows, span_rows), pl.ds(head * head_width, head_width)
            ] = grads[head * span_rows : (head + 1) * span_rows]


def prepare(ctx_count, tile, doc_lengths, queries, out_grads, head_width, line):
    tok_rows, width = queries.shape
    cols = width // head_width * (tok_rows // 2)
    unmoved = [
        pltpu.with_memory_space_constraint(argument, pltpu.HBM)
        for argument in (doc_lengths, queries, out_grads)
    ]
    return pl.pallas_call(
        functools.partial(prepare_kernel, ctx_count, tile),
        out_shape=(
            jax.ShapeDtypeStruct((2, 2, cols, head_width), jnp.bfloat16),
            jax.ShapeDtypeStruct((2, 2, head_width, cols), jnp.bfloat16),
            jax.ShapeDtypeStruct((2, 1, cols), jnp.int32),
            jax.ShapeDtypeStruct((8, 128), jnp.int32),
            jax.ShapeDtypeStruct(line.shape, line.dtype),
        ),
        in_specs=[hbm, hbm, hbm, vmem],
        out_specs=[vmem] * 5,
        scratch_shapes=[
            pltpu.VMEM((2, tok_rows, width), jnp.bfloat16),
            pltpu.SMEM(doc_lengths.shape, jnp.int32),
            pltpu.SemaphoreType.DMA((3,)),
        ],
        compiler_params=pltpu.CompilerParams(vmem_limit_bytes=4 * 1024 * 1024),
    )(*unmoved, line)


def attend(ctx_count, dp_count, inner, tile, moves, tiles, starts, stacked, flipped, pieces, seq):
    cols, head_width = stacked.shape[2:]
    part_count = dp_count * inner
    part = jax.ShapeDtypeStruct((seq // part_count, 2 * head_width), jnp.bfloat16)
    slots = -(-seq // tile)
    results = pl.pallas_call(
        functools.partial(
            attend_kernel, ctx_count, dp_count, inner, tile, moves, len(pieces)
        ),
        out_shape=[
            jax.ShapeDtypeStruct((tile + seq, head_width), jnp.bfloat16),
            jax.ShapeDtypeStruct((2, slots * tile, cols), jnp.bfloat16),
        ]
        + [part] * part_count,
        in_specs=[vmem] * (4 + len(pieces)),
        out_specs=[vmem] * (2 + part_count),
        scratch_shapes=[
            pltpu.VMEM((tile + seq, head_width), jnp.bfloat16),
            pltpu.VMEM((2, tile + seq, head_width), jnp.float32),
            pltpu.VMEM((slots * tile, cols), jnp.float32),
            pltpu.VMEM((slots * tile, cols), jnp.float32),
            pltpu.VMEM((slots, cols), jnp.float32),
            pltpu.SMEM((8, 128), jnp.int32),
            pltpu.SemaphoreType.DMA,
        ],
        compiler_params=pltpu.CompilerParams(vmem_limit_bytes=32 * 1024 * 1024),
    )(tiles, starts, stacked, flipped, *pieces)
    return results[0], results[1], results[2:]


def query_side(ctx_count, tile, tiles, keys_ordered, dlogits, passed, tok_rows):
    cols = dlogits.shape[2]
    head_width = keys_ordered.shape[1]
    return pl.pallas_call(
        functools.partial(query_kernel, ctx_count, tile),
        out_shape=(
            jax.ShapeDtypeStruct(
                (tok_rows, cols // (tok_rows // 2) * head_width), jnp.bfloat16
            ),
            jax.ShapeDtypeStruct(passed.shape, passed.dtype),
        ),
        in_specs=[vmem] * 4,
        out_specs=(vmem, vmem),
        scratch_shapes=[
            pltpu.VMEM((head_width, cols), jnp.float32),
            pltpu.SMEM((8, 128), jnp.int32),
            pltpu.SemaphoreType.DMA,
        ],
        compiler_params=pltpu.CompilerParams(vmem_limit_bytes=8 * 1024 * 1024),
    )(tiles, keys_ordered, dlogits, passed)


def swap(value, axis, offset):
    pairs = [(index, index ^ offset) for index in range(lax.axis_size(axis))]
    return lax.ppermute(value, axis, pairs)


def total_of(terms):
    return sum(term.astype(jnp.float32) for term in terms).astype(jnp.bfloat16)


def swap_axes(value, inner, odd_step, even_step):
    ctx_count = lax.axis_size("ctx")
    pairs = [
        (2 * ctx + dp, 2 * (ctx ^ (odd_step if dp else even_step)) + dp)
        for ctx in range(ctx_count)
        for dp in range(2)
    ]
    return lax.ppermute(value, ("ctx", "dp"), pairs)


def halves(value, part_rows):
    return lax.dynamic_slice_in_dim(value, lax.axis_index("dp") * part_rows, part_rows, 0)


def gather_two_axes(keys, values, inner, part_rows, run_prepare):
    tok_rows, head_width = keys.shape
    lane = lax.broadcasted_iota(jnp.int32, (tok_rows, 2 * head_width), 1)
    zero = jnp.zeros((), keys.dtype)
    own = jnp.where(
        lane < head_width,
        lax.pad(keys, zero, ((0, 0, 0), (0, head_width, 0))),
        lax.pad(values, zero, ((0, 0, 0), (head_width, 0, 0))),
    )
    shards = [swap_axes(own, inner, step * inner, step) for step in range(1, inner)]
    prepared, shards[-1] = run_prepare(shards[-1])
    near = jnp.concatenate(shards, axis=0)
    half_near = jnp.concatenate([halves(shard, part_rows) for shard in shards], axis=0)
    others = [swap_axes(half_near, inner, step, step * inner) for step in range(1, inner)]
    pieces = [own, near, swap(near, "dp", 1)] + others + [swap(piece, "dp", 1) for piece in others]
    return prepared, pieces


def gather_in_stages(keys, values, inner, part_rows, run_prepare):
    outer = lax.axis_size("ctx") // inner
    own = halves(jnp.concatenate([keys, values], axis=1), part_rows)
    line = jnp.concatenate(
        [own] + [swap(own, "ctx", block * inner) for block in range(1, outer)], axis=0
    )
    plane = [line] + [swap(line, "ctx", offset) for offset in range(1, inner)]
    prepared, plane[0] = run_prepare(line)
    pieces = plane + [
        swap(piece, "dp", offset)
        for offset in range(1, lax.axis_size("dp"))
        for piece in plane
    ]
    return prepared, pieces


def body(queries, keys, values, out_grads, doc_lengths):
    ctx_count = lax.axis_size("ctx")
    dp_count = lax.axis_size("dp")
    inner = math.gcd(4, ctx_count)
    outer = ctx_count // inner
    tok_rows, head_width = keys.shape
    part_rows = tok_rows // dp_count
    seq = ctx_count * tok_rows
    tile = math.gcd(256, seq)

    def run_prepare(held):
        *prepared, held = prepare(
            ctx_count, tile, doc_lengths, queries, out_grads, head_width, held
        )
        return prepared, held

    if outer == inner and dp_count == 2:
        gather, moves = gather_two_axes, functools.partial(two_axis_moves, inner, part_rows)
    else:
        gather = gather_in_stages
        moves = functools.partial(part_moves, ctx_count, dp_count, inner, part_rows)
    (stacked, flipped, starts, tiles), pieces = gather(
        keys, values, inner, part_rows, run_prepare
    )
    keys_ordered, dlogits, parts = attend(
        ctx_count, dp_count, inner, tile, moves, tiles, starts, stacked, flipped, pieces, seq
    )
    plane_sums = [
        total_of(
            [parts[offset]]
            + [swap(parts[far * inner + offset], "dp", far) for far in range(1, dp_count)]
        )
        for offset in range(inner)
    ]
    query_grads, plane_sums[0] = query_side(
        ctx_count, tile, tiles, keys_ordered, dlogits, plane_sums[0], tok_rows
    )
    line_sum = total_of(
        [plane_sums[0]] + [swap(plane_sums[offset], "ctx", offset) for offset in range(1, inner)]
    )
    blocks = jnp.split(line_sum, outer, axis=0)
    kv_grads = total_of(
        [blocks[0]] + [swap(blocks[block], "ctx", block * inner) for block in range(1, outer)]
    )
    return (query_grads, kv_grads[:, :head_width], kv_grads[:, head_width:])


def solution(mesh):
    return jax.shard_map(
        body,
        mesh=mesh,
        in_specs=(P("ctx", "dp"), P("ctx", None), P("ctx", None), P("ctx", "dp"), P()),
        out_specs=(P("ctx", "dp"), P(("ctx", "dp"), None), P(("ctx", "dp"), None)),
        check_vma=False,
    )
```

```python
import functools
import math

import jax
import jax.numpy as jnp
from jax import lax
from jax.experimental import pallas as pl
from jax.experimental.pallas import tpu as pltpu
from jax.sharding import PartitionSpec as P

masked_value = -1e30

vmem = pl.BlockSpec(memory_space=pltpu.VMEM)
smem = pl.BlockSpec(memory_space=pltpu.SMEM)
hbm = pl.BlockSpec(memory_space=pltpu.HBM)


def row_position(ctx_index, start, ctx_count, rows, span_rows):
    low = ctx_index * span_rows + start
    high = (2 * ctx_count - 1 - ctx_index) * span_rows + start - span_rows
    return pl.multiple_of(jnp.where(start < span_rows, low, high), rows)


def span_first(half, ctx_count, span_rows):
    ctx_index = lax.axis_index("ctx")
    return (ctx_index if half == 0 else 2 * ctx_count - 1 - ctx_index) * span_rows


def prepare_kernel(
    ctx_count,
    tile,
    lengths_hbm,
    q_hbm,
    g_hbm,
    line_ref,
    stack_ref,
    flip_ref,
    starts_ref,
    tiles_ref,
    zero_ref,
    same_ref,
    raw_ref,
    lengths_ref,
    sems,
):
    tok_rows = q_hbm.shape[0]
    head_width = stack_ref.shape[3]
    cols = stack_ref.shape[2]
    span_rows = tok_rows // 2
    copies = [
        pltpu.make_async_copy(source, raw_ref.at[slot], sems.at[slot])
        for slot, source in enumerate((q_hbm, g_hbm))
    ]
    for copy in copies:
        copy.start()
    lengths_copy = pltpu.make_async_copy(lengths_hbm, lengths_ref, sems.at[2])
    lengths_copy.start()
    same_ref[...] = line_ref[...]
    zero_ref[...] = jnp.zeros_like(zero_ref)
    lane = lax.broadcasted_iota(jnp.int32, tiles_ref.shape, 1)
    tiles = jnp.zeros(tiles_ref.shape, jnp.int32)
    lengths_copy.wait()
    for half in range(2):
        first = span_first(half, ctx_count, span_rows)
        query_pos = first + lax.rem(
            lax.broadcasted_iota(jnp.int32, (1, cols), 1), jnp.int32(span_rows)
        )
        doc_start = jnp.zeros((1, cols), jnp.int32)
        first_key = jnp.int32(0)
        end = jnp.int32(0)
        for doc in range(lengths_ref.shape[0]):
            end = end + lengths_ref[doc]
            doc_start = jnp.where(query_pos >= end, end, doc_start)
            first_key = jnp.where(first >= end, end, first_key)
        starts_ref[half] = doc_start
        count = (first + span_rows - first_key + tile - 1) // tile
        tiles = jnp.where(lane == half, count, tiles)
    tiles_ref[...] = tiles
    for slot, copy in enumerate(copies):
        copy.wait()
        for half in range(2):
            for head in range(q_hbm.shape[1] // head_width):
                stack_ref[half, slot, pl.ds(head * span_rows, span_rows), :] = raw_ref[
                    slot,
                    pl.ds(half * span_rows, span_rows),
                    pl.ds(head * head_width, head_width),
                ]
            flip_ref[half, slot] = stack_ref[half, slot].T


def attend_kernel(
    ctx_count, dp_count, inner, tile, tiles_ref, starts_ref, stack_ref, flip_ref, _, *refs
):
    outer = ctx_count // inner
    piece_count = dp_count * inner
    kv_refs = refs[:piece_count]
    refs = refs[piece_count:]
    keys_ref, dlogits_ref, acc_ref = refs[:3]
    dkv_refs = refs[3 : piece_count + 3]
    values_ref, terms_ref, dweights_ref, tops_ref, counts_ref, sem = refs[piece_count + 3 :]
    cols, head_width = stack_ref.shape[2:]
    tok_rows = (keys_ref.shape[0] - tile) // ctx_count
    part_rows = tok_rows // dp_count
    span_rows = tok_rows // 2
    scale = head_width ** (-0.5)
    ctx_index = lax.axis_index("ctx")
    dp_index = lax.axis_index("dp")
    count_copy = pltpu.make_async_copy(tiles_ref, counts_ref, sem)
    count_copy.start()

    def blocks():
        for piece in range(piece_count):
            for block in range(outer):
                owner = ctx_index ^ (piece % inner) ^ (block * inner)
                first = (dp_index ^ (piece // inner)) * part_rows
                position = row_position(owner, first, ctx_count, part_rows, span_rows)
                row = 2 * block * part_rows
                yield (
                    piece,
                    pl.ds(row, part_rows),
                    pl.ds(row + part_rows, part_rows),
                    pl.ds(tile + position, part_rows),
                )

    dead = jnp.zeros((tile, head_width), jnp.bfloat16)
    keys_ref[:tile, :] = dead
    values_ref[:tile, :] = dead
    for piece, key_rows, value_rows, ordered in blocks():
        keys_ref[ordered, :] = kv_refs[piece][key_rows, :]
        values_ref[ordered, :] = kv_refs[piece][value_rows, :]
    count_copy.wait()
    group = min(256, cols)
    groups = [slice(start, start + group) for start in range(0, cols, group)]

    for half in range(2):
        first = span_first(half, ctx_count, span_rows)
        query_pos = first + lax.rem(
            lax.broadcasted_iota(jnp.int32, (1, group), 1), jnp.int32(span_rows)
        )
        doc_start = starts_ref[half]
        count = counts_ref[0, half]

        def tile_rows(index):
            position = first + span_rows - (index + 1) * tile
            rows = pl.ds(pl.multiple_of(tile + position, span_rows), tile)
            return position, rows, pl.ds(pl.multiple_of(index * tile, tile), tile)

        def sums_step(index, state):
            position, rows, slot = tile_rows(index)
            key_block, value_block = keys_ref[rows, :], values_ref[rows, :]
            all_logits = [
                jnp.dot(key_block, flip_ref[half, 0, :, lanes], preferred_element_type=jnp.float32)
                for lanes in groups
            ]
            all_dweights = [
                jnp.dot(
                    value_block, flip_ref[half, 1, :, lanes], preferred_element_type=jnp.float32
                )
                for lanes in groups
            ]
            following = []
            for lanes, logits, dweights, (top, total, mixed) in zip(
                groups, all_logits, all_dweights, state
            ):
                key_pos = lax.broadcasted_iota(jnp.int32, logits.shape, 0)
                live = (key_pos >= doc_start[:, lanes] - position) & (
                    key_pos <= query_pos - position
                )
                logits = jnp.where(live, logits * (scale * math.log2(math.e)), masked_value)
                new_top = jnp.maximum(top, jnp.max(logits, axis=0, keepdims=True))
                terms = jnp.exp2(logits - new_top)
                terms_ref[slot, lanes] = terms
                dweights_ref[slot, lanes] = dweights
                tops_ref[pl.ds(index, 1), lanes] = new_top
                decay = jnp.exp2(top - new_top)
                following.append(
                    (
                        new_top,
                        total * decay + jnp.sum(terms, axis=0, keepdims=True),
                        mixed * decay + jnp.sum(terms * dweights, axis=0, keepdims=True),
                    )
                )
            return tuple(following)

        zero = jnp.zeros((1, group), jnp.float32)
        empty = (jnp.full_like(zero, masked_value), zero, zero)
        sums = lax.fori_loop(0, count, sums_step, (empty,) * len(groups))
        top, total, mixed = (jnp.concatenate(part, axis=1) for part in zip(*sums))
        inverse = 1.0 / total
        delta = mixed * inverse

        def grads_step(index, carry):
            _, rows, slot = tile_rows(index)
            factor = jnp.exp2(tops_ref[pl.ds(index, 1), :] - top) * inverse
            weights = terms_ref[slot, :] * factor
            dlogits = (weights * (dweights_ref[slot, :] - delta)).astype(jnp.bfloat16)
            for lane_block in range(cols // head_width):
                dlogits_ref[half, lane_block, slot, :] = dlogits[
                    :, lane_block * head_width : (lane_block + 1) * head_width
                ]
            acc_ref[1, rows, :] += jnp.dot(
                weights.astype(jnp.bfloat16),
                stack_ref[half, 1],
                preferred_element_type=jnp.float32,
            )
            acc_ref[0, rows, :] += jnp.dot(
                dlogits, stack_ref[half, 0], preferred_element_type=jnp.float32
            )
            return carry

        lax.fori_loop(0, count, grads_step, 0)

    for piece, key_rows, value_rows, ordered in blocks():
        dkv_refs[piece][key_rows, :] = (scale * acc_ref[0, ordered, :]).astype(jnp.bfloat16)
        dkv_refs[piece][value_rows, :] = acc_ref[1, ordered, :].astype(jnp.bfloat16)


def query_kernel(
    ctx_count,
    tile,
    tiles_ref,
    keys_ref,
    dlogits_ref,
    passed_ref,
    dq_ref,
    same_ref,
    sum_ref,
    counts_ref,
    sem,
):
    tok_rows = dq_ref.shape[0]
    head_width = keys_ref.shape[1]
    span_rows = tok_rows // 2
    scale = head_width ** (-0.5)
    count_copy = pltpu.make_async_copy(tiles_ref, counts_ref, sem)
    count_copy.start()
    same_ref[...] = passed_ref[...]
    count_copy.wait()
    for half in range(2):
        end = span_first(half, ctx_count, span_rows) + span_rows
        sum_ref[...] = jnp.zeros_like(sum_ref)

        def query_step(index, carry):
            rows = pl.ds(pl.multiple_of(end - index * tile, span_rows), tile)
            slot = pl.ds(pl.multiple_of(index * tile, tile), tile)
            dlogits = jnp.concatenate(
                [dlogits_ref[half, block, slot, :] for block in range(dlogits_ref.shape[1])], axis=1
            )
            sum_ref[...] += jnp.dot(
                keys_ref[rows, :].T, dlogits, preferred_element_type=jnp.float32
            )
            return carry

        lax.fori_loop(0, counts_ref[0, half], query_step, 0)
        grads = (scale * sum_ref[...]).T.astype(jnp.bfloat16)
        for head in range(dq_ref.shape[1] // head_width):
            dq_ref[
                pl.ds(half * span_rows, span_rows), pl.ds(head * head_width, head_width)
            ] = grads[head * span_rows : (head + 1) * span_rows]


def prepare(ctx_count, tile, doc_lengths, queries, out_grads, head_width, line):
    tok_rows, width = queries.shape
    cols = width // head_width * (tok_rows // 2)
    unmoved = [
        pltpu.with_memory_space_constraint(argument, pltpu.HBM)
        for argument in (doc_lengths, queries, out_grads)
    ]
    return pl.pallas_call(
        functools.partial(prepare_kernel, ctx_count, tile),
        out_shape=(
            jax.ShapeDtypeStruct((2, 2, cols, head_width), jnp.bfloat16),
            jax.ShapeDtypeStruct((2, 2, head_width, cols), jnp.bfloat16),
            jax.ShapeDtypeStruct((2, 1, cols), jnp.int32),
            jax.ShapeDtypeStruct((8, 128), jnp.int32),
            jax.ShapeDtypeStruct((2, tile + ctx_count * tok_rows, head_width), jnp.float32),
            jax.ShapeDtypeStruct(line.shape, line.dtype),
        ),
        in_specs=[hbm, hbm, hbm, vmem],
        out_specs=[vmem] * 6,
        scratch_shapes=[
            pltpu.VMEM((2, tok_rows, width), jnp.bfloat16),
            pltpu.SMEM(doc_lengths.shape, jnp.int32),
            pltpu.SemaphoreType.DMA((3,)),
        ],
        compiler_params=pltpu.CompilerParams(vmem_limit_bytes=4 * 1024 * 1024),
    )(*unmoved, line)


def attend(ctx_count, dp_count, inner, tile, tiles, starts, stacked, flipped, zeros, pieces):
    cols, head_width = stacked.shape[2:]
    seq = dp_count * inner * pieces[0].shape[0] // 2
    slots = -(-seq // tile)
    results = pl.pallas_call(
        functools.partial(attend_kernel, ctx_count, dp_count, inner, tile),
        out_shape=[
            jax.ShapeDtypeStruct((tile + seq, head_width), jnp.bfloat16),
            jax.ShapeDtypeStruct(
                (2, cols // head_width, slots * tile, head_width), jnp.bfloat16
            ),
            jax.ShapeDtypeStruct(zeros.shape, zeros.dtype),
        ]
        + [jax.ShapeDtypeStruct(piece.shape, jnp.bfloat16) for piece in pieces],
        in_specs=[vmem] * (5 + len(pieces)),
        out_specs=[vmem] * (3 + len(pieces)),
        scratch_shapes=[
            pltpu.VMEM((tile + seq, head_width), jnp.bfloat16),
            pltpu.VMEM((slots * tile, cols), jnp.float32),
            pltpu.VMEM((slots * tile, cols), jnp.float32),
            pltpu.VMEM((slots, cols), jnp.float32),
            pltpu.SMEM((8, 128), jnp.int32),
            pltpu.SemaphoreType.DMA,
        ],
        input_output_aliases={4: 2},
        compiler_params=pltpu.CompilerParams(vmem_limit_bytes=32 * 1024 * 1024),
    )(tiles, starts, stacked, flipped, zeros, *pieces)
    return results[0], results[1], results[3:]


def query_side(ctx_count, tile, tiles, keys_ordered, dlogits, passed, tok_rows):
    head_width = keys_ordered.shape[1]
    cols = dlogits.shape[1] * head_width
    return pl.pallas_call(
        functools.partial(query_kernel, ctx_count, tile),
        out_shape=(
            jax.ShapeDtypeStruct(
                (tok_rows, cols // (tok_rows // 2) * head_width), jnp.bfloat16
            ),
            jax.ShapeDtypeStruct(passed.shape, passed.dtype),
        ),
        in_specs=[vmem] * 4,
        out_specs=(vmem, vmem),
        scratch_shapes=[
            pltpu.VMEM((head_width, cols), jnp.float32),
            pltpu.SMEM((8, 128), jnp.int32),
            pltpu.SemaphoreType.DMA,
        ],
        compiler_params=pltpu.CompilerParams(vmem_limit_bytes=8 * 1024 * 1024),
    )(tiles, keys_ordered, dlogits, passed)


def swap(value, axis, offset):
    pairs = [(index, index ^ offset) for index in range(lax.axis_size(axis))]
    return lax.ppermute(value, axis, pairs)


def total_of(terms):
    return sum(term.astype(jnp.float32) for term in terms).astype(jnp.bfloat16)


def body(queries, keys, values, out_grads, doc_lengths):
    ctx_count = lax.axis_size("ctx")
    dp_count = lax.axis_size("dp")
    inner = math.gcd(4, ctx_count)
    outer = ctx_count // inner
    tok_rows, head_width = keys.shape
    part_rows = tok_rows // dp_count
    tile = math.gcd(256, ctx_count * tok_rows)
    start = lax.axis_index("dp") * part_rows
    own_keys = lax.dynamic_slice_in_dim(keys, start, part_rows, 0)
    own_values = lax.dynamic_slice_in_dim(values, start, part_rows, 0)
    zero = jnp.zeros((), keys.dtype)
    own = jnp.where(
        lax.broadcasted_iota(jnp.int32, (2 * part_rows, head_width), 0) < part_rows,
        lax.pad(own_keys, zero, ((0, part_rows, 0), (0, 0, 0))),
        lax.pad(own_values, zero, ((part_rows, 0, 0), (0, 0, 0))),
    )
    line = jnp.concatenate(
        [own] + [swap(own, "ctx", block * inner) for block in range(1, outer)], axis=0
    )
    plane = [line] + [swap(line, "ctx", offset) for offset in range(1, inner)]
    stacked, flipped, starts, tiles, zeros, plane[0] = prepare(
        ctx_count, tile, doc_lengths, queries, out_grads, head_width, line
    )
    pieces = plane + [
        swap(piece, "dp", offset) for offset in range(1, dp_count) for piece in plane
    ]
    keys_ordered, dlogits, parts = attend(
        ctx_count, dp_count, inner, tile, tiles, starts, stacked, flipped, zeros, pieces
    )
    plane_sums = [
        total_of(
            [parts[offset]]
            + [swap(parts[far * inner + offset], "dp", far) for far in range(1, dp_count)]
        )
        for offset in range(inner)
    ]
    query_grads, plane_sums[0] = query_side(
        ctx_count, tile, tiles, keys_ordered, dlogits, plane_sums[0], tok_rows
    )
    line_sum = total_of(
        [plane_sums[0]] + [swap(plane_sums[offset], "ctx", offset) for offset in range(1, inner)]
    )
    blocks = jnp.split(line_sum, outer, axis=0)
    kv_grads = total_of(
        [blocks[0]] + [swap(blocks[block], "ctx", block * inner) for block in range(1, outer)]
    )
    return (query_grads, kv_grads[:part_rows], kv_grads[part_rows:])


def solution(mesh):
    return jax.shard_map(
        body,
        mesh=mesh,
        in_specs=(P("ctx", "dp"), P("ctx", None), P("ctx", None), P("ctx", "dp"), P()),
        out_specs=(P("ctx", "dp"), P(("ctx", "dp"), None), P(("ctx", "dp"), None)),
        check_vma=False,
    )
```

```python
import functools
import math

import jax
import jax.numpy as jnp
from jax import lax
from jax.experimental import pallas as pl
from jax.experimental.pallas import tpu as pltpu
from jax.sharding import PartitionSpec as P

masked_value = -1e30

vmem = pl.BlockSpec(memory_space=pltpu.VMEM)
smem = pl.BlockSpec(memory_space=pltpu.SMEM)
hbm = pl.BlockSpec(memory_space=pltpu.HBM)


def row_position(ctx_index, start, ctx_count, rows, span_rows):
    low = ctx_index * span_rows + start
    high = (2 * ctx_count - 1 - ctx_index) * span_rows + start - span_rows
    return pl.multiple_of(jnp.where(start < span_rows, low, high), rows)


def span_first(half, ctx_count, span_rows):
    ctx_index = lax.axis_index("ctx")
    return (ctx_index if half == 0 else 2 * ctx_count - 1 - ctx_index) * span_rows


def prepare_kernel(
    ctx_count,
    tile,
    lengths_hbm,
    q_hbm,
    g_hbm,
    line_ref,
    stack_ref,
    flip_ref,
    starts_ref,
    tiles_ref,
    zero_ref,
    same_ref,
    raw_ref,
    lengths_ref,
    sems,
):
    tok_rows = q_hbm.shape[0]
    head_width = stack_ref.shape[3]
    cols = stack_ref.shape[2]
    span_rows = tok_rows // 2
    copies = [
        pltpu.make_async_copy(source, raw_ref.at[slot], sems.at[slot])
        for slot, source in enumerate((q_hbm, g_hbm))
    ]
    for copy in copies:
        copy.start()
    lengths_copy = pltpu.make_async_copy(lengths_hbm, lengths_ref, sems.at[2])
    lengths_copy.start()
    same_ref[...] = line_ref[...]
    zero_ref[...] = jnp.zeros_like(zero_ref)
    lane = lax.broadcasted_iota(jnp.int32, tiles_ref.shape, 1)
    tiles = jnp.zeros(tiles_ref.shape, jnp.int32)
    lengths_copy.wait()
    for half in range(2):
        first = span_first(half, ctx_count, span_rows)
        query_pos = first + lax.rem(
            lax.broadcasted_iota(jnp.int32, (1, cols), 1), jnp.int32(span_rows)
        )
        doc_start = jnp.zeros((1, cols), jnp.int32)
        first_key = jnp.int32(0)
        end = jnp.int32(0)
        for doc in range(lengths_ref.shape[0]):
            end = end + lengths_ref[doc]
            doc_start = jnp.where(query_pos >= end, end, doc_start)
            first_key = jnp.where(first >= end, end, first_key)
        starts_ref[half] = doc_start
        count = (first + span_rows - first_key + tile - 1) // tile
        tiles = jnp.where(lane == half, count, tiles)
    tiles_ref[...] = tiles
    for slot, copy in enumerate(copies):
        copy.wait()
        for half in range(2):
            for head in range(q_hbm.shape[1] // head_width):
                stack_ref[half, slot, pl.ds(head * span_rows, span_rows), :] = raw_ref[
                    slot,
                    pl.ds(half * span_rows, span_rows),
                    pl.ds(head * head_width, head_width),
                ]
            flip_ref[half, slot] = stack_ref[half, slot].T


def line_steps(outer):
    return (0, 1, 3, 2) if outer == 4 else tuple(range(outer))


def send_order(outer):
    return (3, 1, 2) if outer == 4 else tuple(reversed(range(1, outer)))


def attend_kernel(
    ctx_count, dp_count, inner, tile, tiles_ref, starts_ref, stack_ref, flip_ref, _, *refs
):
    outer = ctx_count // inner
    piece_count = dp_count * inner
    kv_refs = refs[:piece_count]
    refs = refs[piece_count:]
    keys_ref, dlogits_ref, acc_ref = refs[:3]
    dkv_refs = refs[3 : piece_count + 3]
    values_ref, terms_ref, dweights_ref, tops_ref, counts_ref, sem = refs[piece_count + 3 :]
    cols, head_width = stack_ref.shape[2:]
    tok_rows = (keys_ref.shape[0] - tile) // ctx_count
    part_rows = tok_rows // dp_count
    span_rows = tok_rows // 2
    scale = head_width ** (-0.5)
    ctx_index = lax.axis_index("ctx")
    dp_index = lax.axis_index("dp")
    count_copy = pltpu.make_async_copy(tiles_ref, counts_ref, sem)
    count_copy.start()

    def blocks(steps):
        for piece in range(piece_count):
            for block, step in enumerate(steps):
                owner = ctx_index ^ (piece % inner) ^ (step * inner)
                first = (dp_index ^ (piece // inner)) * part_rows
                position = row_position(owner, first, ctx_count, part_rows, span_rows)
                row = 2 * block * part_rows
                yield (
                    piece,
                    pl.ds(row, part_rows),
                    pl.ds(row + part_rows, part_rows),
                    pl.ds(tile + position, part_rows),
                )

    dead = jnp.zeros((tile, head_width), jnp.bfloat16)
    keys_ref[:tile, :] = dead
    values_ref[:tile, :] = dead
    for piece, key_rows, value_rows, ordered in blocks(line_steps(outer)):
        keys_ref[ordered, :] = kv_refs[piece][key_rows, :]
        values_ref[ordered, :] = kv_refs[piece][value_rows, :]
    count_copy.wait()
    group = min(256, cols)
    groups = [slice(start, start + group) for start in range(0, cols, group)]

    for half in range(2):
        first = span_first(half, ctx_count, span_rows)
        query_pos = first + lax.rem(
            lax.broadcasted_iota(jnp.int32, (1, group), 1), jnp.int32(span_rows)
        )
        doc_start = starts_ref[half]
        count = counts_ref[0, half]

        def tile_rows(index):
            position = first + span_rows - (index + 1) * tile
            rows = pl.ds(pl.multiple_of(tile + position, span_rows), tile)
            return position, rows, pl.ds(pl.multiple_of(index * tile, tile), tile)

        def sums_step(index, state):
            position, rows, slot = tile_rows(index)
            key_block, value_block = keys_ref[rows, :], values_ref[rows, :]
            all_logits = [
                jnp.dot(key_block, flip_ref[half, 0, :, lanes], preferred_element_type=jnp.float32)
                for lanes in groups
            ]
            all_dweights = [
                jnp.dot(
                    value_block, flip_ref[half, 1, :, lanes], preferred_element_type=jnp.float32
                )
                for lanes in groups
            ]
            following = []
            for lanes, logits, dweights, (top, total, mixed) in zip(
                groups, all_logits, all_dweights, state
            ):
                key_pos = lax.broadcasted_iota(jnp.int32, logits.shape, 0)
                live = (key_pos >= doc_start[:, lanes] - position) & (
                    key_pos <= query_pos - position
                )
                logits = jnp.where(live, logits * (scale * math.log2(math.e)), masked_value)
                new_top = jnp.maximum(top, jnp.max(logits, axis=0, keepdims=True))
                terms = jnp.exp2(logits - new_top)
                terms_ref[slot, lanes] = terms
                dweights_ref[slot, lanes] = dweights
                tops_ref[pl.ds(index, 1), lanes] = new_top
                decay = jnp.exp2(top - new_top)
                following.append(
                    (
                        new_top,
                        total * decay + jnp.sum(terms, axis=0, keepdims=True),
                        mixed * decay + jnp.sum(terms * dweights, axis=0, keepdims=True),
                    )
                )
            return tuple(following)

        zero = jnp.zeros((1, group), jnp.float32)
        empty = (jnp.full_like(zero, masked_value), zero, zero)
        sums = lax.fori_loop(0, count, sums_step, (empty,) * len(groups))
        top, total, mixed = (jnp.concatenate(part, axis=1) for part in zip(*sums))
        inverse = 1.0 / total
        delta = mixed * inverse

        def grads_step(index, carry):
            _, rows, slot = tile_rows(index)
            factor = jnp.exp2(tops_ref[pl.ds(index, 1), :] - top) * inverse
            weights = terms_ref[slot, :] * factor
            dlogits = (weights * (dweights_ref[slot, :] - delta)).astype(jnp.bfloat16)
            for lane_block in range(cols // head_width):
                dlogits_ref[half, lane_block, slot, :] = dlogits[
                    :, lane_block * head_width : (lane_block + 1) * head_width
                ]
            acc_ref[1, rows, :] += jnp.dot(
                weights.astype(jnp.bfloat16),
                stack_ref[half, 1],
                preferred_element_type=jnp.float32,
            )
            acc_ref[0, rows, :] += jnp.dot(
                dlogits, stack_ref[half, 0], preferred_element_type=jnp.float32
            )
            return carry

        lax.fori_loop(0, count, grads_step, 0)

    for piece, key_rows, value_rows, ordered in blocks(range(outer)):
        dkv_refs[piece][key_rows, :] = (scale * acc_ref[0, ordered, :]).astype(jnp.bfloat16)
        dkv_refs[piece][value_rows, :] = acc_ref[1, ordered, :].astype(jnp.bfloat16)


def query_kernel(
    ctx_count,
    tile,
    tiles_ref,
    keys_ref,
    dlogits_ref,
    passed_ref,
    dq_ref,
    same_ref,
    sum_ref,
    counts_ref,
    sem,
):
    tok_rows = dq_ref.shape[0]
    head_width = keys_ref.shape[1]
    span_rows = tok_rows // 2
    scale = head_width ** (-0.5)
    count_copy = pltpu.make_async_copy(tiles_ref, counts_ref, sem)
    count_copy.start()
    same_ref[...] = passed_ref[...]
    count_copy.wait()
    for half in range(2):
        end = span_first(half, ctx_count, span_rows) + span_rows
        sum_ref[...] = jnp.zeros_like(sum_ref)

        def query_step(index, carry):
            rows = pl.ds(pl.multiple_of(end - index * tile, span_rows), tile)
            slot = pl.ds(pl.multiple_of(index * tile, tile), tile)
            dlogits = jnp.concatenate(
                [dlogits_ref[half, block, slot, :] for block in range(dlogits_ref.shape[1])], axis=1
            )
            sum_ref[...] += jnp.dot(
                keys_ref[rows, :].T, dlogits, preferred_element_type=jnp.float32
            )
            return carry

        lax.fori_loop(0, counts_ref[0, half], query_step, 0)
        grads = (scale * sum_ref[...]).T.astype(jnp.bfloat16)
        for head in range(dq_ref.shape[1] // head_width):
            dq_ref[
                pl.ds(half * span_rows, span_rows), pl.ds(head * head_width, head_width)
            ] = grads[head * span_rows : (head + 1) * span_rows]


def prepare(ctx_count, tile, doc_lengths, queries, out_grads, head_width, line):
    tok_rows, width = queries.shape
    cols = width // head_width * (tok_rows // 2)
    unmoved = [
        pltpu.with_memory_space_constraint(argument, pltpu.HBM)
        for argument in (doc_lengths, queries, out_grads)
    ]
    return pl.pallas_call(
        functools.partial(prepare_kernel, ctx_count, tile),
        out_shape=(
            jax.ShapeDtypeStruct((2, 2, cols, head_width), jnp.bfloat16),
            jax.ShapeDtypeStruct((2, 2, head_width, cols), jnp.bfloat16),
            jax.ShapeDtypeStruct((2, 1, cols), jnp.int32),
            jax.ShapeDtypeStruct((8, 128), jnp.int32),
            jax.ShapeDtypeStruct((2, tile + ctx_count * tok_rows, head_width), jnp.float32),
            jax.ShapeDtypeStruct(line.shape, line.dtype),
        ),
        in_specs=[hbm, hbm, hbm, vmem],
        out_specs=[vmem] * 6,
        scratch_shapes=[
            pltpu.VMEM((2, tok_rows, width), jnp.bfloat16),
            pltpu.SMEM(doc_lengths.shape, jnp.int32),
            pltpu.SemaphoreType.DMA((3,)),
        ],
        compiler_params=pltpu.CompilerParams(vmem_limit_bytes=4 * 1024 * 1024),
    )(*unmoved, line)


def attend(ctx_count, dp_count, inner, tile, tiles, starts, stacked, flipped, zeros, pieces):
    cols, head_width = stacked.shape[2:]
    seq = dp_count * inner * pieces[0].shape[0] // 2
    slots = -(-seq // tile)
    results = pl.pallas_call(
        functools.partial(attend_kernel, ctx_count, dp_count, inner, tile),
        out_shape=[
            jax.ShapeDtypeStruct((tile + seq, head_width), jnp.bfloat16),
            jax.ShapeDtypeStruct(
                (2, cols // head_width, slots * tile, head_width), jnp.bfloat16
            ),
            jax.ShapeDtypeStruct(zeros.shape, zeros.dtype),
        ]
        + [jax.ShapeDtypeStruct(piece.shape, jnp.bfloat16) for piece in pieces],
        in_specs=[vmem] * (5 + len(pieces)),
        out_specs=[vmem] * (3 + len(pieces)),
        scratch_shapes=[
            pltpu.VMEM((tile + seq, head_width), jnp.bfloat16),
            pltpu.VMEM((slots * tile, cols), jnp.float32),
            pltpu.VMEM((slots * tile, cols), jnp.float32),
            pltpu.VMEM((slots, cols), jnp.float32),
            pltpu.SMEM((8, 128), jnp.int32),
            pltpu.SemaphoreType.DMA,
        ],
        input_output_aliases={4: 2},
        compiler_params=pltpu.CompilerParams(vmem_limit_bytes=32 * 1024 * 1024),
    )(tiles, starts, stacked, flipped, zeros, *pieces)
    return results[0], results[1], results[3:]


def query_side(ctx_count, tile, tiles, keys_ordered, dlogits, passed, tok_rows):
    head_width = keys_ordered.shape[1]
    cols = dlogits.shape[1] * head_width
    return pl.pallas_call(
        functools.partial(query_kernel, ctx_count, tile),
        out_shape=(
            jax.ShapeDtypeStruct(
                (tok_rows, cols // (tok_rows // 2) * head_width), jnp.bfloat16
            ),
            jax.ShapeDtypeStruct(passed.shape, passed.dtype),
        ),
        in_specs=[vmem] * 4,
        out_specs=(vmem, vmem),
        scratch_shapes=[
            pltpu.VMEM((head_width, cols), jnp.float32),
            pltpu.SMEM((8, 128), jnp.int32),
            pltpu.SemaphoreType.DMA,
        ],
        compiler_params=pltpu.CompilerParams(vmem_limit_bytes=8 * 1024 * 1024),
    )(tiles, keys_ordered, dlogits, passed)


def swap(value, axis, offset):
    pairs = [(index, index ^ offset) for index in range(lax.axis_size(axis))]
    return lax.ppermute(value, axis, pairs)


def total_of(terms):
    return sum(term.astype(jnp.float32) for term in terms).astype(jnp.bfloat16)


def body(queries, keys, values, out_grads, doc_lengths):
    ctx_count = lax.axis_size("ctx")
    dp_count = lax.axis_size("dp")
    inner = math.gcd(4, ctx_count)
    outer = ctx_count // inner
    tok_rows, head_width = keys.shape
    part_rows = tok_rows // dp_count
    tile = math.gcd(256, ctx_count * tok_rows)
    start = lax.axis_index("dp") * part_rows
    own_keys = lax.dynamic_slice_in_dim(keys, start, part_rows, 0)
    own_values = lax.dynamic_slice_in_dim(values, start, part_rows, 0)
    zero = jnp.zeros((), keys.dtype)
    own = jnp.where(
        lax.broadcasted_iota(jnp.int32, (2 * part_rows, head_width), 0) < part_rows,
        lax.pad(own_keys, zero, ((0, part_rows, 0), (0, 0, 0))),
        lax.pad(own_values, zero, ((part_rows, 0, 0), (0, 0, 0))),
    )
    line = jnp.concatenate(
        [own] + [swap(own, "ctx", step * inner) for step in line_steps(outer)[1:]], axis=0
    )
    plane = [line] + [swap(line, "ctx", offset) for offset in range(1, inner)]
    stacked, flipped, starts, tiles, zeros, plane[0] = prepare(
        ctx_count, tile, doc_lengths, queries, out_grads, head_width, line
    )
    pieces = plane + [
        swap(piece, "dp", offset) for offset in range(1, dp_count) for piece in plane
    ]
    keys_ordered, dlogits, parts = attend(
        ctx_count, dp_count, inner, tile, tiles, starts, stacked, flipped, zeros, pieces
    )
    plane_sums = [
        total_of(
            [parts[offset]]
            + [swap(parts[far * inner + offset], "dp", far) for far in range(1, dp_count)]
        )
        for offset in range(inner)
    ]
    query_grads, plane_sums[0] = query_side(
        ctx_count, tile, tiles, keys_ordered, dlogits, plane_sums[0], tok_rows
    )
    line_sum = total_of(
        [plane_sums[0]] + [swap(plane_sums[offset], "ctx", offset) for offset in reversed(range(1, inner))]
    )
    blocks = jnp.split(line_sum, outer, axis=0)
    kv_grads = total_of(
        [blocks[0]] + [swap(blocks[block], "ctx", block * inner) for block in send_order(outer)]
    )
    return (query_grads, kv_grads[:part_rows], kv_grads[part_rows:])


def solution(mesh):
    return jax.shard_map(
        body,
        mesh=mesh,
        in_specs=(P("ctx", "dp"), P("ctx", None), P("ctx", None), P("ctx", "dp"), P()),
        out_specs=(P("ctx", "dp"), P(("ctx", "dp"), None), P(("ctx", "dp"), None)),
        check_vma=False,
    )
```

```python
import functools
import math

import jax
import jax.numpy as jnp
from jax import lax
from jax.experimental import pallas as pl
from jax.experimental.pallas import tpu as pltpu
from jax.sharding import PartitionSpec as P

masked_value = -1e30

vmem = pl.BlockSpec(memory_space=pltpu.VMEM)
smem = pl.BlockSpec(memory_space=pltpu.SMEM)
hbm = pl.BlockSpec(memory_space=pltpu.HBM)


def row_position(ctx_index, start, ctx_count, rows, span_rows):
    low = ctx_index * span_rows + start
    high = (2 * ctx_count - 1 - ctx_index) * span_rows + start - span_rows
    return pl.multiple_of(jnp.where(start < span_rows, low, high), rows)


def span_first(half, ctx_count, span_rows):
    ctx_index = lax.axis_index("ctx")
    return (ctx_index if half == 0 else 2 * ctx_count - 1 - ctx_index) * span_rows


def prepare_kernel(
    ctx_count,
    tile,
    lengths_hbm,
    q_hbm,
    g_hbm,
    line_ref,
    stack_ref,
    flip_ref,
    starts_ref,
    tiles_ref,
    zero_ref,
    same_ref,
    raw_ref,
    lengths_ref,
    sems,
):
    tok_rows = q_hbm.shape[0]
    head_width = stack_ref.shape[3]
    cols = stack_ref.shape[2]
    span_rows = tok_rows // 2
    copies = [
        pltpu.make_async_copy(source, raw_ref.at[slot], sems.at[slot])
        for slot, source in enumerate((q_hbm, g_hbm))
    ]
    for copy in copies:
        copy.start()
    lengths_copy = pltpu.make_async_copy(lengths_hbm, lengths_ref, sems.at[2])
    lengths_copy.start()
    same_ref[...] = line_ref[...]
    zero_ref[...] = jnp.zeros_like(zero_ref)
    lane = lax.broadcasted_iota(jnp.int32, tiles_ref.shape, 1)
    tiles = jnp.zeros(tiles_ref.shape, jnp.int32)
    lengths_copy.wait()
    for half in range(2):
        first = span_first(half, ctx_count, span_rows)
        query_pos = first + lax.rem(
            lax.broadcasted_iota(jnp.int32, (1, cols), 1), jnp.int32(span_rows)
        )
        doc_start = jnp.zeros((1, cols), jnp.int32)
        first_key = jnp.int32(0)
        end = jnp.int32(0)
        for doc in range(lengths_ref.shape[0]):
            end = end + lengths_ref[doc]
            doc_start = jnp.where(query_pos >= end, end, doc_start)
            first_key = jnp.where(first >= end, end, first_key)
        starts_ref[half] = doc_start
        count = (first + span_rows - first_key + tile - 1) // tile
        tiles = jnp.where(lane == half, count, tiles)
    tiles_ref[...] = tiles
    for slot, copy in enumerate(copies):
        copy.wait()
        for half in range(2):
            for head in range(q_hbm.shape[1] // head_width):
                stack_ref[half, slot, pl.ds(head * span_rows, span_rows), :] = raw_ref[
                    slot,
                    pl.ds(half * span_rows, span_rows),
                    pl.ds(head * head_width, head_width),
                ]
            flip_ref[half, slot] = stack_ref[half, slot].T


def line_steps(outer):
    return (0, 1, 3, 2) if outer == 4 else tuple(range(outer))


def send_order(outer):
    return (3, 1, 2) if outer == 4 else tuple(reversed(range(1, outer)))


def attend_kernel(
    ctx_count, dp_count, inner, tile, tiles_ref, starts_ref, stack_ref, flip_ref, _, *refs
):
    outer = ctx_count // inner
    piece_count = dp_count * inner
    kv_refs = refs[:piece_count]
    refs = refs[piece_count:]
    keys_ref, dlogits_ref, acc_ref = refs[:3]
    dkv_refs = refs[3 : piece_count + 3]
    values_ref, terms_ref, dweights_ref, tops_ref, counts_ref, sem = refs[piece_count + 3 :]
    cols, head_width = stack_ref.shape[2:]
    tok_rows = (keys_ref.shape[0] - tile) // ctx_count
    part_rows = tok_rows // dp_count
    span_rows = tok_rows // 2
    scale = head_width ** (-0.5)
    ctx_index = lax.axis_index("ctx")
    dp_index = lax.axis_index("dp")
    count_copy = pltpu.make_async_copy(tiles_ref, counts_ref, sem)
    count_copy.start()

    def blocks(steps):
        for piece in range(piece_count):
            for block, step in enumerate(steps):
                owner = ctx_index ^ (piece % inner) ^ (step * inner)
                first = (dp_index ^ (piece // inner)) * part_rows
                position = row_position(owner, first, ctx_count, part_rows, span_rows)
                row = 2 * block * part_rows
                yield (
                    piece,
                    pl.ds(row, part_rows),
                    pl.ds(row + part_rows, part_rows),
                    pl.ds(tile + position, part_rows),
                )

    dead = jnp.zeros((tile, head_width), jnp.bfloat16)
    keys_ref[:tile, :] = dead
    values_ref[:tile, :] = dead
    for piece, key_rows, value_rows, ordered in blocks(line_steps(outer)):
        keys_ref[ordered, :] = kv_refs[piece][key_rows, :]
        values_ref[ordered, :] = kv_refs[piece][value_rows, :]
    count_copy.wait()
    group = min(256, cols)
    groups = [slice(start, start + group) for start in range(0, cols, group)]

    for half in range(2):
        first = span_first(half, ctx_count, span_rows)
        query_pos = first + lax.rem(
            lax.broadcasted_iota(jnp.int32, (1, group), 1), jnp.int32(span_rows)
        )
        doc_start = starts_ref[half]
        count = counts_ref[0, half]

        def tile_rows(index):
            position = first + span_rows - (index + 1) * tile
            rows = pl.ds(pl.multiple_of(tile + position, span_rows), tile)
            return position, rows, pl.ds(pl.multiple_of(index * tile, tile), tile)

        def sums_step(index, state):
            position, rows, slot = tile_rows(index)
            key_block, value_block = keys_ref[rows, :], values_ref[rows, :]
            all_logits = [
                jnp.dot(key_block, flip_ref[half, 0, :, lanes], preferred_element_type=jnp.float32)
                for lanes in groups
            ]
            all_dweights = [
                jnp.dot(
                    value_block, flip_ref[half, 1, :, lanes], preferred_element_type=jnp.float32
                )
                for lanes in groups
            ]
            following = []
            for lanes, logits, dweights, (top, total, mixed) in zip(
                groups, all_logits, all_dweights, state
            ):
                key_pos = lax.broadcasted_iota(jnp.int32, logits.shape, 0)
                live = (key_pos >= doc_start[:, lanes] - position) & (
                    key_pos <= query_pos - position
                )
                logits = jnp.where(live, logits * (scale * math.log2(math.e)), masked_value)
                new_top = jnp.maximum(top, jnp.max(logits, axis=0, keepdims=True))
                terms = jnp.exp2(logits - new_top)
                terms_ref[slot, lanes] = terms
                dweights_ref[slot, lanes] = dweights
                tops_ref[pl.ds(index, 1), lanes] = new_top
                decay = jnp.exp2(top - new_top)
                following.append(
                    (
                        new_top,
                        total * decay + jnp.sum(terms, axis=0, keepdims=True),
                        mixed * decay + jnp.sum(terms * dweights, axis=0, keepdims=True),
                    )
                )
            return tuple(following)

        zero = jnp.zeros((1, group), jnp.float32)
        empty = (jnp.full_like(zero, masked_value), zero, zero)
        sums = lax.fori_loop(0, count, sums_step, (empty,) * len(groups))
        top, total, mixed = (jnp.concatenate(part, axis=1) for part in zip(*sums))
        inverse = 1.0 / total
        delta = mixed * inverse

        def grads_step(index, carry):
            _, rows, slot = tile_rows(index)
            factor = jnp.exp2(tops_ref[pl.ds(index, 1), :] - top) * inverse
            weights = terms_ref[slot, :] * factor
            dlogits = (weights * (dweights_ref[slot, :] - delta)).astype(jnp.bfloat16)
            for lane_block in range(cols // head_width):
                dlogits_ref[half, lane_block, slot, :] = dlogits[
                    :, lane_block * head_width : (lane_block + 1) * head_width
                ]
            acc_ref[1, rows, :] += jnp.dot(
                weights.astype(jnp.bfloat16),
                stack_ref[half, 1],
                preferred_element_type=jnp.float32,
            )
            acc_ref[0, rows, :] += jnp.dot(
                dlogits, stack_ref[half, 0], preferred_element_type=jnp.float32
            )
            return carry

        lax.fori_loop(0, count, grads_step, 0)

    for piece, key_rows, value_rows, ordered in blocks(range(outer)):
        dkv_refs[piece][key_rows, :] = (scale * acc_ref[0, ordered, :]).astype(jnp.bfloat16)
        dkv_refs[piece][value_rows, :] = acc_ref[1, ordered, :].astype(jnp.bfloat16)


def query_kernel(
    ctx_count,
    tile,
    tiles_ref,
    keys_ref,
    dlogits_ref,
    passed_ref,
    dq_ref,
    same_ref,
    sum_ref,
    counts_ref,
    sem,
):
    tok_rows = dq_ref.shape[0]
    head_width = keys_ref.shape[1]
    span_rows = tok_rows // 2
    scale = head_width ** (-0.5)
    count_copy = pltpu.make_async_copy(tiles_ref, counts_ref, sem)
    count_copy.start()
    same_ref[...] = passed_ref[...]
    count_copy.wait()
    for half in range(2):
        end = span_first(half, ctx_count, span_rows) + span_rows
        sum_ref[...] = jnp.zeros_like(sum_ref)

        def query_step(index, carry):
            rows = pl.ds(pl.multiple_of(end - index * tile, span_rows), tile)
            slot = pl.ds(pl.multiple_of(index * tile, tile), tile)
            dlogits = jnp.concatenate(
                [dlogits_ref[half, block, slot, :] for block in range(dlogits_ref.shape[1])], axis=1
            )
            sum_ref[...] += jnp.dot(
                keys_ref[rows, :].T, dlogits, preferred_element_type=jnp.float32
            )
            return carry

        lax.fori_loop(0, counts_ref[0, half], query_step, 0)
        grads = (scale * sum_ref[...]).T.astype(jnp.bfloat16)
        for head in range(dq_ref.shape[1] // head_width):
            dq_ref[
                pl.ds(half * span_rows, span_rows), pl.ds(head * head_width, head_width)
            ] = grads[head * span_rows : (head + 1) * span_rows]


def prepare(ctx_count, tile, doc_lengths, queries, out_grads, head_width, line):
    tok_rows, width = queries.shape
    cols = width // head_width * (tok_rows // 2)
    unmoved = [
        pltpu.with_memory_space_constraint(argument, pltpu.HBM)
        for argument in (doc_lengths, queries, out_grads)
    ]
    return pl.pallas_call(
        functools.partial(prepare_kernel, ctx_count, tile),
        out_shape=(
            jax.ShapeDtypeStruct((2, 2, cols, head_width), jnp.bfloat16),
            jax.ShapeDtypeStruct((2, 2, head_width, cols), jnp.bfloat16),
            jax.ShapeDtypeStruct((2, 1, cols), jnp.int32),
            jax.ShapeDtypeStruct((8, 128), jnp.int32),
            jax.ShapeDtypeStruct((2, tile + ctx_count * tok_rows, head_width), jnp.float32),
            jax.ShapeDtypeStruct(line.shape, line.dtype),
        ),
        in_specs=[hbm, hbm, hbm, vmem],
        out_specs=[vmem] * 6,
        scratch_shapes=[
            pltpu.VMEM((2, tok_rows, width), jnp.bfloat16),
            pltpu.SMEM(doc_lengths.shape, jnp.int32),
            pltpu.SemaphoreType.DMA((3,)),
        ],
        compiler_params=pltpu.CompilerParams(vmem_limit_bytes=4 * 1024 * 1024),
    )(*unmoved, line)


def attend(ctx_count, dp_count, inner, tile, tiles, starts, stacked, flipped, zeros, pieces):
    cols, head_width = stacked.shape[2:]
    seq = dp_count * inner * pieces[0].shape[0] // 2
    slots = -(-seq // tile)
    results = pl.pallas_call(
        functools.partial(attend_kernel, ctx_count, dp_count, inner, tile),
        out_shape=[
            jax.ShapeDtypeStruct((tile + seq, head_width), jnp.bfloat16),
            jax.ShapeDtypeStruct(
                (2, cols // head_width, slots * tile, head_width), jnp.bfloat16
            ),
            jax.ShapeDtypeStruct(zeros.shape, zeros.dtype),
        ]
        + [jax.ShapeDtypeStruct(piece.shape, jnp.bfloat16) for piece in pieces],
        in_specs=[vmem] * (5 + len(pieces)),
        out_specs=[vmem] * (3 + len(pieces)),
        scratch_shapes=[
            pltpu.VMEM((tile + seq, head_width), jnp.bfloat16),
            pltpu.VMEM((slots * tile, cols), jnp.float32),
            pltpu.VMEM((slots * tile, cols), jnp.float32),
            pltpu.VMEM((slots, cols), jnp.float32),
            pltpu.SMEM((8, 128), jnp.int32),
            pltpu.SemaphoreType.DMA,
        ],
        input_output_aliases={4: 2},
        compiler_params=pltpu.CompilerParams(vmem_limit_bytes=32 * 1024 * 1024),
    )(tiles, starts, stacked, flipped, zeros, *pieces)
    return results[0], results[1], results[3:]


def query_side(ctx_count, tile, tiles, keys_ordered, dlogits, passed, tok_rows):
    head_width = keys_ordered.shape[1]
    cols = dlogits.shape[1] * head_width
    return pl.pallas_call(
        functools.partial(query_kernel, ctx_count, tile),
        out_shape=(
            jax.ShapeDtypeStruct(
                (tok_rows, cols // (tok_rows // 2) * head_width), jnp.bfloat16
            ),
            jax.ShapeDtypeStruct(passed.shape, passed.dtype),
        ),
        in_specs=[vmem] * 4,
        out_specs=(vmem, vmem),
        scratch_shapes=[
            pltpu.VMEM((head_width, cols), jnp.float32),
            pltpu.SMEM((8, 128), jnp.int32),
            pltpu.SemaphoreType.DMA,
        ],
        compiler_params=pltpu.CompilerParams(vmem_limit_bytes=8 * 1024 * 1024),
    )(tiles, keys_ordered, dlogits, passed)


def swap(value, axis, offset):
    pairs = [(index, index ^ offset) for index in range(lax.axis_size(axis))]
    return lax.ppermute(value, axis, pairs)


def total_of(terms):
    return sum(term.astype(jnp.float32) for term in terms).astype(jnp.bfloat16)


def body(queries, keys, values, out_grads, doc_lengths):
    ctx_count = lax.axis_size("ctx")
    dp_count = lax.axis_size("dp")
    inner = math.gcd(4, ctx_count)
    outer = ctx_count // inner
    tok_rows, head_width = keys.shape
    part_rows = tok_rows // dp_count
    tile = math.gcd(512, ctx_count * tok_rows)
    start = lax.axis_index("dp") * part_rows
    own_keys = lax.dynamic_slice_in_dim(keys, start, part_rows, 0)
    own_values = lax.dynamic_slice_in_dim(values, start, part_rows, 0)
    zero = jnp.zeros((), keys.dtype)
    own = jnp.where(
        lax.broadcasted_iota(jnp.int32, (2 * part_rows, head_width), 0) < part_rows,
        lax.pad(own_keys, zero, ((0, part_rows, 0), (0, 0, 0))),
        lax.pad(own_values, zero, ((part_rows, 0, 0), (0, 0, 0))),
    )
    line = jnp.concatenate(
        [own] + [swap(own, "ctx", step * inner) for step in line_steps(outer)[1:]], axis=0
    )
    plane = [line] + [swap(line, "ctx", offset) for offset in range(1, inner)]
    stacked, flipped, starts, tiles, zeros, plane[0] = prepare(
        ctx_count, tile, doc_lengths, queries, out_grads, head_width, line
    )
    pieces = plane + [
        swap(piece, "dp", offset) for offset in range(1, dp_count) for piece in plane
    ]
    keys_ordered, dlogits, parts = attend(
        ctx_count, dp_count, inner, tile, tiles, starts, stacked, flipped, zeros, pieces
    )
    plane_sums = [
        total_of(
            [parts[offset]]
            + [swap(parts[far * inner + offset], "dp", far) for far in range(1, dp_count)]
        )
        for offset in range(inner)
    ]
    query_grads, plane_sums[0] = query_side(
        ctx_count, tile, tiles, keys_ordered, dlogits, plane_sums[0], tok_rows
    )
    line_sum = total_of(
        [plane_sums[0]] + [swap(plane_sums[offset], "ctx", offset) for offset in reversed(range(1, inner))]
    )
    blocks = jnp.split(line_sum, outer, axis=0)
    kv_grads = total_of(
        [blocks[0]] + [swap(blocks[block], "ctx", block * inner) for block in send_order(outer)]
    )
    return (query_grads, kv_grads[:part_rows], kv_grads[part_rows:])


def solution(mesh):
    return jax.shard_map(
        body,
        mesh=mesh,
        in_specs=(P("ctx", "dp"), P("ctx", None), P("ctx", None), P("ctx", "dp"), P()),
        out_specs=(P("ctx", "dp"), P(("ctx", "dp"), None), P(("ctx", "dp"), None)),
        check_vma=False,
    )
```

```python
import functools
import math

import jax
import jax.numpy as jnp
from jax import lax
from jax.experimental import pallas as pl
from jax.experimental.pallas import tpu as pltpu
from jax.sharding import PartitionSpec as P

masked_value = -1e30

vmem = pl.BlockSpec(memory_space=pltpu.VMEM)
smem = pl.BlockSpec(memory_space=pltpu.SMEM)
hbm = pl.BlockSpec(memory_space=pltpu.HBM)


def row_position(ctx_index, start, ctx_count, rows, span_rows):
    low = ctx_index * span_rows + start
    high = (2 * ctx_count - 1 - ctx_index) * span_rows + start - span_rows
    return pl.multiple_of(jnp.where(start < span_rows, low, high), rows)


def span_first(half, ctx_count, span_rows):
    ctx_index = lax.axis_index("ctx")
    return (ctx_index if half == 0 else 2 * ctx_count - 1 - ctx_index) * span_rows


def prepare_kernel(
    ctx_count,
    tile,
    lengths_hbm,
    q_hbm,
    g_hbm,
    line_ref,
    stack_ref,
    flip_ref,
    starts_ref,
    tiles_ref,
    zero_ref,
    same_ref,
    raw_ref,
    lengths_ref,
    sems,
):
    tok_rows = q_hbm.shape[0]
    head_width = stack_ref.shape[3]
    cols = stack_ref.shape[2]
    span_rows = tok_rows // 2
    copies = [
        pltpu.make_async_copy(source, raw_ref.at[slot], sems.at[slot])
        for slot, source in enumerate((q_hbm, g_hbm))
    ]
    for copy in copies:
        copy.start()
    lengths_copy = pltpu.make_async_copy(lengths_hbm, lengths_ref, sems.at[2])
    lengths_copy.start()
    same_ref[...] = line_ref[...]
    zero_ref[...] = jnp.zeros_like(zero_ref)
    lane = lax.broadcasted_iota(jnp.int32, tiles_ref.shape, 1)
    tiles = jnp.zeros(tiles_ref.shape, jnp.int32)
    lengths_copy.wait()
    for half in range(2):
        first = span_first(half, ctx_count, span_rows)
        query_pos = first + lax.rem(
            lax.broadcasted_iota(jnp.int32, (1, cols), 1), jnp.int32(span_rows)
        )
        doc_start = jnp.zeros((1, cols), jnp.int32)
        first_key = jnp.int32(0)
        end = jnp.int32(0)
        for doc in range(lengths_ref.shape[0]):
            end = end + lengths_ref[doc]
            doc_start = jnp.where(query_pos >= end, end, doc_start)
            first_key = jnp.where(first >= end, end, first_key)
        starts_ref[half] = doc_start
        count = (first + span_rows - first_key + tile - 1) // tile
        tiles = jnp.where(lane == half, count, tiles)
    tiles_ref[...] = tiles
    for slot, copy in enumerate(copies):
        copy.wait()
        for half in range(2):
            for head in range(q_hbm.shape[1] // head_width):
                stack_ref[half, slot, pl.ds(head * span_rows, span_rows), :] = raw_ref[
                    slot,
                    pl.ds(half * span_rows, span_rows),
                    pl.ds(head * head_width, head_width),
                ]
            flip_ref[half, slot] = stack_ref[half, slot].T


def staged_moves(ctx_count, dp_count, inner, part_rows, ctx_index, dp_index):
    for piece in range(dp_count * inner):
        for block in range(ctx_count // inner):
            owner = ctx_index ^ (piece % inner) ^ (block * inner)
            start = (dp_index ^ (piece // inner)) * part_rows
            yield piece, 2 * block * part_rows, owner, start


def paired_moves(inner, part_rows, ctx_index, dp_index):
    for side in range(2):
        holder = dp_index ^ side
        for offset in range(inner):
            piece, near = side * inner + offset, ctx_index ^ offset
            whole = near ^ jnp.where(holder == 1, 3 * inner, inner)
            yield piece, 0, near, holder * part_rows
            yield piece, 2 * part_rows, near ^ (2 * inner), holder * part_rows
            yield piece, 4 * part_rows, whole, 0
            yield piece, 6 * part_rows, whole, part_rows


def send_order(outer):
    return (3, 1, 2) if outer == 4 else tuple(reversed(range(1, outer)))


def attend_kernel(
    ctx_count, dp_count, inner, tile, moves, tiles_ref, starts_ref, stack_ref, flip_ref, _, *refs
):
    piece_count = dp_count * inner
    kv_refs = refs[:piece_count]
    refs = refs[piece_count:]
    keys_ref, dlogits_ref, acc_ref = refs[:3]
    dkv_refs = refs[3 : piece_count + 3]
    values_ref, terms_ref, dweights_ref, tops_ref, counts_ref, sem = refs[piece_count + 3 :]
    cols, head_width = stack_ref.shape[2:]
    tok_rows = (keys_ref.shape[0] - tile) // ctx_count
    part_rows = tok_rows // dp_count
    span_rows = tok_rows // 2
    scale = head_width ** (-0.5)
    ctx_index = lax.axis_index("ctx")
    dp_index = lax.axis_index("dp")
    count_copy = pltpu.make_async_copy(tiles_ref, counts_ref, sem)
    count_copy.start()

    def rows_of(row, owner, start):
        position = row_position(owner, start, ctx_count, part_rows, span_rows)
        return (
            pl.ds(row, part_rows),
            pl.ds(row + part_rows, part_rows),
            pl.ds(tile + position, part_rows),
        )

    dead = jnp.zeros((tile, head_width), jnp.bfloat16)
    keys_ref[:tile, :] = dead
    values_ref[:tile, :] = dead
    for piece, *place in moves(ctx_index, dp_index):
        key_rows, value_rows, ordered = rows_of(*place)
        keys_ref[ordered, :] = kv_refs[piece][key_rows, :]
        values_ref[ordered, :] = kv_refs[piece][value_rows, :]
    count_copy.wait()
    group = min(256, cols)
    groups = [slice(start, start + group) for start in range(0, cols, group)]

    for half in range(2):
        first = span_first(half, ctx_count, span_rows)
        query_pos = first + lax.rem(
            lax.broadcasted_iota(jnp.int32, (1, group), 1), jnp.int32(span_rows)
        )
        doc_start = starts_ref[half]
        count = counts_ref[0, half]

        def tile_rows(index):
            position = first + span_rows - (index + 1) * tile
            rows = pl.ds(pl.multiple_of(tile + position, span_rows), tile)
            return position, rows, pl.ds(pl.multiple_of(index * tile, tile), tile)

        def sums_step(index, state, diagonal=False):
            position, rows, slot = tile_rows(index)
            key_block, value_block = keys_ref[rows, :], values_ref[rows, :]
            all_logits = [
                jnp.dot(key_block, flip_ref[half, 0, :, lanes], preferred_element_type=jnp.float32)
                for lanes in groups
            ]
            all_dweights = [
                jnp.dot(
                    value_block, flip_ref[half, 1, :, lanes], preferred_element_type=jnp.float32
                )
                for lanes in groups
            ]
            following = []
            for lanes, logits, dweights, (top, total, mixed) in zip(
                groups, all_logits, all_dweights, state
            ):
                key_pos = lax.broadcasted_iota(jnp.int32, logits.shape, 0)
                live = key_pos >= doc_start[:, lanes] - position
                if diagonal:
                    live = live & (key_pos <= query_pos - position)
                logits = jnp.where(live, logits * (scale * math.log2(math.e)), masked_value)
                new_top = jnp.maximum(top, jnp.max(logits, axis=0, keepdims=True))
                terms = jnp.exp2(logits - new_top)
                terms_ref[slot, lanes] = terms
                dweights_ref[slot, lanes] = dweights
                tops_ref[pl.ds(index, 1), lanes] = new_top
                decay = jnp.exp2(top - new_top)
                following.append(
                    (
                        new_top,
                        total * decay + jnp.sum(terms, axis=0, keepdims=True),
                        mixed * decay + jnp.sum(terms * dweights, axis=0, keepdims=True),
                    )
                )
            return tuple(following)

        zero = jnp.zeros((1, group), jnp.float32)
        empty = (jnp.full_like(zero, masked_value), zero, zero)
        sums = sums_step(0, (empty,) * len(groups), diagonal=True)
        sums = lax.fori_loop(1, count, sums_step, sums)
        top, total, mixed = (jnp.concatenate(part, axis=1) for part in zip(*sums))
        inverse = 1.0 / total
        delta = mixed * inverse

        def grads_step(index, carry):
            _, rows, slot = tile_rows(index)
            factor = jnp.exp2(tops_ref[pl.ds(index, 1), :] - top) * inverse
            weights = terms_ref[slot, :] * factor
            dlogits = (weights * (dweights_ref[slot, :] - delta)).astype(jnp.bfloat16)
            for lane_block in range(cols // head_width):
                dlogits_ref[half, lane_block, slot, :] = dlogits[
                    :, lane_block * head_width : (lane_block + 1) * head_width
                ]
            acc_ref[1, rows, :] += jnp.dot(
                weights.astype(jnp.bfloat16),
                stack_ref[half, 1],
                preferred_element_type=jnp.float32,
            )
            acc_ref[0, rows, :] += jnp.dot(
                dlogits, stack_ref[half, 0], preferred_element_type=jnp.float32
            )
            return carry

        lax.fori_loop(0, count, grads_step, 0)

    for piece, *place in staged_moves(
        ctx_count, dp_count, inner, part_rows, ctx_index, dp_index
    ):
        key_rows, value_rows, ordered = rows_of(*place)
        dkv_refs[piece][key_rows, :] = (scale * acc_ref[0, ordered, :]).astype(jnp.bfloat16)
        dkv_refs[piece][value_rows, :] = acc_ref[1, ordered, :].astype(jnp.bfloat16)


def query_kernel(
    ctx_count,
    tile,
    tiles_ref,
    keys_ref,
    dlogits_ref,
    passed_ref,
    dq_ref,
    same_ref,
    sum_ref,
    counts_ref,
    sem,
):
    tok_rows = dq_ref.shape[0]
    head_width = keys_ref.shape[1]
    span_rows = tok_rows // 2
    scale = head_width ** (-0.5)
    count_copy = pltpu.make_async_copy(tiles_ref, counts_ref, sem)
    count_copy.start()
    same_ref[...] = passed_ref[...]
    count_copy.wait()
    for half in range(2):
        end = span_first(half, ctx_count, span_rows) + span_rows
        sum_ref[...] = jnp.zeros_like(sum_ref)

        def query_step(index, carry):
            rows = pl.ds(pl.multiple_of(end - index * tile, span_rows), tile)
            slot = pl.ds(pl.multiple_of(index * tile, tile), tile)
            dlogits = jnp.concatenate(
                [dlogits_ref[half, block, slot, :] for block in range(dlogits_ref.shape[1])], axis=1
            )
            sum_ref[...] += jnp.dot(
                keys_ref[rows, :].T, dlogits, preferred_element_type=jnp.float32
            )
            return carry

        lax.fori_loop(0, counts_ref[0, half], query_step, 0)
        grads = (scale * sum_ref[...]).T.astype(jnp.bfloat16)
        for head in range(dq_ref.shape[1] // head_width):
            dq_ref[
                pl.ds(half * span_rows, span_rows), pl.ds(head * head_width, head_width)
            ] = grads[head * span_rows : (head + 1) * span_rows]


def prepare(ctx_count, tile, doc_lengths, queries, out_grads, head_width, line):
    tok_rows, width = queries.shape
    cols = width // head_width * (tok_rows // 2)
    unmoved = [
        pltpu.with_memory_space_constraint(argument, pltpu.HBM)
        for argument in (doc_lengths, queries, out_grads)
    ]
    return pl.pallas_call(
        functools.partial(prepare_kernel, ctx_count, tile),
        out_shape=(
            jax.ShapeDtypeStruct((2, 2, cols, head_width), jnp.bfloat16),
            jax.ShapeDtypeStruct((2, 2, head_width, cols), jnp.bfloat16),
            jax.ShapeDtypeStruct((2, 1, cols), jnp.int32),
            jax.ShapeDtypeStruct((8, 128), jnp.int32),
            jax.ShapeDtypeStruct((2, tile + ctx_count * tok_rows, head_width), jnp.float32),
            jax.ShapeDtypeStruct(line.shape, line.dtype),
        ),
        in_specs=[hbm, hbm, hbm, vmem],
        out_specs=[vmem] * 6,
        scratch_shapes=[
            pltpu.VMEM((2, tok_rows, width), jnp.bfloat16),
            pltpu.SMEM(doc_lengths.shape, jnp.int32),
            pltpu.SemaphoreType.DMA((3,)),
        ],
        compiler_params=pltpu.CompilerParams(vmem_limit_bytes=4 * 1024 * 1024),
    )(*unmoved, line)


def attend(ctx_count, dp_count, inner, tile, moves, tiles, starts, stacked, flipped, zeros, pieces):
    cols, head_width = stacked.shape[2:]
    seq = dp_count * inner * pieces[0].shape[0] // 2
    slots = -(-seq // tile)
    results = pl.pallas_call(
        functools.partial(attend_kernel, ctx_count, dp_count, inner, tile, moves),
        out_shape=[
            jax.ShapeDtypeStruct((tile + seq, head_width), jnp.bfloat16),
            jax.ShapeDtypeStruct(
                (2, cols // head_width, slots * tile, head_width), jnp.bfloat16
            ),
            jax.ShapeDtypeStruct(zeros.shape, zeros.dtype),
        ]
        + [jax.ShapeDtypeStruct(piece.shape, jnp.bfloat16) for piece in pieces],
        in_specs=[vmem] * (5 + len(pieces)),
        out_specs=[vmem] * (3 + len(pieces)),
        scratch_shapes=[
            pltpu.VMEM((tile + seq, head_width), jnp.bfloat16),
            pltpu.VMEM((slots * tile, cols), jnp.float32),
            pltpu.VMEM((slots * tile, cols), jnp.float32),
            pltpu.VMEM((slots, cols), jnp.float32),
            pltpu.SMEM((8, 128), jnp.int32),
            pltpu.SemaphoreType.DMA,
        ],
        input_output_aliases={4: 2},
        compiler_params=pltpu.CompilerParams(vmem_limit_bytes=32 * 1024 * 1024),
    )(tiles, starts, stacked, flipped, zeros, *pieces)
    return results[0], results[1], results[3:]


def query_side(ctx_count, tile, tiles, keys_ordered, dlogits, passed, tok_rows):
    head_width = keys_ordered.shape[1]
    cols = dlogits.shape[1] * head_width
    return pl.pallas_call(
        functools.partial(query_kernel, ctx_count, tile),
        out_shape=(
            jax.ShapeDtypeStruct(
                (tok_rows, cols // (tok_rows // 2) * head_width), jnp.bfloat16
            ),
            jax.ShapeDtypeStruct(passed.shape, passed.dtype),
        ),
        in_specs=[vmem] * 4,
        out_specs=(vmem, vmem),
        scratch_shapes=[
            pltpu.VMEM((head_width, cols), jnp.float32),
            pltpu.SMEM((8, 128), jnp.int32),
            pltpu.SemaphoreType.DMA,
        ],
        compiler_params=pltpu.CompilerParams(vmem_limit_bytes=8 * 1024 * 1024),
    )(tiles, keys_ordered, dlogits, passed)


def swap(value, axis, offset):
    pairs = [(index, index ^ offset) for index in range(lax.axis_size(axis))]
    return lax.ppermute(value, axis, pairs)


def total_of(terms):
    return sum(term.astype(jnp.float32) for term in terms).astype(jnp.bfloat16)


def staged_line(keys, values, inner, part_rows):
    head_width = keys.shape[1]
    outer = lax.axis_size("ctx") // inner
    start = lax.axis_index("dp") * part_rows
    own_keys = lax.dynamic_slice_in_dim(keys, start, part_rows, 0)
    own_values = lax.dynamic_slice_in_dim(values, start, part_rows, 0)
    zero = jnp.zeros((), keys.dtype)
    own = jnp.where(
        lax.broadcasted_iota(jnp.int32, (2 * part_rows, head_width), 0) < part_rows,
        lax.pad(own_keys, zero, ((0, part_rows, 0), (0, 0, 0))),
        lax.pad(own_values, zero, ((part_rows, 0, 0), (0, 0, 0))),
    )
    others = [swap(own, "ctx", step * inner) for step in range(1, outer)]
    return jnp.concatenate([own] + others, axis=0)


def paired_line(keys, values, inner, part_rows):
    head_width = keys.shape[1]
    halves = (2, 1, part_rows, head_width)
    own = jnp.where(
        lax.broadcasted_iota(jnp.int32, (2, 2, part_rows, head_width), 1) == 0,
        keys.reshape(halves),
        values.reshape(halves),
    ).reshape(4 * part_rows, head_width)
    rows = 2 * part_rows
    own_half = lax.dynamic_slice_in_dim(own, lax.axis_index("dp") * rows, rows, 0)
    pairs = [
        (2 * ctx + dp, 2 * (ctx ^ ((3 if dp else 1) * inner)) + dp)
        for ctx in range(lax.axis_size("ctx"))
        for dp in range(2)
    ]
    whole = lax.ppermute(own, ("ctx", "dp"), pairs)
    return jnp.concatenate([own_half, swap(own_half, "ctx", 2 * inner), whole], axis=0)


def body(queries, keys, values, out_grads, doc_lengths):
    ctx_count = lax.axis_size("ctx")
    dp_count = lax.axis_size("dp")
    inner = math.gcd(4, ctx_count)
    outer = ctx_count // inner
    tok_rows, head_width = keys.shape
    part_rows = tok_rows // dp_count
    tile = math.gcd(256, ctx_count * tok_rows)
    if outer == 4 and dp_count == 2:
        line = paired_line(keys, values, inner, part_rows)
        moves = functools.partial(paired_moves, inner, part_rows)
    else:
        line = staged_line(keys, values, inner, part_rows)
        moves = functools.partial(staged_moves, ctx_count, dp_count, inner, part_rows)
    plane = [line] + [swap(line, "ctx", offset) for offset in range(1, inner)]
    stacked, flipped, starts, tiles, zeros, plane[0] = prepare(
        ctx_count, tile, doc_lengths, queries, out_grads, head_width, line
    )
    pieces = plane + [
        swap(piece, "dp", offset) for offset in range(1, dp_count) for piece in plane
    ]
    keys_ordered, dlogits, parts = attend(
        ctx_count, dp_count, inner, tile, moves, tiles, starts, stacked, flipped, zeros, pieces
    )
    plane_sums = [
        total_of(
            [parts[offset]]
            + [swap(parts[far * inner + offset], "dp", far) for far in range(1, dp_count)]
        )
        for offset in range(inner)
    ]
    query_grads, plane_sums[0] = query_side(
        ctx_count, tile, tiles, keys_ordered, dlogits, plane_sums[0], tok_rows
    )
    line_sum = total_of(
        [plane_sums[0]] + [swap(plane_sums[offset], "ctx", offset) for offset in reversed(range(1, inner))]
    )
    blocks = jnp.split(line_sum, outer, axis=0)
    kv_grads = total_of(
        [blocks[0]] + [swap(blocks[block], "ctx", block * inner) for block in send_order(outer)]
    )
    return (query_grads, kv_grads[:part_rows], kv_grads[part_rows:])


def solution(mesh):
    return jax.shard_map(
        body,
        mesh=mesh,
        in_specs=(P("ctx", "dp"), P("ctx", None), P("ctx", None), P("ctx", "dp"), P()),
        out_specs=(P("ctx", "dp"), P(("ctx", "dp"), None), P(("ctx", "dp"), None)),
        check_vma=False,
    )
```

```python
import functools
import math

import jax
import jax.numpy as jnp
from jax import lax
from jax.experimental import pallas as pl
from jax.experimental.pallas import tpu as pltpu
from jax.sharding import PartitionSpec as P

masked_value = -1e30

vmem = pl.BlockSpec(memory_space=pltpu.VMEM)
smem = pl.BlockSpec(memory_space=pltpu.SMEM)
hbm = pl.BlockSpec(memory_space=pltpu.HBM)


def span_first(half, ctx_count, span_rows):
    ctx_index = lax.axis_index("ctx")
    return (ctx_index if half == 0 else 2 * ctx_count - 1 - ctx_index) * span_rows


def prepare_kernel(
    ctx_count,
    lengths_hbm,
    q_hbm,
    g_hbm,
    line_ref,
    stack_ref,
    flip_ref,
    starts_ref,
    bounds_ref,
    same_ref,
    raw_ref,
    lengths_ref,
    sems,
):
    tok_rows = q_hbm.shape[0]
    head_width = stack_ref.shape[3]
    cols = stack_ref.shape[2]
    span_rows = tok_rows // 2
    copies = [
        pltpu.make_async_copy(source, raw_ref.at[slot], sems.at[slot])
        for slot, source in enumerate((q_hbm, g_hbm))
    ]
    for copy in copies:
        copy.start()
    lengths_copy = pltpu.make_async_copy(lengths_hbm, lengths_ref, sems.at[2])
    lengths_copy.start()
    same_ref[...] = line_ref[...]
    lane = lax.broadcasted_iota(jnp.int32, bounds_ref.shape, 1)
    bounds = jnp.zeros(bounds_ref.shape, jnp.int32)
    lengths_copy.wait()
    for half in range(2):
        first = span_first(half, ctx_count, span_rows)
        query_pos = first + lax.rem(
            lax.broadcasted_iota(jnp.int32, (1, cols), 1), jnp.int32(span_rows)
        )
        doc_start = jnp.zeros((1, cols), jnp.int32)
        first_key = jnp.int32(0)
        end = jnp.int32(0)
        for doc in range(lengths_ref.shape[0]):
            end = end + lengths_ref[doc]
            doc_start = jnp.where(query_pos >= end, end, doc_start)
            first_key = jnp.where(first >= end, end, first_key)
        starts_ref[half] = doc_start
        bounds = jnp.where(lane == half, first_key, bounds)
    bounds_ref[...] = bounds
    for slot, copy in enumerate(copies):
        copy.wait()
        for half in range(2):
            for head in range(q_hbm.shape[1] // head_width):
                stack_ref[half, slot, pl.ds(head * span_rows, span_rows), :] = raw_ref[
                    slot,
                    pl.ds(half * span_rows, span_rows),
                    pl.ds(head * head_width, head_width),
                ]
            flip_ref[half, slot] = stack_ref[half, slot].T


def staged_moves(ctx_count, dp_count, inner, part_rows, ctx_index, dp_index):
    for piece in range(dp_count * inner):
        for block in range(ctx_count // inner):
            owner = ctx_index ^ (piece % inner) ^ (block * inner)
            start = (dp_index ^ (piece // inner)) * part_rows
            yield piece, 2 * block * part_rows, owner, start


def paired_moves(inner, part_rows, ctx_index, dp_index):
    for side in range(2):
        holder = dp_index ^ side
        for offset in range(inner):
            piece, near = side * inner + offset, ctx_index ^ offset
            whole = near ^ jnp.where(holder == 1, 3 * inner, inner)
            yield piece, 0, near, holder * part_rows
            yield piece, 2 * part_rows, near ^ (2 * inner), holder * part_rows
            yield piece, 4 * part_rows, whole, 0
            yield piece, 6 * part_rows, whole, part_rows


def send_order(outer):
    return (3, 1, 2) if outer == 4 else tuple(reversed(range(1, outer)))


def tile_spans(ctx_count, inner, offset):
    lane = lax.axis_index("ctx") ^ offset
    lane = lane & (inner - 1)
    low = lane
    high = ctx_count + inner - 1 - lane
    return low, low, high


tile_halves = (0, 1, 1)


def tile_live(ctx_count, inner, offset, span_rows, bounds_ref):
    outer = ctx_count // inner
    ctx_index = lax.axis_index("ctx")
    alive = []
    for half, first in zip(tile_halves, tile_spans(ctx_count, inner, offset)):
        span = ctx_index if half == 0 else 2 * ctx_count - 1 - ctx_index
        steps = jnp.minimum(lax.div(span - first, jnp.int32(inner)), outer - 1)
        last = first + inner * steps
        alive.append((first <= span) & ((last + 1) * span_rows > bounds_ref[0, half]))
    return alive


def tile_row(ctx_count, inner, part_rows, span_rows, owner, start):
    outer = ctx_count // inner
    step = lax.div(owner, jnp.int32(inner))
    low = step * span_rows + start
    high = (2 * outer - 1 - step) * span_rows + start - span_rows
    return pl.ds(pl.multiple_of(jnp.where(start < span_rows, low, high), part_rows), part_rows)


def scores_kernel(
    ctx_count, dp_count, inner, offset, moves, bounds_vmem, starts_ref, flip_ref, *refs
):
    kv_refs = refs[:dp_count]
    passed_ref, keys_ref, terms_ref, dweights_ref, stats_ref, same_ref = refs[
        dp_count : dp_count + 6
    ]
    values_ref, bounds_ref, sem = refs[dp_count + 6 :]
    same_ref[...] = passed_ref[...]
    outer = ctx_count // inner
    cols = flip_ref.shape[3]
    head_width = keys_ref.shape[1]
    tile = keys_ref.shape[0] // 2
    span_rows = tile // outer
    part_rows = 2 * span_rows // dp_count
    scale = head_width ** (-0.5)
    bounds_copy = pltpu.make_async_copy(bounds_vmem, bounds_ref, sem)
    bounds_copy.start()
    for piece, row, owner, start in moves(lax.axis_index("ctx"), lax.axis_index("dp")):
        if piece % inner == offset:
            rows = tile_row(ctx_count, inner, part_rows, span_rows, owner, start)
            source = kv_refs[piece // inner]
            keys_ref[rows, :] = source[pl.ds(row, part_rows), :]
            values_ref[rows, :] = source[pl.ds(row + part_rows, part_rows), :]
    lane_groups = [
        slice(start, start + min(256, cols)) for start in range(0, cols, min(256, cols))
    ]
    stat_row = lax.broadcasted_iota(jnp.int32, stats_ref.shape, 0)
    stats_ref[...] = jnp.where(lax.rem(stat_row, 3) == 0, masked_value, 0.0)
    bounds_copy.wait()
    alive = tile_live(ctx_count, inner, offset, span_rows, bounds_ref)
    for kind, first in enumerate(tile_spans(ctx_count, inner, offset)):
        half = tile_halves[kind]
        rows = slice(tile, 2 * tile) if kind == 2 else slice(0, tile)

        @pl.when(alive[kind])
        def _():
            for lanes in lane_groups:
                logits = jnp.dot(
                    keys_ref[rows, :], flip_ref[half, 0, :, lanes],
                    preferred_element_type=jnp.float32,
                )
                dweights = jnp.dot(
                    values_ref[rows, :], flip_ref[half, 1, :, lanes],
                    preferred_element_type=jnp.float32,
                )
                group = logits.shape[1]
                query_pos = span_first(half, ctx_count, span_rows) + lax.rem(
                    lax.broadcasted_iota(jnp.int32, (1, group), 1), jnp.int32(span_rows)
                )
                key_row = lax.broadcasted_iota(jnp.int32, (span_rows, group), 0)
                masked = []
                for step in range(outer):
                    position = (first + inner * step) * span_rows
                    live = key_row >= starts_ref[half, :, lanes] - position
                    if kind != 1:
                        live = live & (key_row <= query_pos - position)
                    part = logits[step * span_rows : (step + 1) * span_rows]
                    masked.append(
                        jnp.where(live, part * (scale * math.log2(math.e)), masked_value)
                    )
                top = jnp.max(functools.reduce(jnp.maximum, masked), axis=0, keepdims=True)
                total, mixed = 0.0, 0.0
                for step in range(outer):
                    part_rows_here = slice(step * span_rows, (step + 1) * span_rows)
                    terms = jnp.exp2(masked[step] - top)
                    part = dweights[part_rows_here]
                    terms_ref[kind, part_rows_here, lanes] = terms
                    dweights_ref[kind, part_rows_here, lanes] = part
                    total = total + terms
                    mixed = mixed + terms * part
                stats_ref[3 * kind : 3 * kind + 1, lanes] = top
                stats_ref[3 * kind + 1 : 3 * kind + 2, lanes] = jnp.sum(
                    total, axis=0, keepdims=True
                )
                stats_ref[3 * kind + 2 : 3 * kind + 3, lanes] = jnp.sum(
                    mixed, axis=0, keepdims=True
                )


def grads_kernel(ctx_count, dp_count, inner, offset, bounds_vmem, stack_ref, _, *refs):
    stats_refs = refs[:inner]
    terms_ref, dweights_ref = refs[inner : inner + 2]
    dlogits_ref = refs[inner + 2]
    dkv_refs = refs[inner + 3 : inner + 3 + dp_count]
    acc_ref, bounds_ref, sem = refs[inner + 3 + dp_count :]
    outer = ctx_count // inner
    cols, head_width = stack_ref.shape[2:]
    tile = terms_ref.shape[1]
    span_rows = tile // outer
    part_rows = 2 * span_rows // dp_count
    scale = head_width ** (-0.5)
    bounds_copy = pltpu.make_async_copy(bounds_vmem, bounds_ref, sem)
    bounds_copy.start()
    acc_ref[...] = jnp.zeros_like(acc_ref)
    sums = []
    for half in range(2):
        tiles = [
            [ref[3 * kind + which : 3 * kind + which + 1, :] for which in range(3)]
            for ref in stats_refs
            for kind in range(3)
            if tile_halves[kind] == half
        ]
        top = functools.reduce(jnp.maximum, [tops for tops, _, _ in tiles])
        decays = [jnp.exp2(tops - top) for tops, _, _ in tiles]
        total = sum(decay * part for decay, (_, part, _) in zip(decays, tiles))
        mixed = sum(decay * part for decay, (_, _, part) in zip(decays, tiles))
        inverse = 1.0 / total
        sums.append((top, inverse, mixed * inverse))
    bounds_copy.wait()
    alive = tile_live(ctx_count, inner, offset, span_rows, bounds_ref)
    for kind, half in enumerate(tile_halves):
        rows = slice(tile, 2 * tile) if kind == 2 else slice(0, tile)
        top, inverse, delta = sums[half]

        @pl.when(alive[kind])
        def _():
            factor = jnp.exp2(stats_refs[offset][3 * kind : 3 * kind + 1, :] - top) * inverse
            weights = terms_ref[kind] * factor
            dlogits = (weights * (dweights_ref[kind] - delta)).astype(jnp.bfloat16)
            for lane_block in range(cols // head_width):
                dlogits_ref[kind, lane_block] = dlogits[
                    :, lane_block * head_width : (lane_block + 1) * head_width
                ]
            acc_ref[1, rows, :] += jnp.dot(
                weights.astype(jnp.bfloat16),
                stack_ref[half, 1],
                preferred_element_type=jnp.float32,
            )
            acc_ref[0, rows, :] += jnp.dot(
                dlogits, stack_ref[half, 0], preferred_element_type=jnp.float32
            )

    for piece, row, owner, start in staged_moves(
        ctx_count, dp_count, inner, part_rows, lax.axis_index("ctx"), lax.axis_index("dp")
    ):
        if piece % inner == offset:
            rows = tile_row(ctx_count, inner, part_rows, span_rows, owner, start)
            target = dkv_refs[piece // inner]
            target[pl.ds(row, part_rows), :] = (scale * acc_ref[0, rows, :]).astype(jnp.bfloat16)
            target[pl.ds(row + part_rows, part_rows), :] = acc_ref[1, rows, :].astype(jnp.bfloat16)


def query_kernel(ctx_count, inner, bounds_vmem, *refs):
    keys_refs = refs[:inner]
    dlogits_refs = refs[inner : 2 * inner]
    passed_ref, dq_ref, same_ref, sum_ref, bounds_ref, sem = refs[2 * inner :]
    head_width = keys_refs[0].shape[1]
    tile = keys_refs[0].shape[0] // 2
    span_rows = dq_ref.shape[0] // 2
    scale = head_width ** (-0.5)
    bounds_copy = pltpu.make_async_copy(bounds_vmem, bounds_ref, sem)
    bounds_copy.start()
    same_ref[...] = passed_ref[...]
    sum_ref[...] = jnp.zeros_like(sum_ref)
    bounds_copy.wait()
    for offset in range(inner):
        alive = tile_live(ctx_count, inner, offset, span_rows, bounds_ref)
        for kind, half in enumerate(tile_halves):

            @pl.when(alive[kind])
            def _():
                rows = slice(tile, 2 * tile) if kind == 2 else slice(0, tile)
                dlogits = jnp.concatenate(
                    [
                        dlogits_refs[offset][kind, lane_block]
                        for lane_block in range(dlogits_refs[offset].shape[1])
                    ],
                    axis=1,
                )
                sum_ref[half] += jnp.dot(
                    keys_refs[offset][rows, :].T, dlogits, preferred_element_type=jnp.float32
                )

    for half in range(2):
        grads = (scale * sum_ref[half]).T.astype(jnp.bfloat16)
        for head in range(dq_ref.shape[1] // head_width):
            dq_ref[
                pl.ds(half * span_rows, span_rows), pl.ds(head * head_width, head_width)
            ] = grads[head * span_rows : (head + 1) * span_rows]


def prepare(ctx_count, doc_lengths, queries, out_grads, head_width, line):
    tok_rows, width = queries.shape
    cols = width // head_width * (tok_rows // 2)
    unmoved = [
        pltpu.with_memory_space_constraint(argument, pltpu.HBM)
        for argument in (doc_lengths, queries, out_grads)
    ]
    return pl.pallas_call(
        functools.partial(prepare_kernel, ctx_count),
        out_shape=(
            jax.ShapeDtypeStruct((2, 2, cols, head_width), jnp.bfloat16),
            jax.ShapeDtypeStruct((2, 2, head_width, cols), jnp.bfloat16),
            jax.ShapeDtypeStruct((2, 1, cols), jnp.int32),
            jax.ShapeDtypeStruct((8, 128), jnp.int32),
            jax.ShapeDtypeStruct(line.shape, line.dtype),
        ),
        in_specs=[hbm, hbm, hbm, vmem],
        out_specs=[vmem] * 5,
        scratch_shapes=[
            pltpu.VMEM((2, tok_rows, width), jnp.bfloat16),
            pltpu.SMEM(doc_lengths.shape, jnp.int32),
            pltpu.SemaphoreType.DMA((3,)),
        ],
        compiler_params=pltpu.CompilerParams(vmem_limit_bytes=4 * 1024 * 1024),
    )(*unmoved, line)


def bounds_scratch():
    return [pltpu.SMEM((8, 128), jnp.int32), pltpu.SemaphoreType.DMA]


def scores(ctx_count, dp_count, inner, offset, moves, bounds, starts, flipped, pieces, passed):
    head_width, cols = flipped.shape[2:]
    tile = dp_count * pieces[0].shape[0] // 4
    return pl.pallas_call(
        functools.partial(scores_kernel, ctx_count, dp_count, inner, offset, moves),
        out_shape=(
            jax.ShapeDtypeStruct((2 * tile, head_width), jnp.bfloat16),
            jax.ShapeDtypeStruct((3, tile, cols), jnp.float32),
            jax.ShapeDtypeStruct((3, tile, cols), jnp.float32),
            jax.ShapeDtypeStruct((16, cols), jnp.float32),
            jax.ShapeDtypeStruct(passed.shape, passed.dtype),
        ),
        in_specs=[vmem] * (4 + dp_count),
        out_specs=[vmem] * 5,
        scratch_shapes=[pltpu.VMEM((2 * tile, head_width), jnp.bfloat16)] + bounds_scratch(),
        compiler_params=pltpu.CompilerParams(vmem_limit_bytes=12 * 1024 * 1024),
    )(bounds, starts, flipped, *pieces, passed)


def piece_grads(
    ctx_count, dp_count, inner, offset, bounds, stacked, after, stats, terms, dweights
):
    cols, head_width = stacked.shape[2:]
    tile = terms.shape[1]
    part = jax.ShapeDtypeStruct((4 * tile // dp_count, head_width), jnp.bfloat16)
    dlogits, *parts = pl.pallas_call(
        functools.partial(grads_kernel, ctx_count, dp_count, inner, offset),
        out_shape=[
            jax.ShapeDtypeStruct((3, cols // head_width, tile, head_width), jnp.bfloat16)
        ]
        + [part] * dp_count,
        in_specs=[vmem] * 2 + [pl.BlockSpec(memory_space=pl.ANY)] + [vmem] * (2 + inner),
        out_specs=[vmem] * (1 + dp_count),
        scratch_shapes=[pltpu.VMEM((2, 2 * tile, head_width), jnp.float32)] + bounds_scratch(),
        compiler_params=pltpu.CompilerParams(vmem_limit_bytes=12 * 1024 * 1024),
    )(bounds, stacked, after, *stats, terms, dweights)
    return dlogits, parts


def query_side(ctx_count, inner, bounds, keys_ordered, dlogits, passed, tok_rows):
    head_width = keys_ordered[0].shape[1]
    cols = dlogits[0].shape[1] * head_width
    return pl.pallas_call(
        functools.partial(query_kernel, ctx_count, inner),
        out_shape=(
            jax.ShapeDtypeStruct(
                (tok_rows, cols // (tok_rows // 2) * head_width), jnp.bfloat16
            ),
            jax.ShapeDtypeStruct(passed.shape, passed.dtype),
        ),
        in_specs=[vmem] * (2 + 2 * inner),
        out_specs=(vmem, vmem),
        scratch_shapes=[pltpu.VMEM((2, head_width, cols), jnp.float32)] + bounds_scratch(),
        compiler_params=pltpu.CompilerParams(vmem_limit_bytes=8 * 1024 * 1024),
    )(bounds, *keys_ordered, *dlogits, passed)


def swap(value, axis, offset):
    pairs = [(index, index ^ offset) for index in range(lax.axis_size(axis))]
    return lax.ppermute(value, axis, pairs)


def total_of(terms):
    return sum(term.astype(jnp.float32) for term in terms).astype(jnp.bfloat16)


def staged_line(keys, values, inner, part_rows, run_prepare):
    head_width = keys.shape[1]
    outer = lax.axis_size("ctx") // inner
    start = lax.axis_index("dp") * part_rows
    own_keys = lax.dynamic_slice_in_dim(keys, start, part_rows, 0)
    own_values = lax.dynamic_slice_in_dim(values, start, part_rows, 0)
    zero = jnp.zeros((), keys.dtype)
    own = jnp.where(
        lax.broadcasted_iota(jnp.int32, (2 * part_rows, head_width), 0) < part_rows,
        lax.pad(own_keys, zero, ((0, part_rows, 0), (0, 0, 0))),
        lax.pad(own_values, zero, ((part_rows, 0, 0), (0, 0, 0))),
    )
    others = [swap(own, "ctx", step * inner) for step in range(1, outer)]
    prepared, others[-1] = run_prepare(others[-1])
    return prepared, jnp.concatenate([own] + others, axis=0)


def paired_line(keys, values, inner, part_rows, run_prepare):
    head_width = keys.shape[1]
    halves = (2, 1, part_rows, head_width)
    own = jnp.where(
        lax.broadcasted_iota(jnp.int32, (2, 2, part_rows, head_width), 1) == 0,
        keys.reshape(halves),
        values.reshape(halves),
    ).reshape(4 * part_rows, head_width)
    rows = 2 * part_rows
    own_half = lax.dynamic_slice_in_dim(own, lax.axis_index("dp") * rows, rows, 0)
    pairs = [
        (2 * ctx + dp, 2 * (ctx ^ ((3 if dp else 1) * inner)) + dp)
        for ctx in range(lax.axis_size("ctx"))
        for dp in range(2)
    ]
    whole = lax.ppermute(own, ("ctx", "dp"), pairs)
    prepared, whole = run_prepare(whole)
    line = jnp.concatenate([own_half, swap(own_half, "ctx", 2 * inner), whole], axis=0)
    return prepared, line


def body(queries, keys, values, out_grads, doc_lengths):
    ctx_count = lax.axis_size("ctx")
    dp_count = lax.axis_size("dp")
    inner = math.gcd(4, ctx_count)
    outer = ctx_count // inner
    tok_rows, head_width = keys.shape
    part_rows = tok_rows // dp_count

    def run_prepare(held):
        *prepared, held = prepare(ctx_count, doc_lengths, queries, out_grads, head_width, held)
        return prepared, held

    if outer == 4 and dp_count == 2:
        make_line, moves = paired_line, functools.partial(paired_moves, inner, part_rows)
    else:
        make_line = staged_line
        moves = functools.partial(staged_moves, ctx_count, dp_count, inner, part_rows)
    (stacked, flipped, starts, bounds), line = make_line(
        keys, values, inner, part_rows, run_prepare
    )
    plane = [line] + [swap(line, "ctx", offset) for offset in range(1, inner)]
    scored = {}
    for offset in [0] + list(reversed(range(1, inner))):
        pieces = [plane[offset]] + [swap(plane[offset], "dp", far) for far in range(1, dp_count)]
        passed = plane[-1] if offset == 0 else bounds
        *scored[offset], passed = scores(
            ctx_count, dp_count, inner, offset, moves, bounds, starts, flipped, pieces, passed
        )
        if offset == 0:
            plane[-1] = passed
    stats = [scored[offset][3] for offset in range(inner)]
    dlogits, plane_sums = [None] * inner, [None] * inner
    for offset in reversed(range(inner)):
        after = plane_sums[offset + 2] if offset + 2 < inner else bounds
        dlogits[offset], parts = piece_grads(
            ctx_count, dp_count, inner, offset, bounds, stacked, after, stats, *scored[offset][1:3]
        )
        plane_sums[offset] = total_of(
            [parts[0]] + [swap(parts[far], "dp", far) for far in range(1, dp_count)]
        )
    query_grads, plane_sums[0] = query_side(
        ctx_count,
        inner,
        bounds,
        [scored[offset][0] for offset in range(inner)],
        dlogits,
        plane_sums[0],
        tok_rows,
    )
    line_sum = total_of(
        [plane_sums[0]] + [swap(plane_sums[offset], "ctx", offset) for offset in reversed(range(1, inner))]
    )
    blocks = jnp.split(line_sum, outer, axis=0)
    kv_grads = total_of(
        [blocks[0]] + [swap(blocks[block], "ctx", block * inner) for block in send_order(outer)]
    )
    return (query_grads, kv_grads[:part_rows], kv_grads[part_rows:])


def solution(mesh):
    return jax.shard_map(
        body,
        mesh=mesh,
        in_specs=(P("ctx", "dp"), P("ctx", None), P("ctx", None), P("ctx", "dp"), P()),
        out_specs=(P("ctx", "dp"), P(("ctx", "dp"), None), P(("ctx", "dp"), None)),
        check_vma=False,
    )
```

```python
import functools
import math

import jax
import jax.numpy as jnp
from jax import lax
from jax.experimental import pallas as pl
from jax.experimental.pallas import tpu as pltpu
from jax.sharding import PartitionSpec as P

masked_value = -1e30

vmem = pl.BlockSpec(memory_space=pltpu.VMEM)
smem = pl.BlockSpec(memory_space=pltpu.SMEM)
hbm = pl.BlockSpec(memory_space=pltpu.HBM)


def row_position(ctx_index, start, ctx_count, rows, span_rows):
    low = ctx_index * span_rows + start
    high = (2 * ctx_count - 1 - ctx_index) * span_rows + start - span_rows
    return pl.multiple_of(jnp.where(start < span_rows, low, high), rows)


def span_first(half, ctx_count, span_rows):
    ctx_index = lax.axis_index("ctx")
    return (ctx_index if half == 0 else 2 * ctx_count - 1 - ctx_index) * span_rows


def prepare_kernel(
    ctx_count,
    tile,
    lengths_hbm,
    q_hbm,
    g_hbm,
    line_ref,
    stack_ref,
    flip_ref,
    starts_ref,
    tiles_ref,
    zero_ref,
    same_ref,
    raw_ref,
    lengths_ref,
    sems,
):
    tok_rows = q_hbm.shape[0]
    head_width = stack_ref.shape[3]
    cols = stack_ref.shape[2]
    span_rows = tok_rows // 2
    copies = [
        pltpu.make_async_copy(source, raw_ref.at[slot], sems.at[slot])
        for slot, source in enumerate((q_hbm, g_hbm))
    ]
    for copy in copies:
        copy.start()
    lengths_copy = pltpu.make_async_copy(lengths_hbm, lengths_ref, sems.at[2])
    lengths_copy.start()
    same_ref[...] = line_ref[...]
    zero_ref[...] = jnp.zeros_like(zero_ref)
    lane = lax.broadcasted_iota(jnp.int32, tiles_ref.shape, 1)
    tiles = jnp.zeros(tiles_ref.shape, jnp.int32)
    lengths_copy.wait()
    for half in range(2):
        first = span_first(half, ctx_count, span_rows)
        query_pos = first + lax.rem(
            lax.broadcasted_iota(jnp.int32, (1, cols), 1), jnp.int32(span_rows)
        )
        doc_start = jnp.zeros((1, cols), jnp.int32)
        first_key = jnp.int32(0)
        end = jnp.int32(0)
        for doc in range(lengths_ref.shape[0]):
            end = end + lengths_ref[doc]
            doc_start = jnp.where(query_pos >= end, end, doc_start)
            first_key = jnp.where(first >= end, end, first_key)
        starts_ref[half] = doc_start
        count = (first + span_rows - first_key + tile - 1) // tile
        tiles = jnp.where(lane == half, count, tiles)
    tiles_ref[...] = tiles
    for slot, copy in enumerate(copies):
        copy.wait()
        for half in range(2):
            for head in range(q_hbm.shape[1] // head_width):
                stack_ref[half, slot, pl.ds(head * span_rows, span_rows), :] = raw_ref[
                    slot,
                    pl.ds(half * span_rows, span_rows),
                    pl.ds(head * head_width, head_width),
                ]
            flip_ref[half, slot] = stack_ref[half, slot].T


def staged_moves(ctx_count, dp_count, inner, part_rows, ctx_index, dp_index):
    for piece in range(dp_count * inner):
        for block in range(ctx_count // inner):
            owner = ctx_index ^ (piece % inner) ^ (block * inner)
            start = (dp_index ^ (piece // inner)) * part_rows
            yield piece, 2 * block * part_rows, owner, start


def paired_moves(inner, part_rows, ctx_index, dp_index):
    yield 0, 0, ctx_index, 0
    yield 0, 2 * part_rows, ctx_index, part_rows
    for side in range(2):
        holder = dp_index ^ side
        pieces = 1 + side * (inner + 1)
        for offset in range(1, inner):
            near = ctx_index ^ offset
            yield pieces, 2 * (offset - 1) * part_rows, near, holder * part_rows
        for offset in range(inner):
            piece, near = pieces + 1 + offset, ctx_index ^ offset
            whole = near ^ jnp.where(holder == 1, 3 * inner, inner)
            yield piece, 0, whole, 0
            yield piece, 2 * part_rows, whole, part_rows
            yield piece, 4 * part_rows, near ^ (2 * inner), holder * part_rows


def part_moves(ctx_count, dp_count, inner, part_rows, ctx_index, dp_index):
    for far in range(dp_count):
        start = (dp_index ^ far) * part_rows
        for offset in range(inner):
            near = ctx_index ^ offset
            yield far * (inner + 1), 2 * offset * part_rows, near, start
            for block in range(1, ctx_count // inner):
                piece = far * (inner + 1) + 1 + offset
                yield piece, 2 * (block - 1) * part_rows, near ^ (block * inner), start


def send_order(outer):
    return (3, 1, 2) if outer == 4 else tuple(reversed(range(1, outer)))


def attend_kernel(
    ctx_count,
    dp_count,
    inner,
    tile,
    moves,
    piece_count,
    part_count,
    tiles_ref,
    starts_ref,
    stack_ref,
    flip_ref,
    _,
    *refs,
):
    kv_refs = refs[:piece_count]
    refs = refs[piece_count:]
    keys_ref, dlogits_ref, acc_ref = refs[:3]
    dkv_refs = refs[3 : part_count + 3]
    values_ref, terms_ref, dweights_ref, tops_ref, counts_ref, sem = refs[part_count + 3 :]
    cols, head_width = stack_ref.shape[2:]
    tok_rows = (keys_ref.shape[0] - tile) // ctx_count
    part_rows = tok_rows // dp_count
    span_rows = tok_rows // 2
    scale = head_width ** (-0.5)
    ctx_index = lax.axis_index("ctx")
    dp_index = lax.axis_index("dp")
    count_copy = pltpu.make_async_copy(tiles_ref, counts_ref, sem)
    count_copy.start()

    def rows_of(row, owner, start):
        position = row_position(owner, start, ctx_count, part_rows, span_rows)
        return (
            pl.ds(row, part_rows),
            pl.ds(row + part_rows, part_rows),
            pl.ds(tile + position, part_rows),
        )

    dead = jnp.zeros((tile, head_width), jnp.bfloat16)
    keys_ref[:tile, :] = dead
    values_ref[:tile, :] = dead
    for piece, *place in moves(ctx_index, dp_index):
        key_rows, value_rows, ordered = rows_of(*place)
        keys_ref[ordered, :] = kv_refs[piece][key_rows, :]
        values_ref[ordered, :] = kv_refs[piece][value_rows, :]
    count_copy.wait()
    group = min(256, cols)
    groups = [slice(start, start + group) for start in range(0, cols, group)]

    for half in range(2):
        first = span_first(half, ctx_count, span_rows)
        query_pos = first + lax.rem(
            lax.broadcasted_iota(jnp.int32, (1, group), 1), jnp.int32(span_rows)
        )
        doc_start = starts_ref[half]
        count = counts_ref[0, half]

        def tile_rows(index):
            position = first + span_rows - (index + 1) * tile
            rows = pl.ds(pl.multiple_of(tile + position, span_rows), tile)
            return position, rows, pl.ds(pl.multiple_of(index * tile, tile), tile)

        def sums_step(index, state, diagonal=False):
            position, rows, slot = tile_rows(index)
            key_block, value_block = keys_ref[rows, :], values_ref[rows, :]
            all_logits = [
                jnp.dot(key_block, flip_ref[half, 0, :, lanes], preferred_element_type=jnp.float32)
                for lanes in groups
            ]
            all_dweights = [
                jnp.dot(
                    value_block, flip_ref[half, 1, :, lanes], preferred_element_type=jnp.float32
                )
                for lanes in groups
            ]
            following = []
            for lanes, logits, dweights, (top, total, mixed) in zip(
                groups, all_logits, all_dweights, state
            ):
                key_pos = lax.broadcasted_iota(jnp.int32, logits.shape, 0)
                live = key_pos >= doc_start[:, lanes] - position
                if diagonal:
                    live = live & (key_pos <= query_pos - position)
                logits = jnp.where(live, logits * (scale * math.log2(math.e)), masked_value)
                new_top = jnp.maximum(top, jnp.max(logits, axis=0, keepdims=True))
                terms = jnp.exp2(logits - new_top)
                terms_ref[slot, lanes] = terms
                dweights_ref[slot, lanes] = dweights
                tops_ref[pl.ds(index, 1), lanes] = new_top
                decay = jnp.exp2(top - new_top)
                following.append(
                    (
                        new_top,
                        total * decay + jnp.sum(terms, axis=0, keepdims=True),
                        mixed * decay + jnp.sum(terms * dweights, axis=0, keepdims=True),
                    )
                )
            return tuple(following)

        zero = jnp.zeros((1, group), jnp.float32)
        empty = (jnp.full_like(zero, masked_value), zero, zero)
        sums = sums_step(0, (empty,) * len(groups), diagonal=True)
        sums = lax.fori_loop(1, count, sums_step, sums)
        top, total, mixed = (jnp.concatenate(part, axis=1) for part in zip(*sums))
        inverse = 1.0 / total
        delta = mixed * inverse

        def grads_step(index, carry):
            _, rows, slot = tile_rows(index)
            factor = jnp.exp2(tops_ref[pl.ds(index, 1), :] - top) * inverse
            weights = terms_ref[slot, :] * factor
            dlogits = (weights * (dweights_ref[slot, :] - delta)).astype(jnp.bfloat16)
            for lane_block in range(cols // head_width):
                dlogits_ref[half, lane_block, slot, :] = dlogits[
                    :, lane_block * head_width : (lane_block + 1) * head_width
                ]
            acc_ref[1, rows, :] += jnp.dot(
                weights.astype(jnp.bfloat16),
                stack_ref[half, 1],
                preferred_element_type=jnp.float32,
            )
            acc_ref[0, rows, :] += jnp.dot(
                dlogits, stack_ref[half, 0], preferred_element_type=jnp.float32
            )
            return carry

        lax.fori_loop(0, count, grads_step, 0)

    for piece, *place in part_moves(
        ctx_count, dp_count, inner, part_rows, ctx_index, dp_index
    ):
        key_rows, value_rows, ordered = rows_of(*place)
        dkv_refs[piece][key_rows, :] = (scale * acc_ref[0, ordered, :]).astype(jnp.bfloat16)
        dkv_refs[piece][value_rows, :] = acc_ref[1, ordered, :].astype(jnp.bfloat16)


def query_kernel(
    ctx_count,
    tile,
    tiles_ref,
    keys_ref,
    dlogits_ref,
    passed_ref,
    dq_ref,
    same_ref,
    sum_ref,
    counts_ref,
    sem,
):
    tok_rows = dq_ref.shape[0]
    head_width = keys_ref.shape[1]
    span_rows = tok_rows // 2
    scale = head_width ** (-0.5)
    count_copy = pltpu.make_async_copy(tiles_ref, counts_ref, sem)
    count_copy.start()
    same_ref[...] = passed_ref[...]
    count_copy.wait()
    for half in range(2):
        end = span_first(half, ctx_count, span_rows) + span_rows
        sum_ref[...] = jnp.zeros_like(sum_ref)

        def query_step(index, carry):
            rows = pl.ds(pl.multiple_of(end - index * tile, span_rows), tile)
            slot = pl.ds(pl.multiple_of(index * tile, tile), tile)
            dlogits = jnp.concatenate(
                [dlogits_ref[half, block, slot, :] for block in range(dlogits_ref.shape[1])], axis=1
            )
            sum_ref[...] += jnp.dot(
                keys_ref[rows, :].T, dlogits, preferred_element_type=jnp.float32
            )
            return carry

        lax.fori_loop(0, counts_ref[0, half], query_step, 0)
        grads = (scale * sum_ref[...]).T.astype(jnp.bfloat16)
        for head in range(dq_ref.shape[1] // head_width):
            dq_ref[
                pl.ds(half * span_rows, span_rows), pl.ds(head * head_width, head_width)
            ] = grads[head * span_rows : (head + 1) * span_rows]


def prepare(ctx_count, tile, doc_lengths, queries, out_grads, head_width, line):
    tok_rows, width = queries.shape
    cols = width // head_width * (tok_rows // 2)
    unmoved = [
        pltpu.with_memory_space_constraint(argument, pltpu.HBM)
        for argument in (doc_lengths, queries, out_grads)
    ]
    return pl.pallas_call(
        functools.partial(prepare_kernel, ctx_count, tile),
        out_shape=(
            jax.ShapeDtypeStruct((2, 2, cols, head_width), jnp.bfloat16),
            jax.ShapeDtypeStruct((2, 2, head_width, cols), jnp.bfloat16),
            jax.ShapeDtypeStruct((2, 1, cols), jnp.int32),
            jax.ShapeDtypeStruct((8, 128), jnp.int32),
            jax.ShapeDtypeStruct((2, tile + ctx_count * tok_rows, head_width), jnp.float32),
            jax.ShapeDtypeStruct(line.shape, line.dtype),
        ),
        in_specs=[hbm, hbm, hbm, vmem],
        out_specs=[vmem] * 6,
        scratch_shapes=[
            pltpu.VMEM((2, tok_rows, width), jnp.bfloat16),
            pltpu.SMEM(doc_lengths.shape, jnp.int32),
            pltpu.SemaphoreType.DMA((3,)),
        ],
        compiler_params=pltpu.CompilerParams(vmem_limit_bytes=4 * 1024 * 1024),
    )(*unmoved, line)


def attend(
    ctx_count, dp_count, inner, tile, moves, tiles, starts, stacked, flipped, zeros, pieces, seq
):
    cols, head_width = stacked.shape[2:]
    slots = -(-seq // tile)
    block_rows = 2 * seq // (ctx_count * dp_count)
    away_rows = (ctx_count // inner - 1) * block_rows
    parts = [
        jax.ShapeDtypeStruct((rows, head_width), jnp.bfloat16)
        for rows in ([inner * block_rows] + [away_rows] * inner) * dp_count
    ]
    results = pl.pallas_call(
        functools.partial(
            attend_kernel, ctx_count, dp_count, inner, tile, moves, len(pieces), len(parts)
        ),
        out_shape=[
            jax.ShapeDtypeStruct((tile + seq, head_width), jnp.bfloat16),
            jax.ShapeDtypeStruct(
                (2, cols // head_width, slots * tile, head_width), jnp.bfloat16
            ),
            jax.ShapeDtypeStruct(zeros.shape, zeros.dtype),
        ]
        + parts,
        in_specs=[vmem] * (5 + len(pieces)),
        out_specs=[vmem] * (3 + len(parts)),
        scratch_shapes=[
            pltpu.VMEM((tile + seq, head_width), jnp.bfloat16),
            pltpu.VMEM((slots * tile, cols), jnp.float32),
            pltpu.VMEM((slots * tile, cols), jnp.float32),
            pltpu.VMEM((slots, cols), jnp.float32),
            pltpu.SMEM((8, 128), jnp.int32),
            pltpu.SemaphoreType.DMA,
        ],
        input_output_aliases={4: 2},
        compiler_params=pltpu.CompilerParams(vmem_limit_bytes=32 * 1024 * 1024),
    )(tiles, starts, stacked, flipped, zeros, *pieces)
    return results[0], results[1], results[3:]


def query_side(ctx_count, tile, tiles, keys_ordered, dlogits, passed, tok_rows):
    head_width = keys_ordered.shape[1]
    cols = dlogits.shape[1] * head_width
    return pl.pallas_call(
        functools.partial(query_kernel, ctx_count, tile),
        out_shape=(
            jax.ShapeDtypeStruct(
                (tok_rows, cols // (tok_rows // 2) * head_width), jnp.bfloat16
            ),
            jax.ShapeDtypeStruct(passed.shape, passed.dtype),
        ),
        in_specs=[vmem] * 4,
        out_specs=(vmem, vmem),
        scratch_shapes=[
            pltpu.VMEM((head_width, cols), jnp.float32),
            pltpu.SMEM((8, 128), jnp.int32),
            pltpu.SemaphoreType.DMA,
        ],
        compiler_params=pltpu.CompilerParams(vmem_limit_bytes=8 * 1024 * 1024),
    )(tiles, keys_ordered, dlogits, passed)


def swap(value, axis, offset):
    pairs = [(index, index ^ offset) for index in range(lax.axis_size(axis))]
    return lax.ppermute(value, axis, pairs)


def total_of(terms):
    return sum(term.astype(jnp.float32) for term in terms).astype(jnp.bfloat16)


def gather_staged(keys, values, inner, part_rows, run_prepare):
    head_width = keys.shape[1]
    outer = lax.axis_size("ctx") // inner
    start = lax.axis_index("dp") * part_rows
    own = jnp.concatenate(
        [
            lax.dynamic_slice_in_dim(keys, start, part_rows, 0),
            lax.dynamic_slice_in_dim(values, start, part_rows, 0),
        ],
        axis=0,
    )
    line = jnp.concatenate(
        [own] + [swap(own, "ctx", step * inner) for step in range(1, outer)], axis=0
    )
    plane = [line] + [swap(line, "ctx", offset) for offset in range(1, inner)]
    prepared, plane[0] = run_prepare(line)
    pieces = plane + [
        swap(piece, "dp", far) for far in range(1, lax.axis_size("dp")) for piece in plane
    ]
    return prepared, pieces


def gather_paired(keys, values, inner, part_rows, run_prepare):
    head_width = keys.shape[1]
    lowest = jnp.array(-jnp.inf, keys.dtype)
    halves = (2, 1, part_rows, head_width)
    own = jnp.maximum(
        lax.pad(keys.reshape(halves), lowest, ((0, 0, 0), (0, 1, 0), (0, 0, 0), (0, 0, 0))),
        lax.pad(values.reshape(halves), lowest, ((0, 0, 0), (1, 0, 0), (0, 0, 0), (0, 0, 0))),
    ).reshape(4 * part_rows, head_width)
    rows = 2 * part_rows
    own_half = lax.dynamic_slice_in_dim(own, lax.axis_index("dp") * rows, rows, 0)
    pairs = [
        (2 * ctx + dp, 2 * (ctx ^ ((3 if dp else 1) * inner)) + dp)
        for ctx in range(lax.axis_size("ctx"))
        for dp in range(2)
    ]
    whole = lax.ppermute(own, ("ctx", "dp"), pairs)
    away = jnp.concatenate([whole, swap(own_half, "ctx", 2 * inner)], axis=0)
    nears = [swap(own_half, "ctx", offset) for offset in range(1, inner)]
    nears, away = lax.optimization_barrier((nears, away))
    aways = [swap(away, "ctx", offset) for offset in range(1, inner)]
    nears, aways[-1] = lax.optimization_barrier((nears, aways[-1]))
    held = [jnp.concatenate(nears, axis=0), away] + aways
    prepared, held[1] = run_prepare(away)
    return prepared, [own] + held + [swap(piece, "dp", 1) for piece in held]


def body(queries, keys, values, out_grads, doc_lengths):
    ctx_count = lax.axis_size("ctx")
    dp_count = lax.axis_size("dp")
    inner = math.gcd(4, ctx_count)
    outer = ctx_count // inner
    tok_rows, head_width = keys.shape
    part_rows = tok_rows // dp_count
    seq = ctx_count * tok_rows
    tile = math.gcd(256, seq)

    def run_prepare(held):
        *prepared, held = prepare(
            ctx_count, tile, doc_lengths, queries, out_grads, head_width, held
        )
        return prepared, held

    if outer == 4 and dp_count == 2:
        gather, moves = gather_paired, functools.partial(paired_moves, inner, part_rows)
    else:
        gather = gather_staged
        moves = functools.partial(staged_moves, ctx_count, dp_count, inner, part_rows)
    (stacked, flipped, starts, tiles, zeros), pieces = gather(
        keys, values, inner, part_rows, run_prepare
    )
    keys_ordered, dlogits, parts = attend(
        ctx_count, dp_count, inner, tile, moves, tiles, starts, stacked, flipped, zeros, pieces, seq
    )
    kinds = inner + 1
    home, *plane_sums = [
        total_of(
            [parts[kind]] + [swap(parts[far * kinds + kind], "dp", far) for far in range(1, dp_count)]
        )
        for kind in range(kinds)
    ]
    query_grads, plane_sums[0] = query_side(
        ctx_count, tile, tiles, keys_ordered, dlogits, plane_sums[0], tok_rows
    )
    line_sum = total_of(
        [plane_sums[0]]
        + [swap(plane_sums[offset], "ctx", offset) for offset in reversed(range(1, inner))]
    )
    line_sum, home = lax.optimization_barrier((line_sum, home))
    blocks = jnp.split(line_sum, outer - 1, axis=0)
    home = jnp.split(home, inner, axis=0)
    kv_grads = total_of(
        [home[0]]
        + [swap(home[offset], "ctx", offset) for offset in range(1, inner)]
        + [swap(blocks[step - 1], "ctx", step * inner) for step in send_order(outer)]
    )
    return (query_grads, kv_grads[:part_rows], kv_grads[part_rows:])


def solution(mesh):
    return jax.shard_map(
        body,
        mesh=mesh,
        in_specs=(P("ctx", "dp"), P("ctx", None), P("ctx", None), P("ctx", "dp"), P()),
        out_specs=(P("ctx", "dp"), P(("ctx", "dp"), None), P(("ctx", "dp"), None)),
        check_vma=False,
    )
```

```python
import functools
import math

import jax
import jax.numpy as jnp
from jax import lax
from jax.experimental import pallas as pl
from jax.experimental.pallas import tpu as pltpu
from jax.sharding import PartitionSpec as P

masked_value = -1e30

vmem = pl.BlockSpec(memory_space=pltpu.VMEM)
smem = pl.BlockSpec(memory_space=pltpu.SMEM)
hbm = pl.BlockSpec(memory_space=pltpu.HBM)


def row_position(ctx_index, start, ctx_count, rows, span_rows):
    low = ctx_index * span_rows + start
    high = (2 * ctx_count - 1 - ctx_index) * span_rows + start - span_rows
    return pl.multiple_of(jnp.where(start < span_rows, low, high), rows)


def span_first(half, ctx_count, span_rows):
    ctx_index = lax.axis_index("ctx")
    return (ctx_index if half == 0 else 2 * ctx_count - 1 - ctx_index) * span_rows


def prepare_kernel(
    ctx_count,
    tile,
    lengths_hbm,
    q_hbm,
    g_hbm,
    line_ref,
    stack_ref,
    flip_ref,
    starts_ref,
    tiles_ref,
    zero_ref,
    same_ref,
    raw_ref,
    lengths_ref,
    sems,
):
    tok_rows = q_hbm.shape[0]
    head_width = stack_ref.shape[3]
    cols = stack_ref.shape[2]
    span_rows = tok_rows // 2
    copies = [
        pltpu.make_async_copy(source, raw_ref.at[slot], sems.at[slot])
        for slot, source in enumerate((q_hbm, g_hbm))
    ]
    for copy in copies:
        copy.start()
    lengths_copy = pltpu.make_async_copy(lengths_hbm, lengths_ref, sems.at[2])
    lengths_copy.start()
    same_ref[...] = line_ref[...]
    zero_ref[...] = jnp.zeros_like(zero_ref)
    lane = lax.broadcasted_iota(jnp.int32, tiles_ref.shape, 1)
    tiles = jnp.zeros(tiles_ref.shape, jnp.int32)
    lengths_copy.wait()
    for half in range(2):
        first = span_first(half, ctx_count, span_rows)
        query_pos = first + lax.rem(
            lax.broadcasted_iota(jnp.int32, (1, cols), 1), jnp.int32(span_rows)
        )
        doc_start = jnp.zeros((1, cols), jnp.int32)
        first_key = jnp.int32(0)
        end = jnp.int32(0)
        for doc in range(lengths_ref.shape[0]):
            end = end + lengths_ref[doc]
            doc_start = jnp.where(query_pos >= end, end, doc_start)
            first_key = jnp.where(first >= end, end, first_key)
        starts_ref[half] = doc_start
        count = (first + span_rows - first_key + tile - 1) // tile
        tiles = jnp.where(lane == half, count, tiles)
    tiles_ref[...] = tiles
    for slot, copy in enumerate(copies):
        copy.wait()
        for half in range(2):
            for head in range(q_hbm.shape[1] // head_width):
                stack_ref[half, slot, pl.ds(head * span_rows, span_rows), :] = raw_ref[
                    slot,
                    pl.ds(half * span_rows, span_rows),
                    pl.ds(head * head_width, head_width),
                ]
            flip_ref[half, slot] = stack_ref[half, slot].T


def staged_moves(ctx_count, dp_count, inner, part_rows, ctx_index, dp_index):
    for piece in range(dp_count * inner):
        for block in range(ctx_count // inner):
            owner = ctx_index ^ (piece % inner) ^ (block * inner)
            start = (dp_index ^ (piece // inner)) * part_rows
            yield piece, 2 * block * part_rows, owner, start


def paired_moves(inner, part_rows, ctx_index, dp_index):
    for side in range(2):
        holder = dp_index ^ side
        for offset in range(inner):
            piece, near = side * inner + offset, ctx_index ^ offset
            whole = near ^ jnp.where(holder == 1, 3 * inner, inner)
            yield piece, 0, near, holder * part_rows
            yield piece, 2 * part_rows, near ^ (2 * inner), holder * part_rows
            yield piece, 4 * part_rows, whole, 0
            yield piece, 6 * part_rows, whole, part_rows


def part_moves(ctx_count, dp_count, inner, part_rows, ctx_index, dp_index):
    for far in range(dp_count):
        start = (dp_index ^ far) * part_rows
        for offset in range(inner):
            near = ctx_index ^ offset
            yield far * (inner + 1), 2 * offset * part_rows, near, start
            for block in range(1, ctx_count // inner):
                piece = far * (inner + 1) + 1 + offset
                yield piece, 2 * (block - 1) * part_rows, near ^ (block * inner), start


def send_order(outer):
    return (3, 1, 2) if outer == 4 else tuple(reversed(range(1, outer)))


def attend_kernel(
    ctx_count,
    dp_count,
    inner,
    tile,
    moves,
    piece_count,
    part_count,
    tiles_ref,
    starts_ref,
    stack_ref,
    flip_ref,
    _,
    *refs,
):
    kv_refs = refs[:piece_count]
    refs = refs[piece_count:]
    keys_ref, dlogits_ref, acc_ref = refs[:3]
    dkv_refs = refs[3 : part_count + 3]
    values_ref, terms_ref, dweights_ref, tops_ref, counts_ref, sem = refs[part_count + 3 :]
    cols, head_width = stack_ref.shape[2:]
    tok_rows = (keys_ref.shape[0] - tile) // ctx_count
    part_rows = tok_rows // dp_count
    span_rows = tok_rows // 2
    scale = head_width ** (-0.5)
    ctx_index = lax.axis_index("ctx")
    dp_index = lax.axis_index("dp")
    count_copy = pltpu.make_async_copy(tiles_ref, counts_ref, sem)
    count_copy.start()

    def rows_of(row, owner, start):
        position = row_position(owner, start, ctx_count, part_rows, span_rows)
        return (
            pl.ds(row, part_rows),
            pl.ds(row + part_rows, part_rows),
            pl.ds(tile + position, part_rows),
        )

    dead = jnp.zeros((tile, head_width), jnp.bfloat16)
    keys_ref[:tile, :] = dead
    values_ref[:tile, :] = dead
    for piece, *place in moves(ctx_index, dp_index):
        key_rows, value_rows, ordered = rows_of(*place)
        keys_ref[ordered, :] = kv_refs[piece][key_rows, :]
        values_ref[ordered, :] = kv_refs[piece][value_rows, :]
    count_copy.wait()
    group = min(256, cols)
    groups = [slice(start, start + group) for start in range(0, cols, group)]

    for half in range(2):
        first = span_first(half, ctx_count, span_rows)
        query_pos = first + lax.rem(
            lax.broadcasted_iota(jnp.int32, (1, group), 1), jnp.int32(span_rows)
        )
        doc_start = starts_ref[half]
        count = counts_ref[0, half]

        def tile_rows(index):
            position = first + span_rows - (index + 1) * tile
            rows = pl.ds(pl.multiple_of(tile + position, span_rows), tile)
            return position, rows, pl.ds(pl.multiple_of(index * tile, tile), tile)

        def sums_step(index, state, diagonal=False):
            position, rows, slot = tile_rows(index)
            key_block, value_block = keys_ref[rows, :], values_ref[rows, :]
            all_logits = [
                jnp.dot(key_block, flip_ref[half, 0, :, lanes], preferred_element_type=jnp.float32)
                for lanes in groups
            ]
            all_dweights = [
                jnp.dot(
                    value_block, flip_ref[half, 1, :, lanes], preferred_element_type=jnp.float32
                )
                for lanes in groups
            ]
            following = []
            for lanes, logits, dweights, (top, total, mixed) in zip(
                groups, all_logits, all_dweights, state
            ):
                key_pos = lax.broadcasted_iota(jnp.int32, logits.shape, 0)
                live = key_pos >= doc_start[:, lanes] - position
                if diagonal:
                    live = live & (key_pos <= query_pos - position)
                logits = jnp.where(live, logits * (scale * math.log2(math.e)), masked_value)
                new_top = jnp.maximum(top, jnp.max(logits, axis=0, keepdims=True))
                terms = jnp.exp2(logits - new_top)
                terms_ref[slot, lanes] = terms
                dweights_ref[slot, lanes] = dweights
                tops_ref[pl.ds(index, 1), lanes] = new_top
                decay = jnp.exp2(top - new_top)
                following.append(
                    (
                        new_top,
                        total * decay + jnp.sum(terms, axis=0, keepdims=True),
                        mixed * decay + jnp.sum(terms * dweights, axis=0, keepdims=True),
                    )
                )
            return tuple(following)

        zero = jnp.zeros((1, group), jnp.float32)
        empty = (jnp.full_like(zero, masked_value), zero, zero)
        sums = sums_step(0, (empty,) * len(groups), diagonal=True)
        sums = lax.fori_loop(1, count, sums_step, sums)
        top, total, mixed = (jnp.concatenate(part, axis=1) for part in zip(*sums))
        inverse = 1.0 / total
        delta = mixed * inverse

        def grads_step(index, carry):
            _, rows, slot = tile_rows(index)
            factor = jnp.exp2(tops_ref[pl.ds(index, 1), :] - top) * inverse
            weights = terms_ref[slot, :] * factor
            dlogits = (weights * (dweights_ref[slot, :] - delta)).astype(jnp.bfloat16)
            for lane_block in range(cols // head_width):
                dlogits_ref[half, lane_block, slot, :] = dlogits[
                    :, lane_block * head_width : (lane_block + 1) * head_width
                ]
            acc_ref[1, rows, :] += jnp.dot(
                weights.astype(jnp.bfloat16),
                stack_ref[half, 1],
                preferred_element_type=jnp.float32,
            )
            acc_ref[0, rows, :] += jnp.dot(
                dlogits, stack_ref[half, 0], preferred_element_type=jnp.float32
            )
            return carry

        lax.fori_loop(0, count, grads_step, 0)

    for piece, *place in part_moves(
        ctx_count, dp_count, inner, part_rows, ctx_index, dp_index
    ):
        key_rows, value_rows, ordered = rows_of(*place)
        dkv_refs[piece][key_rows, :] = (scale * acc_ref[0, ordered, :]).astype(jnp.bfloat16)
        dkv_refs[piece][value_rows, :] = acc_ref[1, ordered, :].astype(jnp.bfloat16)


def query_kernel(
    ctx_count,
    tile,
    tiles_ref,
    keys_ref,
    dlogits_ref,
    passed_ref,
    dq_ref,
    same_ref,
    sum_ref,
    counts_ref,
    sem,
):
    tok_rows = dq_ref.shape[0]
    head_width = keys_ref.shape[1]
    span_rows = tok_rows // 2
    scale = head_width ** (-0.5)
    count_copy = pltpu.make_async_copy(tiles_ref, counts_ref, sem)
    count_copy.start()
    same_ref[...] = passed_ref[...]
    count_copy.wait()
    for half in range(2):
        end = span_first(half, ctx_count, span_rows) + span_rows
        sum_ref[...] = jnp.zeros_like(sum_ref)

        def query_step(index, carry):
            rows = pl.ds(pl.multiple_of(end - index * tile, span_rows), tile)
            slot = pl.ds(pl.multiple_of(index * tile, tile), tile)
            dlogits = jnp.concatenate(
                [dlogits_ref[half, block, slot, :] for block in range(dlogits_ref.shape[1])], axis=1
            )
            sum_ref[...] += jnp.dot(
                keys_ref[rows, :].T, dlogits, preferred_element_type=jnp.float32
            )
            return carry

        lax.fori_loop(0, counts_ref[0, half], query_step, 0)
        grads = (scale * sum_ref[...]).T.astype(jnp.bfloat16)
        for head in range(dq_ref.shape[1] // head_width):
            dq_ref[
                pl.ds(half * span_rows, span_rows), pl.ds(head * head_width, head_width)
            ] = grads[head * span_rows : (head + 1) * span_rows]


def prepare(ctx_count, tile, doc_lengths, queries, out_grads, head_width, line):
    tok_rows, width = queries.shape
    cols = width // head_width * (tok_rows // 2)
    unmoved = [
        pltpu.with_memory_space_constraint(argument, pltpu.HBM)
        for argument in (doc_lengths, queries, out_grads)
    ]
    return pl.pallas_call(
        functools.partial(prepare_kernel, ctx_count, tile),
        out_shape=(
            jax.ShapeDtypeStruct((2, 2, cols, head_width), jnp.bfloat16),
            jax.ShapeDtypeStruct((2, 2, head_width, cols), jnp.bfloat16),
            jax.ShapeDtypeStruct((2, 1, cols), jnp.int32),
            jax.ShapeDtypeStruct((8, 128), jnp.int32),
            jax.ShapeDtypeStruct((2, tile + ctx_count * tok_rows, head_width), jnp.float32),
            jax.ShapeDtypeStruct(line.shape, line.dtype),
        ),
        in_specs=[hbm, hbm, hbm, vmem],
        out_specs=[vmem] * 6,
        scratch_shapes=[
            pltpu.VMEM((2, tok_rows, width), jnp.bfloat16),
            pltpu.SMEM(doc_lengths.shape, jnp.int32),
            pltpu.SemaphoreType.DMA((3,)),
        ],
        compiler_params=pltpu.CompilerParams(vmem_limit_bytes=4 * 1024 * 1024),
    )(*unmoved, line)


def attend(
    ctx_count, dp_count, inner, tile, moves, tiles, starts, stacked, flipped, zeros, pieces, seq
):
    cols, head_width = stacked.shape[2:]
    slots = -(-seq // tile)
    block_rows = 2 * seq // (ctx_count * dp_count)
    away_rows = (ctx_count // inner - 1) * block_rows
    parts = [
        jax.ShapeDtypeStruct((rows, head_width), jnp.bfloat16)
        for rows in ([inner * block_rows] + [away_rows] * inner) * dp_count
    ]
    results = pl.pallas_call(
        functools.partial(
            attend_kernel, ctx_count, dp_count, inner, tile, moves, len(pieces), len(parts)
        ),
        out_shape=[
            jax.ShapeDtypeStruct((tile + seq, head_width), jnp.bfloat16),
            jax.ShapeDtypeStruct(
                (2, cols // head_width, slots * tile, head_width), jnp.bfloat16
            ),
            jax.ShapeDtypeStruct(zeros.shape, zeros.dtype),
        ]
        + parts,
        in_specs=[vmem] * (5 + len(pieces)),
        out_specs=[vmem] * (3 + len(parts)),
        scratch_shapes=[
            pltpu.VMEM((tile + seq, head_width), jnp.bfloat16),
            pltpu.VMEM((slots * tile, cols), jnp.float32),
            pltpu.VMEM((slots * tile, cols), jnp.float32),
            pltpu.VMEM((slots, cols), jnp.float32),
            pltpu.SMEM((8, 128), jnp.int32),
            pltpu.SemaphoreType.DMA,
        ],
        input_output_aliases={4: 2},
        compiler_params=pltpu.CompilerParams(vmem_limit_bytes=32 * 1024 * 1024),
    )(tiles, starts, stacked, flipped, zeros, *pieces)
    return results[0], results[1], results[3:]


def query_side(ctx_count, tile, tiles, keys_ordered, dlogits, passed, tok_rows):
    head_width = keys_ordered.shape[1]
    cols = dlogits.shape[1] * head_width
    return pl.pallas_call(
        functools.partial(query_kernel, ctx_count, tile),
        out_shape=(
            jax.ShapeDtypeStruct(
                (tok_rows, cols // (tok_rows // 2) * head_width), jnp.bfloat16
            ),
            jax.ShapeDtypeStruct(passed.shape, passed.dtype),
        ),
        in_specs=[vmem] * 4,
        out_specs=(vmem, vmem),
        scratch_shapes=[
            pltpu.VMEM((head_width, cols), jnp.float32),
            pltpu.SMEM((8, 128), jnp.int32),
            pltpu.SemaphoreType.DMA,
        ],
        compiler_params=pltpu.CompilerParams(vmem_limit_bytes=8 * 1024 * 1024),
    )(tiles, keys_ordered, dlogits, passed)


def swap(value, axis, offset):
    pairs = [(index, index ^ offset) for index in range(lax.axis_size(axis))]
    return lax.ppermute(value, axis, pairs)


def total_of(terms):
    return sum(term.astype(jnp.float32) for term in terms).astype(jnp.bfloat16)


def gather_staged(keys, values, inner, part_rows, run_prepare):
    head_width = keys.shape[1]
    outer = lax.axis_size("ctx") // inner
    start = lax.axis_index("dp") * part_rows
    own = jnp.concatenate(
        [
            lax.dynamic_slice_in_dim(keys, start, part_rows, 0),
            lax.dynamic_slice_in_dim(values, start, part_rows, 0),
        ],
        axis=0,
    )
    line = jnp.concatenate(
        [own] + [swap(own, "ctx", step * inner) for step in range(1, outer)], axis=0
    )
    plane = [line] + [swap(line, "ctx", offset) for offset in range(1, inner)]
    prepared, plane[0] = run_prepare(line)
    pieces = plane + [
        swap(piece, "dp", far) for far in range(1, lax.axis_size("dp")) for piece in plane
    ]
    return prepared, pieces


def gather_paired(keys, values, inner, part_rows, run_prepare):
    head_width = keys.shape[1]
    lowest = jnp.array(-jnp.inf, keys.dtype)
    halves = (2, 1, part_rows, head_width)
    own = jnp.maximum(
        lax.pad(keys.reshape(halves), lowest, ((0, 0, 0), (0, 1, 0), (0, 0, 0), (0, 0, 0))),
        lax.pad(values.reshape(halves), lowest, ((0, 0, 0), (1, 0, 0), (0, 0, 0), (0, 0, 0))),
    ).reshape(4 * part_rows, head_width)
    rows = 2 * part_rows
    own_half = lax.dynamic_slice_in_dim(own, lax.axis_index("dp") * rows, rows, 0)
    pairs = [
        (2 * ctx + dp, 2 * (ctx ^ ((3 if dp else 1) * inner)) + dp)
        for ctx in range(lax.axis_size("ctx"))
        for dp in range(2)
    ]
    whole = lax.ppermute(own, ("ctx", "dp"), pairs)
    line = jnp.concatenate([own_half, swap(own_half, "ctx", 2 * inner), whole], axis=0)
    plane = [line] + [swap(line, "ctx", offset) for offset in range(1, inner)]
    prepared, plane[0] = run_prepare(line)
    return prepared, plane + [swap(piece, "dp", 1) for piece in plane]


def body(queries, keys, values, out_grads, doc_lengths):
    ctx_count = lax.axis_size("ctx")
    dp_count = lax.axis_size("dp")
    inner = math.gcd(4, ctx_count)
    outer = ctx_count // inner
    tok_rows, head_width = keys.shape
    part_rows = tok_rows // dp_count
    seq = ctx_count * tok_rows
    tile = math.gcd(256, seq)

    def run_prepare(held):
        *prepared, held = prepare(
            ctx_count, tile, doc_lengths, queries, out_grads, head_width, held
        )
        return prepared, held

    if outer == 4 and dp_count == 2:
        gather, moves = gather_paired, functools.partial(paired_moves, inner, part_rows)
    else:
        gather = gather_staged
        moves = functools.partial(staged_moves, ctx_count, dp_count, inner, part_rows)
    (stacked, flipped, starts, tiles, zeros), pieces = gather(
        keys, values, inner, part_rows, run_prepare
    )
    keys_ordered, dlogits, parts = attend(
        ctx_count, dp_count, inner, tile, moves, tiles, starts, stacked, flipped, zeros, pieces, seq
    )
    kinds = inner + 1
    home, *plane_sums = [
        total_of(
            [parts[kind]] + [swap(parts[far * kinds + kind], "dp", far) for far in range(1, dp_count)]
        )
        for kind in range(kinds)
    ]
    query_grads, plane_sums[0] = query_side(
        ctx_count, tile, tiles, keys_ordered, dlogits, plane_sums[0], tok_rows
    )
    plane_sums[0], home = lax.optimization_barrier((plane_sums[0], home))
    line_sum = total_of(
        [plane_sums[0]]
        + [swap(plane_sums[offset], "ctx", offset) for offset in reversed(range(1, inner))]
    )
    blocks = jnp.split(line_sum, outer - 1, axis=0)
    home = jnp.split(home, inner, axis=0)
    kv_grads = total_of(
        [home[0]]
        + [swap(home[offset], "ctx", offset) for offset in range(1, inner)]
        + [swap(blocks[step - 1], "ctx", step * inner) for step in send_order(outer)]
    )
    return (query_grads, kv_grads[:part_rows], kv_grads[part_rows:])


def solution(mesh):
    return jax.shard_map(
        body,
        mesh=mesh,
        in_specs=(P("ctx", "dp"), P("ctx", None), P("ctx", None), P("ctx", "dp"), P()),
        out_specs=(P("ctx", "dp"), P(("ctx", "dp"), None), P(("ctx", "dp"), None)),
        check_vma=False,
    )
```

```python
import functools
import math

import jax
import jax.numpy as jnp
from jax import lax
from jax.experimental import pallas as pl
from jax.experimental.pallas import tpu as pltpu
from jax.sharding import PartitionSpec as P

masked_value = -1e30

vmem = pl.BlockSpec(memory_space=pltpu.VMEM)
smem = pl.BlockSpec(memory_space=pltpu.SMEM)
hbm = pl.BlockSpec(memory_space=pltpu.HBM)


def row_position(ctx_index, start, ctx_count, rows, span_rows):
    low = ctx_index * span_rows + start
    high = (2 * ctx_count - 1 - ctx_index) * span_rows + start - span_rows
    return pl.multiple_of(jnp.where(start < span_rows, low, high), rows)


def span_first(half, ctx_count, span_rows):
    ctx_index = lax.axis_index("ctx")
    return (ctx_index if half == 0 else 2 * ctx_count - 1 - ctx_index) * span_rows


def tile_count(tiles_ref, half):
    return jnp.max(tiles_ref[half]).astype(jnp.int32)


def prepare_kernel(
    ctx_count,
    tile,
    lengths_hbm,
    q_hbm,
    g_hbm,
    line_ref,
    stack_ref,
    flip_ref,
    starts_ref,
    tiles_ref,
    zero_ref,
    same_ref,
    raw_ref,
    lengths_ref,
    sems,
):
    tok_rows = q_hbm.shape[0]
    head_width = stack_ref.shape[3]
    cols = stack_ref.shape[2]
    span_rows = tok_rows // 2
    copies = [
        pltpu.make_async_copy(source, raw_ref.at[slot], sems.at[slot])
        for slot, source in enumerate((q_hbm, g_hbm))
    ]
    for copy in copies:
        copy.start()
    lengths_copy = pltpu.make_async_copy(lengths_hbm, lengths_ref, sems.at[2])
    lengths_copy.start()
    same_ref[...] = line_ref[...]
    zero_ref[...] = jnp.zeros_like(zero_ref)
    lengths_copy.wait()
    for half in range(2):
        first = span_first(half, ctx_count, span_rows)
        query_pos = first + lax.rem(
            lax.broadcasted_iota(jnp.int32, (1, cols), 1), jnp.int32(span_rows)
        )
        doc_start = jnp.zeros((1, cols), jnp.int32)
        first_key = jnp.int32(0)
        end = jnp.int32(0)
        for doc in range(lengths_ref.shape[0]):
            end = end + lengths_ref[doc]
            doc_start = jnp.where(query_pos >= end, end, doc_start)
            first_key = jnp.where(first >= end, end, first_key)
        starts_ref[half] = doc_start
        count = (first + span_rows - first_key + tile - 1) // tile
        tiles_ref[half] = jnp.full(tiles_ref.shape[1:], count.astype(jnp.float32))
    for slot, copy in enumerate(copies):
        copy.wait()
        for half in range(2):
            for head in range(q_hbm.shape[1] // head_width):
                stack_ref[half, slot, pl.ds(head * span_rows, span_rows), :] = raw_ref[
                    slot,
                    pl.ds(half * span_rows, span_rows),
                    pl.ds(head * head_width, head_width),
                ]
            flip_ref[half, slot] = stack_ref[half, slot].T


def staged_moves(ctx_count, dp_count, inner, part_rows, ctx_index, dp_index):
    for piece in range(dp_count * inner):
        for block in range(ctx_count // inner):
            owner = ctx_index ^ (piece % inner) ^ (block * inner)
            start = (dp_index ^ (piece // inner)) * part_rows
            yield piece, 2 * block * part_rows, owner, start


def paired_moves(inner, part_rows, ctx_index, dp_index):
    for side in range(2):
        holder = dp_index ^ side
        for offset in range(inner):
            piece, near = side * inner + offset, ctx_index ^ offset
            whole = near ^ jnp.where(holder == 1, 3 * inner, inner)
            yield piece, 0, near, holder * part_rows
            yield piece, 2 * part_rows, near ^ (2 * inner), holder * part_rows
            yield piece, 4 * part_rows, whole, 0
            yield piece, 6 * part_rows, whole, part_rows


def send_order(outer):
    return (3, 1, 2) if outer == 4 else tuple(reversed(range(1, outer)))


def attend_kernel(
    ctx_count, dp_count, inner, tile, moves, tiles_ref, starts_ref, stack_ref, flip_ref, _, *refs
):
    piece_count = dp_count * inner
    kv_refs = refs[:piece_count]
    refs = refs[piece_count:]
    keys_ref, dlogits_ref, acc_ref = refs[:3]
    dkv_refs = refs[3 : piece_count + 3]
    values_ref, terms_ref, dweights_ref, tops_ref = refs[piece_count + 3 :]
    cols, head_width = stack_ref.shape[2:]
    tok_rows = (keys_ref.shape[0] - tile) // ctx_count
    part_rows = tok_rows // dp_count
    span_rows = tok_rows // 2
    scale = head_width ** (-0.5)
    ctx_index = lax.axis_index("ctx")
    dp_index = lax.axis_index("dp")

    def rows_of(row, owner, start):
        position = row_position(owner, start, ctx_count, part_rows, span_rows)
        return (
            pl.ds(row, part_rows),
            pl.ds(row + part_rows, part_rows),
            pl.ds(tile + position, part_rows),
        )

    dead = jnp.zeros((tile, head_width), jnp.bfloat16)
    keys_ref[:tile, :] = dead
    values_ref[:tile, :] = dead
    for piece, *place in moves(ctx_index, dp_index):
        key_rows, value_rows, ordered = rows_of(*place)
        keys_ref[ordered, :] = kv_refs[piece][key_rows, :]
        values_ref[ordered, :] = kv_refs[piece][value_rows, :]
    group = min(256, cols)
    groups = [slice(start, start + group) for start in range(0, cols, group)]

    for half in range(2):
        first = span_first(half, ctx_count, span_rows)
        query_pos = first + lax.rem(
            lax.broadcasted_iota(jnp.int32, (1, group), 1), jnp.int32(span_rows)
        )
        doc_start = starts_ref[half]
        count = tile_count(tiles_ref, half)

        def tile_rows(index):
            position = first + span_rows - (index + 1) * tile
            rows = pl.ds(pl.multiple_of(tile + position, span_rows), tile)
            return position, rows, pl.ds(pl.multiple_of(index * tile, tile), tile)

        def sums_step(index, state):
            position, rows, slot = tile_rows(index)
            key_block, value_block = keys_ref[rows, :], values_ref[rows, :]
            all_logits = [
                jnp.dot(key_block, flip_ref[half, 0, :, lanes], preferred_element_type=jnp.float32)
                for lanes in groups
            ]
            all_dweights = [
                jnp.dot(
                    value_block, flip_ref[half, 1, :, lanes], preferred_element_type=jnp.float32
                )
                for lanes in groups
            ]
            following = []
            for lanes, logits, dweights, (top, total, mixed) in zip(
                groups, all_logits, all_dweights, state
            ):
                key_pos = lax.broadcasted_iota(jnp.int32, logits.shape, 0)
                live = (key_pos >= doc_start[:, lanes] - position) & (
                    key_pos <= query_pos - position
                )
                logits = jnp.where(live, logits * (scale * math.log2(math.e)), masked_value)
                new_top = jnp.maximum(top, jnp.max(logits, axis=0, keepdims=True))
                terms = jnp.exp2(logits - new_top)
                terms_ref[slot, lanes] = terms
                dweights_ref[slot, lanes] = dweights
                tops_ref[pl.ds(index, 1), lanes] = new_top
                decay = jnp.exp2(top - new_top)
                following.append(
                    (
                        new_top,
                        total * decay + jnp.sum(terms, axis=0, keepdims=True),
                        mixed * decay + jnp.sum(terms * dweights, axis=0, keepdims=True),
                    )
                )
            return tuple(following)

        zero = jnp.zeros((1, group), jnp.float32)
        empty = (jnp.full_like(zero, masked_value), zero, zero)
        sums = lax.fori_loop(0, count, sums_step, (empty,) * len(groups))
        top, total, mixed = (jnp.concatenate(part, axis=1) for part in zip(*sums))
        inverse = 1.0 / total
        delta = mixed * inverse

        def grads_step(index, carry):
            _, rows, slot = tile_rows(index)
            factor = jnp.exp2(tops_ref[pl.ds(index, 1), :] - top) * inverse
            weights = terms_ref[slot, :] * factor
            dlogits = (weights * (dweights_ref[slot, :] - delta)).astype(jnp.bfloat16)
            for lane_block in range(cols // head_width):
                dlogits_ref[half, lane_block, slot, :] = dlogits[
                    :, lane_block * head_width : (lane_block + 1) * head_width
                ]
            acc_ref[1, rows, :] += jnp.dot(
                weights.astype(jnp.bfloat16),
                stack_ref[half, 1],
                preferred_element_type=jnp.float32,
            )
            acc_ref[0, rows, :] += jnp.dot(
                dlogits, stack_ref[half, 0], preferred_element_type=jnp.float32
            )
            return carry

        lax.fori_loop(0, count, grads_step, 0)

    for piece, *place in staged_moves(
        ctx_count, dp_count, inner, part_rows, ctx_index, dp_index
    ):
        key_rows, value_rows, ordered = rows_of(*place)
        dkv_refs[piece][key_rows, :] = (scale * acc_ref[0, ordered, :]).astype(jnp.bfloat16)
        dkv_refs[piece][value_rows, :] = acc_ref[1, ordered, :].astype(jnp.bfloat16)


def query_kernel(
    ctx_count,
    tile,
    tiles_ref,
    keys_ref,
    dlogits_ref,
    passed_ref,
    dq_ref,
    same_ref,
    sum_ref,
):
    tok_rows = dq_ref.shape[0]
    head_width = keys_ref.shape[1]
    span_rows = tok_rows // 2
    scale = head_width ** (-0.5)
    same_ref[...] = passed_ref[...]
    for half in range(2):
        end = span_first(half, ctx_count, span_rows) + span_rows
        sum_ref[...] = jnp.zeros_like(sum_ref)

        def query_step(index, carry):
            rows = pl.ds(pl.multiple_of(end - index * tile, span_rows), tile)
            slot = pl.ds(pl.multiple_of(index * tile, tile), tile)
            dlogits = jnp.concatenate(
                [dlogits_ref[half, block, slot, :] for block in range(dlogits_ref.shape[1])], axis=1
            )
            sum_ref[...] += jnp.dot(
                keys_ref[rows, :].T, dlogits, preferred_element_type=jnp.float32
            )
            return carry

        lax.fori_loop(0, tile_count(tiles_ref, half), query_step, 0)
        grads = (scale * sum_ref[...]).T.astype(jnp.bfloat16)
        for head in range(dq_ref.shape[1] // head_width):
            dq_ref[
                pl.ds(half * span_rows, span_rows), pl.ds(head * head_width, head_width)
            ] = grads[head * span_rows : (head + 1) * span_rows]


def prepare(ctx_count, tile, doc_lengths, queries, out_grads, head_width, line):
    tok_rows, width = queries.shape
    cols = width // head_width * (tok_rows // 2)
    unmoved = [
        pltpu.with_memory_space_constraint(argument, pltpu.HBM)
        for argument in (doc_lengths, queries, out_grads)
    ]
    return pl.pallas_call(
        functools.partial(prepare_kernel, ctx_count, tile),
        out_shape=(
            jax.ShapeDtypeStruct((2, 2, cols, head_width), jnp.bfloat16),
            jax.ShapeDtypeStruct((2, 2, head_width, cols), jnp.bfloat16),
            jax.ShapeDtypeStruct((2, 1, cols), jnp.int32),
            jax.ShapeDtypeStruct((2, 8, 128), jnp.float32),
            jax.ShapeDtypeStruct((2, tile + ctx_count * tok_rows, head_width), jnp.float32),
            jax.ShapeDtypeStruct(line.shape, line.dtype),
        ),
        in_specs=[hbm, hbm, hbm, vmem],
        out_specs=[vmem] * 6,
        scratch_shapes=[
            pltpu.VMEM((2, tok_rows, width), jnp.bfloat16),
            pltpu.SMEM(doc_lengths.shape, jnp.int32),
            pltpu.SemaphoreType.DMA((3,)),
        ],
        compiler_params=pltpu.CompilerParams(vmem_limit_bytes=4 * 1024 * 1024),
    )(*unmoved, line)


def attend(ctx_count, dp_count, inner, tile, moves, tiles, starts, stacked, flipped, zeros, pieces):
    cols, head_width = stacked.shape[2:]
    seq = dp_count * inner * pieces[0].shape[0] // 2
    slots = -(-seq // tile)
    results = pl.pallas_call(
        functools.partial(attend_kernel, ctx_count, dp_count, inner, tile, moves),
        out_shape=[
            jax.ShapeDtypeStruct((tile + seq, head_width), jnp.bfloat16),
            jax.ShapeDtypeStruct(
                (2, cols // head_width, slots * tile, head_width), jnp.bfloat16
            ),
            jax.ShapeDtypeStruct(zeros.shape, zeros.dtype),
        ]
        + [jax.ShapeDtypeStruct(piece.shape, jnp.bfloat16) for piece in pieces],
        in_specs=[vmem] * (5 + len(pieces)),
        out_specs=[vmem] * (3 + len(pieces)),
        scratch_shapes=[
            pltpu.VMEM((tile + seq, head_width), jnp.bfloat16),
            pltpu.VMEM((slots * tile, cols), jnp.float32),
            pltpu.VMEM((slots * tile, cols), jnp.float32),
            pltpu.VMEM((slots, cols), jnp.float32),
        ],
        input_output_aliases={4: 2},
        compiler_params=pltpu.CompilerParams(vmem_limit_bytes=32 * 1024 * 1024),
    )(tiles, starts, stacked, flipped, zeros, *pieces)
    return results[0], results[1], results[3:]


def query_side(ctx_count, tile, tiles, keys_ordered, dlogits, passed, tok_rows):
    head_width = keys_ordered.shape[1]
    cols = dlogits.shape[1] * head_width
    return pl.pallas_call(
        functools.partial(query_kernel, ctx_count, tile),
        out_shape=(
            jax.ShapeDtypeStruct(
                (tok_rows, cols // (tok_rows // 2) * head_width), jnp.bfloat16
            ),
            jax.ShapeDtypeStruct(passed.shape, passed.dtype),
        ),
        in_specs=[vmem] * 4,
        out_specs=(vmem, vmem),
        scratch_shapes=[
            pltpu.VMEM((head_width, cols), jnp.float32),
        ],
        compiler_params=pltpu.CompilerParams(vmem_limit_bytes=8 * 1024 * 1024),
    )(tiles, keys_ordered, dlogits, passed)


def swap(value, axis, offset):
    pairs = [(index, index ^ offset) for index in range(lax.axis_size(axis))]
    return lax.ppermute(value, axis, pairs)


def total_of(terms):
    return sum(term.astype(jnp.float32) for term in terms).astype(jnp.bfloat16)


def staged_line(keys, values, inner, part_rows):
    head_width = keys.shape[1]
    outer = lax.axis_size("ctx") // inner
    start = lax.axis_index("dp") * part_rows
    own_keys = lax.dynamic_slice_in_dim(keys, start, part_rows, 0)
    own_values = lax.dynamic_slice_in_dim(values, start, part_rows, 0)
    zero = jnp.zeros((), keys.dtype)
    own = jnp.where(
        lax.broadcasted_iota(jnp.int32, (2 * part_rows, head_width), 0) < part_rows,
        lax.pad(own_keys, zero, ((0, part_rows, 0), (0, 0, 0))),
        lax.pad(own_values, zero, ((part_rows, 0, 0), (0, 0, 0))),
    )
    others = [swap(own, "ctx", step * inner) for step in range(1, outer)]
    return jnp.concatenate([own] + others, axis=0)


def paired_line(keys, values, inner, part_rows):
    head_width = keys.shape[1]
    lowest = jnp.array(-jnp.inf, keys.dtype)
    halves = (2, 1, part_rows, head_width)
    own = jnp.maximum(
        lax.pad(keys.reshape(halves), lowest, ((0, 0, 0), (0, 1, 0), (0, 0, 0), (0, 0, 0))),
        lax.pad(values.reshape(halves), lowest, ((0, 0, 0), (1, 0, 0), (0, 0, 0), (0, 0, 0))),
    ).reshape(4 * part_rows, head_width)
    rows = 2 * part_rows
    own_half = lax.dynamic_slice_in_dim(own, lax.axis_index("dp") * rows, rows, 0)
    pairs = [
        (2 * ctx + dp, 2 * (ctx ^ ((3 if dp else 1) * inner)) + dp)
        for ctx in range(lax.axis_size("ctx"))
        for dp in range(2)
    ]
    whole = lax.ppermute(own, ("ctx", "dp"), pairs)
    return jnp.concatenate([own_half, swap(own_half, "ctx", 2 * inner), whole], axis=0)


def body(queries, keys, values, out_grads, doc_lengths):
    ctx_count = lax.axis_size("ctx")
    dp_count = lax.axis_size("dp")
    inner = math.gcd(4, ctx_count)
    outer = ctx_count // inner
    tok_rows, head_width = keys.shape
    part_rows = tok_rows // dp_count
    tile = math.gcd(256, ctx_count * tok_rows)
    if outer == 4 and dp_count == 2:
        line = paired_line(keys, values, inner, part_rows)
        moves = functools.partial(paired_moves, inner, part_rows)
    else:
        line = staged_line(keys, values, inner, part_rows)
        moves = functools.partial(staged_moves, ctx_count, dp_count, inner, part_rows)
    plane = [line] + [swap(line, "ctx", offset) for offset in range(1, inner)]
    stacked, flipped, starts, tiles, zeros, plane[0] = prepare(
        ctx_count, tile, doc_lengths, queries, out_grads, head_width, line
    )
    pieces = plane + [
        swap(piece, "dp", offset) for offset in range(1, dp_count) for piece in plane
    ]
    keys_ordered, dlogits, parts = attend(
        ctx_count, dp_count, inner, tile, moves, tiles, starts, stacked, flipped, zeros, pieces
    )
    plane_sums = [
        total_of(
            [parts[offset]]
            + [swap(parts[far * inner + offset], "dp", far) for far in range(1, dp_count)]
        )
        for offset in range(inner)
    ]
    query_grads, plane_sums[0] = query_side(
        ctx_count, tile, tiles, keys_ordered, dlogits, plane_sums[0], tok_rows
    )
    line_sum = total_of(
        [plane_sums[0]] + [swap(plane_sums[offset], "ctx", offset) for offset in reversed(range(1, inner))]
    )
    blocks = jnp.split(line_sum, outer, axis=0)
    kv_grads = total_of(
        [blocks[0]] + [swap(blocks[block], "ctx", block * inner) for block in send_order(outer)]
    )
    return (query_grads, kv_grads[:part_rows], kv_grads[part_rows:])


def solution(mesh):
    return jax.shard_map(
        body,
        mesh=mesh,
        in_specs=(P("ctx", "dp"), P("ctx", None), P("ctx", None), P("ctx", "dp"), P()),
        out_specs=(P("ctx", "dp"), P(("ctx", "dp"), None), P(("ctx", "dp"), None)),
        check_vma=False,
    )
```

```python
import functools
import math

import jax
import jax.numpy as jnp
from jax import lax
from jax.experimental import pallas as pl
from jax.experimental.pallas import tpu as pltpu
from jax.sharding import PartitionSpec as P

masked_value = -1e30

vmem = pl.BlockSpec(memory_space=pltpu.VMEM)
smem = pl.BlockSpec(memory_space=pltpu.SMEM)
hbm = pl.BlockSpec(memory_space=pltpu.HBM)


def row_position(ctx_index, start, ctx_count, rows, span_rows):
    low = ctx_index * span_rows + start
    high = (2 * ctx_count - 1 - ctx_index) * span_rows + start - span_rows
    return pl.multiple_of(jnp.where(start < span_rows, low, high), rows)


def span_first(half, ctx_count, span_rows):
    ctx_index = lax.axis_index("ctx")
    return (ctx_index if half == 0 else 2 * ctx_count - 1 - ctx_index) * span_rows


def tile_count(tiles_ref, half):
    return jnp.max(tiles_ref[half]).astype(jnp.int32)


def prepare_kernel(
    ctx_count,
    tile,
    lengths_hbm,
    q_hbm,
    g_hbm,
    line_ref,
    stack_ref,
    flip_ref,
    starts_ref,
    tiles_ref,
    zero_ref,
    same_ref,
    raw_ref,
    lengths_ref,
    sems,
):
    tok_rows = q_hbm.shape[0]
    head_width = stack_ref.shape[3]
    cols = stack_ref.shape[2]
    span_rows = tok_rows // 2
    copies = [
        pltpu.make_async_copy(source, raw_ref.at[slot], sems.at[slot])
        for slot, source in enumerate((q_hbm, g_hbm))
    ]
    for copy in copies:
        copy.start()
    lengths_copy = pltpu.make_async_copy(lengths_hbm, lengths_ref, sems.at[2])
    lengths_copy.start()
    same_ref[...] = line_ref[...]
    zero_ref[...] = jnp.zeros_like(zero_ref)
    lengths_copy.wait()
    for half in range(2):
        first = span_first(half, ctx_count, span_rows)
        query_pos = first + lax.rem(
            lax.broadcasted_iota(jnp.int32, (1, cols), 1), jnp.int32(span_rows)
        )
        doc_start = jnp.zeros((1, cols), jnp.int32)
        first_key = jnp.int32(0)
        end = jnp.int32(0)
        for doc in range(lengths_ref.shape[0]):
            end = end + lengths_ref[doc]
            doc_start = jnp.where(query_pos >= end, end, doc_start)
            first_key = jnp.where(first >= end, end, first_key)
        starts_ref[half] = doc_start
        count = (first + span_rows - first_key + tile - 1) // tile
        tiles_ref[half] = jnp.full(tiles_ref.shape[1:], count.astype(jnp.float32))
    for slot, copy in enumerate(copies):
        copy.wait()
        for half in range(2):
            for head in range(q_hbm.shape[1] // head_width):
                stack_ref[half, slot, pl.ds(head * span_rows, span_rows), :] = raw_ref[
                    slot,
                    pl.ds(half * span_rows, span_rows),
                    pl.ds(head * head_width, head_width),
                ]
            flip_ref[half, slot] = stack_ref[half, slot].T


def staged_moves(ctx_count, dp_count, inner, part_rows, ctx_index, dp_index):
    for piece in range(dp_count * inner):
        for block in range(ctx_count // inner):
            owner = ctx_index ^ (piece % inner) ^ (block * inner)
            start = (dp_index ^ (piece // inner)) * part_rows
            yield piece, 2 * block * part_rows, owner, start


def paired_moves(inner, part_rows, ctx_index, dp_index):
    for side in range(2):
        holder = dp_index ^ side
        for offset in range(inner):
            piece, near = side * inner + offset, ctx_index ^ offset
            whole = near ^ jnp.where(holder == 1, 3 * inner, inner)
            yield piece, 0, near, holder * part_rows
            yield piece, 2 * part_rows, near ^ (2 * inner), holder * part_rows
            yield piece, 4 * part_rows, whole, 0
            yield piece, 6 * part_rows, whole, part_rows


def send_order(outer):
    return (3, 1, 2) if outer == 4 else tuple(reversed(range(1, outer)))


def attend_kernel(
    ctx_count, dp_count, inner, tile, moves, tiles_ref, starts_ref, stack_ref, flip_ref, _, *refs
):
    piece_count = dp_count * inner
    kv_refs = refs[:piece_count]
    refs = refs[piece_count:]
    keys_ref, dlogits_ref, acc_ref = refs[:3]
    dkv_refs = refs[3 : piece_count + 3]
    values_ref, terms_ref, dweights_ref, tops_ref = refs[piece_count + 3 :]
    cols, head_width = stack_ref.shape[2:]
    tok_rows = (keys_ref.shape[0] - tile) // ctx_count
    part_rows = tok_rows // dp_count
    span_rows = tok_rows // 2
    scale = head_width ** (-0.5)
    ctx_index = lax.axis_index("ctx")
    dp_index = lax.axis_index("dp")

    def rows_of(row, owner, start):
        position = row_position(owner, start, ctx_count, part_rows, span_rows)
        return (
            pl.ds(row, part_rows),
            pl.ds(row + part_rows, part_rows),
            pl.ds(tile + position, part_rows),
        )

    dead = jnp.zeros((tile, head_width), jnp.bfloat16)
    keys_ref[:tile, :] = dead
    values_ref[:tile, :] = dead
    for piece, *place in moves(ctx_index, dp_index):
        key_rows, value_rows, ordered = rows_of(*place)
        keys_ref[ordered, :] = kv_refs[piece][key_rows, :]
        values_ref[ordered, :] = kv_refs[piece][value_rows, :]
    group = min(256, cols)
    groups = [slice(start, start + group) for start in range(0, cols, group)]

    for half in range(2):
        first = span_first(half, ctx_count, span_rows)
        query_pos = first + lax.rem(
            lax.broadcasted_iota(jnp.int32, (1, group), 1), jnp.int32(span_rows)
        )
        doc_start = starts_ref[half]
        count = tile_count(tiles_ref, half)

        def tile_rows(index):
            position = first + span_rows - (index + 1) * tile
            rows = pl.ds(pl.multiple_of(tile + position, span_rows), tile)
            return position, rows, pl.ds(pl.multiple_of(index * tile, tile), tile)

        def sums_step(index, state):
            position, rows, slot = tile_rows(index)
            key_block, value_block = keys_ref[rows, :], values_ref[rows, :]
            all_logits = [
                jnp.dot(key_block, flip_ref[half, 0, :, lanes], preferred_element_type=jnp.float32)
                for lanes in groups
            ]
            all_dweights = [
                jnp.dot(
                    value_block, flip_ref[half, 1, :, lanes], preferred_element_type=jnp.float32
                )
                for lanes in groups
            ]
            following = []
            for lanes, logits, dweights, (top, total, mixed) in zip(
                groups, all_logits, all_dweights, state
            ):
                key_pos = lax.broadcasted_iota(jnp.int32, logits.shape, 0)
                live = (key_pos >= doc_start[:, lanes] - position) & (
                    key_pos <= query_pos - position
                )
                logits = jnp.where(live, logits * (scale * math.log2(math.e)), masked_value)
                new_top = jnp.maximum(top, jnp.max(logits, axis=0, keepdims=True))
                terms = jnp.exp2(logits - new_top)
                terms_ref[slot, lanes] = terms
                dweights_ref[slot, lanes] = dweights
                tops_ref[pl.ds(index, 1), lanes] = new_top
                decay = jnp.exp2(top - new_top)
                following.append(
                    (
                        new_top,
                        total * decay + jnp.sum(terms, axis=0, keepdims=True),
                        mixed * decay + jnp.sum(terms * dweights, axis=0, keepdims=True),
                    )
                )
            return tuple(following)

        zero = jnp.zeros((1, group), jnp.float32)
        empty = (jnp.full_like(zero, masked_value), zero, zero)
        sums = lax.fori_loop(0, count, sums_step, (empty,) * len(groups))
        top, total, mixed = (jnp.concatenate(part, axis=1) for part in zip(*sums))
        inverse = 1.0 / total
        delta = mixed * inverse

        def grads_step(index, carry):
            _, rows, slot = tile_rows(index)
            factor = jnp.exp2(tops_ref[pl.ds(index, 1), :] - top) * inverse
            weights = terms_ref[slot, :] * factor
            dlogits = (weights * (dweights_ref[slot, :] - delta)).astype(jnp.bfloat16)
            for lane_block in range(cols // head_width):
                dlogits_ref[half, lane_block, slot, :] = dlogits[
                    :, lane_block * head_width : (lane_block + 1) * head_width
                ]
            acc_ref[1, rows, :] += jnp.dot(
                weights.astype(jnp.bfloat16),
                stack_ref[half, 1],
                preferred_element_type=jnp.float32,
            )
            acc_ref[0, rows, :] += jnp.dot(
                dlogits, stack_ref[half, 0], preferred_element_type=jnp.float32
            )
            return carry

        lax.fori_loop(0, count, grads_step, 0)

    for piece, *place in staged_moves(
        ctx_count, dp_count, inner, part_rows, ctx_index, dp_index
    ):
        key_rows, value_rows, ordered = rows_of(*place)
        dkv_refs[piece][key_rows, :] = (scale * acc_ref[0, ordered, :]).astype(jnp.bfloat16)
        dkv_refs[piece][value_rows, :] = acc_ref[1, ordered, :].astype(jnp.bfloat16)


def query_kernel(
    ctx_count,
    tile,
    tiles_ref,
    keys_ref,
    dlogits_ref,
    passed_ref,
    dq_ref,
    same_ref,
    sum_ref,
):
    tok_rows = dq_ref.shape[0]
    head_width = keys_ref.shape[1]
    span_rows = tok_rows // 2
    scale = head_width ** (-0.5)
    same_ref[...] = passed_ref[...]
    for half in range(2):
        end = span_first(half, ctx_count, span_rows) + span_rows
        sum_ref[...] = jnp.zeros_like(sum_ref)

        def query_step(index, carry):
            rows = pl.ds(pl.multiple_of(end - index * tile, span_rows), tile)
            slot = pl.ds(pl.multiple_of(index * tile, tile), tile)
            dlogits = jnp.concatenate(
                [dlogits_ref[half, block, slot, :] for block in range(dlogits_ref.shape[1])], axis=1
            )
            sum_ref[...] += jnp.dot(
                keys_ref[rows, :].T, dlogits, preferred_element_type=jnp.float32
            )
            return carry

        lax.fori_loop(0, tile_count(tiles_ref, half), query_step, 0)
        grads = (scale * sum_ref[...]).T.astype(jnp.bfloat16)
        for head in range(dq_ref.shape[1] // head_width):
            dq_ref[
                pl.ds(half * span_rows, span_rows), pl.ds(head * head_width, head_width)
            ] = grads[head * span_rows : (head + 1) * span_rows]


def prepare(ctx_count, tile, doc_lengths, queries, out_grads, head_width, line):
    tok_rows, width = queries.shape
    cols = width // head_width * (tok_rows // 2)
    unmoved = [
        pltpu.with_memory_space_constraint(argument, pltpu.HBM)
        for argument in (doc_lengths, queries, out_grads)
    ]
    return pl.pallas_call(
        functools.partial(prepare_kernel, ctx_count, tile),
        out_shape=(
            jax.ShapeDtypeStruct((2, 2, cols, head_width), jnp.bfloat16),
            jax.ShapeDtypeStruct((2, 2, head_width, cols), jnp.bfloat16),
            jax.ShapeDtypeStruct((2, 1, cols), jnp.int32),
            jax.ShapeDtypeStruct((2, 8, 128), jnp.float32),
            jax.ShapeDtypeStruct((2, tile + ctx_count * tok_rows, head_width), jnp.float32),
            jax.ShapeDtypeStruct(line.shape, line.dtype),
        ),
        in_specs=[hbm, hbm, hbm, vmem],
        out_specs=[vmem] * 6,
        scratch_shapes=[
            pltpu.VMEM((2, tok_rows, width), jnp.bfloat16),
            pltpu.SMEM(doc_lengths.shape, jnp.int32),
            pltpu.SemaphoreType.DMA((3,)),
        ],
        compiler_params=pltpu.CompilerParams(vmem_limit_bytes=4 * 1024 * 1024),
    )(*unmoved, line)


def attend(ctx_count, dp_count, inner, tile, moves, tiles, starts, stacked, flipped, zeros, pieces):
    cols, head_width = stacked.shape[2:]
    seq = dp_count * inner * pieces[0].shape[0] // 2
    slots = -(-seq // tile)
    results = pl.pallas_call(
        functools.partial(attend_kernel, ctx_count, dp_count, inner, tile, moves),
        out_shape=[
            jax.ShapeDtypeStruct((tile + seq, head_width), jnp.bfloat16),
            jax.ShapeDtypeStruct(
                (2, cols // head_width, slots * tile, head_width), jnp.bfloat16
            ),
            jax.ShapeDtypeStruct(zeros.shape, zeros.dtype),
        ]
        + [jax.ShapeDtypeStruct(piece.shape, jnp.bfloat16) for piece in pieces],
        in_specs=[vmem] * (5 + len(pieces)),
        out_specs=[vmem] * (3 + len(pieces)),
        scratch_shapes=[
            pltpu.VMEM((tile + seq, head_width), jnp.bfloat16),
            pltpu.VMEM((slots * tile, cols), jnp.float32),
            pltpu.VMEM((slots * tile, cols), jnp.float32),
            pltpu.VMEM((slots, cols), jnp.float32),
        ],
        input_output_aliases={4: 2},
        compiler_params=pltpu.CompilerParams(vmem_limit_bytes=32 * 1024 * 1024),
    )(tiles, starts, stacked, flipped, zeros, *pieces)
    return results[0], results[1], results[3:]


def query_side(ctx_count, tile, tiles, keys_ordered, dlogits, passed, tok_rows):
    head_width = keys_ordered.shape[1]
    cols = dlogits.shape[1] * head_width
    return pl.pallas_call(
        functools.partial(query_kernel, ctx_count, tile),
        out_shape=(
            jax.ShapeDtypeStruct(
                (tok_rows, cols // (tok_rows // 2) * head_width), jnp.bfloat16
            ),
            jax.ShapeDtypeStruct(passed.shape, passed.dtype),
        ),
        in_specs=[vmem] * 4,
        out_specs=(vmem, vmem),
        scratch_shapes=[
            pltpu.VMEM((head_width, cols), jnp.float32),
        ],
        compiler_params=pltpu.CompilerParams(vmem_limit_bytes=8 * 1024 * 1024),
    )(tiles, keys_ordered, dlogits, passed)


def swap(value, axis, offset):
    pairs = [(index, index ^ offset) for index in range(lax.axis_size(axis))]
    return lax.ppermute(value, axis, pairs)


def total_of(terms):
    return sum(term.astype(jnp.float32) for term in terms).astype(jnp.bfloat16)


def staged_line(keys, values, inner, part_rows):
    head_width = keys.shape[1]
    outer = lax.axis_size("ctx") // inner
    start = lax.axis_index("dp") * part_rows
    own_keys = lax.dynamic_slice_in_dim(keys, start, part_rows, 0)
    own_values = lax.dynamic_slice_in_dim(values, start, part_rows, 0)
    zero = jnp.zeros((), keys.dtype)
    own = jnp.where(
        lax.broadcasted_iota(jnp.int32, (2 * part_rows, head_width), 0) < part_rows,
        lax.pad(own_keys, zero, ((0, part_rows, 0), (0, 0, 0))),
        lax.pad(own_values, zero, ((part_rows, 0, 0), (0, 0, 0))),
    )
    others = [swap(own, "ctx", step * inner) for step in range(1, outer)]
    return jnp.concatenate([own] + others, axis=0)


def paired_line(keys, values, inner, part_rows):
    head_width = keys.shape[1]
    lowest = jnp.array(-jnp.inf, keys.dtype)
    halves = (2, 1, part_rows, head_width)
    own = jnp.maximum(
        lax.pad(keys.reshape(halves), lowest, ((0, 0, 0), (0, 1, 0), (0, 0, 0), (0, 0, 0))),
        lax.pad(values.reshape(halves), lowest, ((0, 0, 0), (1, 0, 0), (0, 0, 0), (0, 0, 0))),
    ).reshape(4 * part_rows, head_width)
    rows = 2 * part_rows
    own_half = lax.dynamic_slice_in_dim(own, lax.axis_index("dp") * rows, rows, 0)
    pairs = [
        (2 * ctx + dp, 2 * (ctx ^ ((3 if dp else 1) * inner)) + dp)
        for ctx in range(lax.axis_size("ctx"))
        for dp in range(2)
    ]
    whole = lax.ppermute(own, ("ctx", "dp"), pairs)
    return jnp.concatenate([own_half, swap(own_half, "ctx", 2 * inner), whole], axis=0)


def body(queries, keys, values, out_grads, doc_lengths):
    ctx_count = lax.axis_size("ctx")
    dp_count = lax.axis_size("dp")
    inner = math.gcd(4, ctx_count)
    outer = ctx_count // inner
    tok_rows, head_width = keys.shape
    part_rows = tok_rows // dp_count
    tile = math.gcd(128, ctx_count * tok_rows)
    if outer == 4 and dp_count == 2:
        line = paired_line(keys, values, inner, part_rows)
        moves = functools.partial(paired_moves, inner, part_rows)
    else:
        line = staged_line(keys, values, inner, part_rows)
        moves = functools.partial(staged_moves, ctx_count, dp_count, inner, part_rows)
    plane = [line] + [swap(line, "ctx", offset) for offset in range(1, inner)]
    stacked, flipped, starts, tiles, zeros, plane[0] = prepare(
        ctx_count, tile, doc_lengths, queries, out_grads, head_width, line
    )
    pieces = plane + [
        swap(piece, "dp", offset) for offset in range(1, dp_count) for piece in plane
    ]
    keys_ordered, dlogits, parts = attend(
        ctx_count, dp_count, inner, tile, moves, tiles, starts, stacked, flipped, zeros, pieces
    )
    plane_sums = [
        total_of(
            [parts[offset]]
            + [swap(parts[far * inner + offset], "dp", far) for far in range(1, dp_count)]
        )
        for offset in range(inner)
    ]
    query_grads, plane_sums[0] = query_side(
        ctx_count, tile, tiles, keys_ordered, dlogits, plane_sums[0], tok_rows
    )
    line_sum = total_of(
        [plane_sums[0]] + [swap(plane_sums[offset], "ctx", offset) for offset in reversed(range(1, inner))]
    )
    blocks = jnp.split(line_sum, outer, axis=0)
    kv_grads = total_of(
        [blocks[0]] + [swap(blocks[block], "ctx", block * inner) for block in send_order(outer)]
    )
    return (query_grads, kv_grads[:part_rows], kv_grads[part_rows:])


def solution(mesh):
    return jax.shard_map(
        body,
        mesh=mesh,
        in_specs=(P("ctx", "dp"), P("ctx", None), P("ctx", None), P("ctx", "dp"), P()),
        out_specs=(P("ctx", "dp"), P(("ctx", "dp"), None), P(("ctx", "dp"), None)),
        check_vma=False,
    )
```

```python
import functools
import math

import jax
import jax.numpy as jnp
from jax import lax
from jax.experimental import pallas as pl
from jax.experimental.pallas import tpu as pltpu
from jax.sharding import PartitionSpec as P

masked_value = -1e30

vmem = pl.BlockSpec(memory_space=pltpu.VMEM)
smem = pl.BlockSpec(memory_space=pltpu.SMEM)
hbm = pl.BlockSpec(memory_space=pltpu.HBM)


def row_position(ctx_index, start, ctx_count, rows, span_rows):
    low = ctx_index * span_rows + start
    high = (2 * ctx_count - 1 - ctx_index) * span_rows + start - span_rows
    return pl.multiple_of(jnp.where(start < span_rows, low, high), rows)


def span_first(half, ctx_count, span_rows):
    ctx_index = lax.axis_index("ctx")
    return (ctx_index if half == 0 else 2 * ctx_count - 1 - ctx_index) * span_rows


def tile_count(tiles_ref, half):
    return jnp.max(tiles_ref[half]).astype(jnp.int32)


def prepare_kernel(
    ctx_count,
    tile,
    lengths_hbm,
    q_hbm,
    g_hbm,
    line_ref,
    stack_ref,
    flip_ref,
    starts_ref,
    tiles_ref,
    zero_ref,
    same_ref,
    raw_ref,
    lengths_ref,
    sems,
):
    tok_rows = q_hbm.shape[0]
    head_width = stack_ref.shape[3]
    cols = stack_ref.shape[2]
    span_rows = tok_rows // 2
    copies = [
        pltpu.make_async_copy(source, raw_ref.at[slot], sems.at[slot])
        for slot, source in enumerate((q_hbm, g_hbm))
    ]
    for copy in copies:
        copy.start()
    lengths_copy = pltpu.make_async_copy(lengths_hbm, lengths_ref, sems.at[2])
    lengths_copy.start()
    same_ref[...] = line_ref[...]
    zero_ref[...] = jnp.zeros_like(zero_ref)
    lengths_copy.wait()
    for half in range(2):
        first = span_first(half, ctx_count, span_rows)
        query_pos = first + lax.rem(
            lax.broadcasted_iota(jnp.int32, (1, cols), 1), jnp.int32(span_rows)
        )
        doc_start = jnp.zeros((1, cols), jnp.int32)
        first_key = jnp.int32(0)
        end = jnp.int32(0)
        for doc in range(lengths_ref.shape[0]):
            end = end + lengths_ref[doc]
            doc_start = jnp.where(query_pos >= end, end, doc_start)
            first_key = jnp.where(first >= end, end, first_key)
        starts_ref[half] = doc_start
        count = (first + span_rows - first_key + tile - 1) // tile
        tiles_ref[half] = jnp.full(tiles_ref.shape[1:], count.astype(jnp.float32))
    for slot, copy in enumerate(copies):
        copy.wait()
        for half in range(2):
            for head in range(q_hbm.shape[1] // head_width):
                stack_ref[half, slot, pl.ds(head * span_rows, span_rows), :] = raw_ref[
                    slot,
                    pl.ds(half * span_rows, span_rows),
                    pl.ds(head * head_width, head_width),
                ]
            flip_ref[half, slot] = stack_ref[half, slot].T


def staged_moves(ctx_count, dp_count, inner, part_rows, ctx_index, dp_index):
    for piece in range(dp_count * inner):
        for block in range(ctx_count // inner):
            owner = ctx_index ^ (piece % inner) ^ (block * inner)
            start = (dp_index ^ (piece // inner)) * part_rows
            yield piece, 2 * block * part_rows, owner, start


def paired_moves(inner, part_rows, ctx_index, dp_index):
    for side in range(2):
        holder = dp_index ^ side
        for offset in range(inner):
            piece, near = side * inner + offset, ctx_index ^ offset
            whole = near ^ jnp.where(holder == 1, 3 * inner, inner)
            yield piece, 0, near, holder * part_rows
            yield piece, 2 * part_rows, near ^ (2 * inner), holder * part_rows
            yield piece, 4 * part_rows, whole, 0
            yield piece, 6 * part_rows, whole, part_rows


def send_order(outer):
    return (3, 1, 2) if outer == 4 else tuple(reversed(range(1, outer)))


def attend_kernel(
    ctx_count, dp_count, inner, tile, moves, tiles_ref, starts_ref, stack_ref, flip_ref, _, *refs
):
    piece_count = dp_count * inner
    kv_refs = refs[:piece_count]
    refs = refs[piece_count:]
    keys_ref, dlogits_ref, acc_ref = refs[:3]
    dkv_refs = refs[3 : piece_count + 3]
    values_ref, terms_ref, dweights_ref, tops_ref, stats_ref = refs[piece_count + 3 :]
    cols, head_width = stack_ref.shape[2:]
    tok_rows = (keys_ref.shape[0] - tile) // ctx_count
    part_rows = tok_rows // dp_count
    span_rows = tok_rows // 2
    scale = head_width ** (-0.5)
    ctx_index = lax.axis_index("ctx")
    dp_index = lax.axis_index("dp")

    def rows_of(row, owner, start):
        position = row_position(owner, start, ctx_count, part_rows, span_rows)
        return (
            pl.ds(row, part_rows),
            pl.ds(row + part_rows, part_rows),
            pl.ds(tile + position, part_rows),
        )

    dead = jnp.zeros((tile, head_width), jnp.bfloat16)
    keys_ref[:tile, :] = dead
    values_ref[:tile, :] = dead
    for piece, *place in moves(ctx_index, dp_index):
        key_rows, value_rows, ordered = rows_of(*place)
        keys_ref[ordered, :] = kv_refs[piece][key_rows, :]
        values_ref[ordered, :] = kv_refs[piece][value_rows, :]
    group = min(256, cols)
    groups = [slice(start, start + group) for start in range(0, cols, group)]
    counts = [tile_count(tiles_ref, half) for half in range(2)]
    firsts = [span_first(half, ctx_count, span_rows) for half in range(2)]
    offset_in_span = lax.rem(
        lax.broadcasted_iota(jnp.int32, (1, group), 1), jnp.int32(span_rows)
    )
    for half in range(2):
        stats_ref[half, 0:1, :] = jnp.full((1, cols), masked_value, jnp.float32)
        stats_ref[half, 1:3, :] = jnp.zeros((2, cols), jnp.float32)

    def tile_place(step):
        half = (step >= counts[0]).astype(jnp.int32)
        index = step - half * counts[0]
        first = jnp.where(half == 1, firsts[1], firsts[0])
        position = first + span_rows - (index + 1) * tile
        rows = pl.ds(pl.multiple_of(tile + position, span_rows), tile)
        slot = pl.ds(pl.multiple_of(step * tile, tile), tile)
        return half, index, first, position, rows, slot

    def sums_step(step, carry):
        half, _, first, position, rows, slot = tile_place(step)
        key_block, value_block = keys_ref[rows, :], values_ref[rows, :]
        all_logits = [
            jnp.dot(key_block, flip_ref[half, 0, :, lanes], preferred_element_type=jnp.float32)
            for lanes in groups
        ]
        all_dweights = [
            jnp.dot(value_block, flip_ref[half, 1, :, lanes], preferred_element_type=jnp.float32)
            for lanes in groups
        ]
        for lanes, logits, dweights in zip(groups, all_logits, all_dweights):
            top = stats_ref[half, 0:1, lanes]
            key_pos = lax.broadcasted_iota(jnp.int32, logits.shape, 0)
            live = (key_pos >= starts_ref[half, :, lanes] - position) & (
                key_pos <= offset_in_span + (first - position)
            )
            logits = jnp.where(live, logits * (scale * math.log2(math.e)), masked_value)
            new_top = jnp.maximum(top, jnp.max(logits, axis=0, keepdims=True))
            terms = jnp.exp2(logits - new_top)
            terms_ref[slot, lanes] = terms
            dweights_ref[slot, lanes] = dweights
            tops_ref[pl.ds(step, 1), lanes] = new_top
            decay = jnp.exp2(top - new_top)
            stats_ref[half, 0:1, lanes] = new_top
            stats_ref[half, 1:2, lanes] = stats_ref[half, 1:2, lanes] * decay + jnp.sum(
                terms, axis=0, keepdims=True
            )
            stats_ref[half, 2:3, lanes] = stats_ref[half, 2:3, lanes] * decay + jnp.sum(
                terms * dweights, axis=0, keepdims=True
            )
        return carry

    lax.fori_loop(0, counts[0] + counts[1], sums_step, 0)
    for half in range(2):
        inverse = 1.0 / stats_ref[half, 1:2, :]
        stats_ref[half, 1:2, :] = inverse
        stats_ref[half, 2:3, :] = stats_ref[half, 2:3, :] * inverse

    def grads_step(step, carry):
        half, index, _, _, rows, slot = tile_place(step)
        top, inverse, delta = (stats_ref[half, row : row + 1, :] for row in range(3))
        factor = jnp.exp2(tops_ref[pl.ds(step, 1), :] - top) * inverse
        weights = terms_ref[slot, :] * factor
        dlogits = (weights * (dweights_ref[slot, :] - delta)).astype(jnp.bfloat16)
        kept = pl.ds(pl.multiple_of(index * tile, tile), tile)
        for lane_block in range(cols // head_width):
            dlogits_ref[half, lane_block, kept, :] = dlogits[
                :, lane_block * head_width : (lane_block + 1) * head_width
            ]
        acc_ref[1, rows, :] += jnp.dot(
            weights.astype(jnp.bfloat16), stack_ref[half, 1], preferred_element_type=jnp.float32
        )
        acc_ref[0, rows, :] += jnp.dot(
            dlogits, stack_ref[half, 0], preferred_element_type=jnp.float32
        )
        return carry

    lax.fori_loop(0, counts[0] + counts[1], grads_step, 0)

    for piece, *place in staged_moves(
        ctx_count, dp_count, inner, part_rows, ctx_index, dp_index
    ):
        key_rows, value_rows, ordered = rows_of(*place)
        dkv_refs[piece][key_rows, :] = (scale * acc_ref[0, ordered, :]).astype(jnp.bfloat16)
        dkv_refs[piece][value_rows, :] = acc_ref[1, ordered, :].astype(jnp.bfloat16)


def query_kernel(
    ctx_count,
    tile,
    tiles_ref,
    keys_ref,
    dlogits_ref,
    passed_ref,
    dq_ref,
    same_ref,
    sum_ref,
):
    tok_rows = dq_ref.shape[0]
    head_width = keys_ref.shape[1]
    span_rows = tok_rows // 2
    scale = head_width ** (-0.5)
    same_ref[...] = passed_ref[...]
    for half in range(2):
        end = span_first(half, ctx_count, span_rows) + span_rows
        sum_ref[...] = jnp.zeros_like(sum_ref)

        def query_step(index, carry):
            rows = pl.ds(pl.multiple_of(end - index * tile, span_rows), tile)
            slot = pl.ds(pl.multiple_of(index * tile, tile), tile)
            dlogits = jnp.concatenate(
                [dlogits_ref[half, block, slot, :] for block in range(dlogits_ref.shape[1])], axis=1
            )
            sum_ref[...] += jnp.dot(
                keys_ref[rows, :].T, dlogits, preferred_element_type=jnp.float32
            )
            return carry

        lax.fori_loop(0, tile_count(tiles_ref, half), query_step, 0)
        grads = (scale * sum_ref[...]).T.astype(jnp.bfloat16)
        for head in range(dq_ref.shape[1] // head_width):
            dq_ref[
                pl.ds(half * span_rows, span_rows), pl.ds(head * head_width, head_width)
            ] = grads[head * span_rows : (head + 1) * span_rows]


def prepare(ctx_count, tile, doc_lengths, queries, out_grads, head_width, line):
    tok_rows, width = queries.shape
    cols = width // head_width * (tok_rows // 2)
    unmoved = [
        pltpu.with_memory_space_constraint(argument, pltpu.HBM)
        for argument in (doc_lengths, queries, out_grads)
    ]
    return pl.pallas_call(
        functools.partial(prepare_kernel, ctx_count, tile),
        out_shape=(
            jax.ShapeDtypeStruct((2, 2, cols, head_width), jnp.bfloat16),
            jax.ShapeDtypeStruct((2, 2, head_width, cols), jnp.bfloat16),
            jax.ShapeDtypeStruct((2, 1, cols), jnp.int32),
            jax.ShapeDtypeStruct((2, 8, 128), jnp.float32),
            jax.ShapeDtypeStruct((2, tile + ctx_count * tok_rows, head_width), jnp.float32),
            jax.ShapeDtypeStruct(line.shape, line.dtype),
        ),
        in_specs=[hbm, hbm, hbm, vmem],
        out_specs=[vmem] * 6,
        scratch_shapes=[
            pltpu.VMEM((2, tok_rows, width), jnp.bfloat16),
            pltpu.SMEM(doc_lengths.shape, jnp.int32),
            pltpu.SemaphoreType.DMA((3,)),
        ],
        compiler_params=pltpu.CompilerParams(vmem_limit_bytes=4 * 1024 * 1024),
    )(*unmoved, line)


def attend(ctx_count, dp_count, inner, tile, moves, tiles, starts, stacked, flipped, zeros, pieces):
    cols, head_width = stacked.shape[2:]
    seq = dp_count * inner * pieces[0].shape[0] // 2
    slots = -(-seq // tile)
    steps = slots + -(-(seq // 2) // tile)
    results = pl.pallas_call(
        functools.partial(attend_kernel, ctx_count, dp_count, inner, tile, moves),
        out_shape=[
            jax.ShapeDtypeStruct((tile + seq, head_width), jnp.bfloat16),
            jax.ShapeDtypeStruct(
                (2, cols // head_width, slots * tile, head_width), jnp.bfloat16
            ),
            jax.ShapeDtypeStruct(zeros.shape, zeros.dtype),
        ]
        + [jax.ShapeDtypeStruct(piece.shape, jnp.bfloat16) for piece in pieces],
        in_specs=[vmem] * (5 + len(pieces)),
        out_specs=[vmem] * (3 + len(pieces)),
        scratch_shapes=[
            pltpu.VMEM((tile + seq, head_width), jnp.bfloat16),
            pltpu.VMEM((steps * tile, cols), jnp.float32),
            pltpu.VMEM((steps * tile, cols), jnp.float32),
            pltpu.VMEM((steps, cols), jnp.float32),
            pltpu.VMEM((2, 8, cols), jnp.float32),
        ],
        input_output_aliases={4: 2},
        compiler_params=pltpu.CompilerParams(vmem_limit_bytes=32 * 1024 * 1024),
    )(tiles, starts, stacked, flipped, zeros, *pieces)
    return results[0], results[1], results[3:]


def query_side(ctx_count, tile, tiles, keys_ordered, dlogits, passed, tok_rows):
    head_width = keys_ordered.shape[1]
    cols = dlogits.shape[1] * head_width
    return pl.pallas_call(
        functools.partial(query_kernel, ctx_count, tile),
        out_shape=(
            jax.ShapeDtypeStruct(
                (tok_rows, cols // (tok_rows // 2) * head_width), jnp.bfloat16
            ),
            jax.ShapeDtypeStruct(passed.shape, passed.dtype),
        ),
        in_specs=[vmem] * 4,
        out_specs=(vmem, vmem),
        scratch_shapes=[
            pltpu.VMEM((head_width, cols), jnp.float32),
        ],
        compiler_params=pltpu.CompilerParams(vmem_limit_bytes=8 * 1024 * 1024),
    )(tiles, keys_ordered, dlogits, passed)


def swap(value, axis, offset):
    pairs = [(index, index ^ offset) for index in range(lax.axis_size(axis))]
    return lax.ppermute(value, axis, pairs)


def total_of(terms):
    return sum(term.astype(jnp.float32) for term in terms).astype(jnp.bfloat16)


def staged_line(keys, values, inner, part_rows):
    head_width = keys.shape[1]
    outer = lax.axis_size("ctx") // inner
    start = lax.axis_index("dp") * part_rows
    own_keys = lax.dynamic_slice_in_dim(keys, start, part_rows, 0)
    own_values = lax.dynamic_slice_in_dim(values, start, part_rows, 0)
    zero = jnp.zeros((), keys.dtype)
    own = jnp.where(
        lax.broadcasted_iota(jnp.int32, (2 * part_rows, head_width), 0) < part_rows,
        lax.pad(own_keys, zero, ((0, part_rows, 0), (0, 0, 0))),
        lax.pad(own_values, zero, ((part_rows, 0, 0), (0, 0, 0))),
    )
    others = [swap(own, "ctx", step * inner) for step in range(1, outer)]
    return jnp.concatenate([own] + others, axis=0)


def paired_line(keys, values, inner, part_rows):
    head_width = keys.shape[1]
    lowest = jnp.array(-jnp.inf, keys.dtype)
    halves = (2, 1, part_rows, head_width)
    own = jnp.maximum(
        lax.pad(keys.reshape(halves), lowest, ((0, 0, 0), (0, 1, 0), (0, 0, 0), (0, 0, 0))),
        lax.pad(values.reshape(halves), lowest, ((0, 0, 0), (1, 0, 0), (0, 0, 0), (0, 0, 0))),
    ).reshape(4 * part_rows, head_width)
    rows = 2 * part_rows
    own_half = lax.dynamic_slice_in_dim(own, lax.axis_index("dp") * rows, rows, 0)
    pairs = [
        (2 * ctx + dp, 2 * (ctx ^ ((3 if dp else 1) * inner)) + dp)
        for ctx in range(lax.axis_size("ctx"))
        for dp in range(2)
    ]
    whole = lax.ppermute(own, ("ctx", "dp"), pairs)
    return jnp.concatenate([own_half, swap(own_half, "ctx", 2 * inner), whole], axis=0)


def body(queries, keys, values, out_grads, doc_lengths):
    ctx_count = lax.axis_size("ctx")
    dp_count = lax.axis_size("dp")
    inner = math.gcd(4, ctx_count)
    outer = ctx_count // inner
    tok_rows, head_width = keys.shape
    part_rows = tok_rows // dp_count
    tile = math.gcd(256, ctx_count * tok_rows)
    if outer == 4 and dp_count == 2:
        line = paired_line(keys, values, inner, part_rows)
        moves = functools.partial(paired_moves, inner, part_rows)
    else:
        line = staged_line(keys, values, inner, part_rows)
        moves = functools.partial(staged_moves, ctx_count, dp_count, inner, part_rows)
    plane = [line] + [swap(line, "ctx", offset) for offset in range(1, inner)]
    stacked, flipped, starts, tiles, zeros, plane[0] = prepare(
        ctx_count, tile, doc_lengths, queries, out_grads, head_width, line
    )
    pieces = plane + [
        swap(piece, "dp", offset) for offset in range(1, dp_count) for piece in plane
    ]
    keys_ordered, dlogits, parts = attend(
        ctx_count, dp_count, inner, tile, moves, tiles, starts, stacked, flipped, zeros, pieces
    )
    plane_sums = [
        total_of(
            [parts[offset]]
            + [swap(parts[far * inner + offset], "dp", far) for far in range(1, dp_count)]
        )
        for offset in range(inner)
    ]
    query_grads, plane_sums[0] = query_side(
        ctx_count, tile, tiles, keys_ordered, dlogits, plane_sums[0], tok_rows
    )
    line_sum = total_of(
        [plane_sums[0]] + [swap(plane_sums[offset], "ctx", offset) for offset in reversed(range(1, inner))]
    )
    blocks = jnp.split(line_sum, outer, axis=0)
    kv_grads = total_of(
        [blocks[0]] + [swap(blocks[block], "ctx", block * inner) for block in send_order(outer)]
    )
    return (query_grads, kv_grads[:part_rows], kv_grads[part_rows:])


def solution(mesh):
    return jax.shard_map(
        body,
        mesh=mesh,
        in_specs=(P("ctx", "dp"), P("ctx", None), P("ctx", None), P("ctx", "dp"), P()),
        out_specs=(P("ctx", "dp"), P(("ctx", "dp"), None), P(("ctx", "dp"), None)),
        check_vma=False,
    )
```

```python
import functools
import math

import jax
import jax.numpy as jnp
from jax import lax
from jax.experimental import pallas as pl
from jax.experimental.pallas import tpu as pltpu
from jax.sharding import PartitionSpec as P

masked_value = -1e30

vmem = pl.BlockSpec(memory_space=pltpu.VMEM)
smem = pl.BlockSpec(memory_space=pltpu.SMEM)
hbm = pl.BlockSpec(memory_space=pltpu.HBM)


def row_position(ctx_index, start, ctx_count, rows, span_rows):
    low = ctx_index * span_rows + start
    high = (2 * ctx_count - 1 - ctx_index) * span_rows + start - span_rows
    return pl.multiple_of(jnp.where(start < span_rows, low, high), rows)


def span_first(half, ctx_count, span_rows):
    ctx_index = lax.axis_index("ctx")
    return (ctx_index if half == 0 else 2 * ctx_count - 1 - ctx_index) * span_rows


def tile_count(tiles_ref, half):
    return jnp.max(tiles_ref[half]).astype(jnp.int32)


def prepare_kernel(
    ctx_count,
    tile,
    lengths_hbm,
    q_hbm,
    g_hbm,
    line_ref,
    stack_ref,
    flip_ref,
    starts_ref,
    tiles_ref,
    zero_ref,
    same_ref,
    raw_ref,
    lengths_ref,
    sems,
):
    tok_rows = q_hbm.shape[0]
    head_width = stack_ref.shape[3]
    cols = stack_ref.shape[2]
    span_rows = tok_rows // 2
    copies = [
        pltpu.make_async_copy(source, raw_ref.at[slot], sems.at[slot])
        for slot, source in enumerate((q_hbm, g_hbm))
    ]
    for copy in copies:
        copy.start()
    lengths_copy = pltpu.make_async_copy(lengths_hbm, lengths_ref, sems.at[2])
    lengths_copy.start()
    same_ref[...] = line_ref[...]
    zero_ref[...] = jnp.zeros_like(zero_ref)
    lengths_copy.wait()
    for half in range(2):
        first = span_first(half, ctx_count, span_rows)
        query_pos = first + lax.rem(
            lax.broadcasted_iota(jnp.int32, (1, cols), 1), jnp.int32(span_rows)
        )
        doc_start = jnp.zeros((1, cols), jnp.int32)
        first_key = jnp.int32(0)
        end = jnp.int32(0)
        for doc in range(lengths_ref.shape[0]):
            end = end + lengths_ref[doc]
            doc_start = jnp.where(query_pos >= end, end, doc_start)
            first_key = jnp.where(first >= end, end, first_key)
        starts_ref[half] = doc_start
        count = (first + span_rows - first_key + tile - 1) // tile
        tiles_ref[half] = jnp.full(tiles_ref.shape[1:], count.astype(jnp.float32))
    for slot, copy in enumerate(copies):
        copy.wait()
        for half in range(2):
            for head in range(q_hbm.shape[1] // head_width):
                stack_ref[half, slot, pl.ds(head * span_rows, span_rows), :] = raw_ref[
                    slot,
                    pl.ds(half * span_rows, span_rows),
                    pl.ds(head * head_width, head_width),
                ]
            flip_ref[half, slot] = stack_ref[half, slot].T


def staged_moves(ctx_count, dp_count, inner, part_rows, ctx_index, dp_index):
    for piece in range(dp_count * inner):
        for block in range(ctx_count // inner):
            owner = ctx_index ^ (piece % inner) ^ (block * inner)
            start = (dp_index ^ (piece // inner)) * part_rows
            yield piece, 2 * block * part_rows, owner, start


def paired_moves(inner, part_rows, ctx_index, dp_index):
    for side in range(2):
        holder = dp_index ^ side
        for offset in range(inner):
            piece, near = side * inner + offset, ctx_index ^ offset
            whole = near ^ jnp.where(holder == 1, 3 * inner, inner)
            yield piece, 0, near, holder * part_rows
            yield piece, 2 * part_rows, near ^ (2 * inner), holder * part_rows
            yield piece, 4 * part_rows, whole, 0
            yield piece, 6 * part_rows, whole, part_rows


def send_order(outer):
    return (3, 1, 2) if outer == 4 else tuple(reversed(range(1, outer)))


def attend_kernel(
    ctx_count, dp_count, inner, tile, moves, tiles_ref, starts_ref, stack_ref, flip_ref, _, *refs
):
    piece_count = dp_count * inner
    kv_refs = refs[:piece_count]
    refs = refs[piece_count:]
    keys_ref, dlogits_ref, acc_ref = refs[:3]
    dkv_refs = refs[3 : piece_count + 3]
    values_ref, terms_ref, dweights_ref, tops_ref = refs[piece_count + 3 :]
    cols, head_width = stack_ref.shape[2:]
    tok_rows = (keys_ref.shape[0] - tile) // ctx_count
    part_rows = tok_rows // dp_count
    span_rows = tok_rows // 2
    scale = head_width ** (-0.5)
    ctx_index = lax.axis_index("ctx")
    dp_index = lax.axis_index("dp")

    def rows_of(row, owner, start):
        position = row_position(owner, start, ctx_count, part_rows, span_rows)
        return (
            pl.ds(row, part_rows),
            pl.ds(row + part_rows, part_rows),
            pl.ds(tile + position, part_rows),
        )

    dead = jnp.zeros((tile, head_width), jnp.bfloat16)
    keys_ref[:tile, :] = dead
    values_ref[:tile, :] = dead
    for piece, *place in moves(ctx_index, dp_index):
        key_rows, value_rows, ordered = rows_of(*place)
        keys_ref[ordered, :] = kv_refs[piece][key_rows, :]
        values_ref[ordered, :] = kv_refs[piece][value_rows, :]
    group = min(256, cols)
    groups = [slice(start, start + group) for start in range(0, cols, group)]

    for half in range(2):
        first = span_first(half, ctx_count, span_rows)
        query_pos = first + lax.rem(
            lax.broadcasted_iota(jnp.int32, (1, group), 1), jnp.int32(span_rows)
        )
        doc_start = starts_ref[half]
        count = tile_count(tiles_ref, half)

        def tile_rows(index):
            position = first + span_rows - (index + 1) * tile
            rows = pl.ds(pl.multiple_of(tile + position, span_rows), tile)
            return position, rows, pl.ds(pl.multiple_of(index * tile, tile), tile)

        def sums_step(index, state):
            position, rows, slot = tile_rows(index)
            key_block, value_block = keys_ref[rows, :], values_ref[rows, :]
            all_logits = [
                jnp.dot(key_block, flip_ref[half, 0, :, lanes], preferred_element_type=jnp.float32)
                for lanes in groups
            ]
            all_dweights = [
                jnp.dot(
                    value_block, flip_ref[half, 1, :, lanes], preferred_element_type=jnp.float32
                )
                for lanes in groups
            ]
            following = []
            for lanes, logits, dweights, (top, total, mixed) in zip(
                groups, all_logits, all_dweights, state
            ):
                key_pos = lax.broadcasted_iota(jnp.int32, logits.shape, 0)
                live = (key_pos >= doc_start[:, lanes] - position) & (
                    key_pos <= query_pos - position
                )
                logits = jnp.where(live, logits * (scale * math.log2(math.e)), masked_value)
                logits = logits.reshape(tile // 8, 8, group)
                new_top = jnp.maximum(top, jnp.max(logits, axis=0))
                terms = jnp.exp2(logits - new_top[None])
                terms_ref[slot, lanes] = terms.reshape(tile, group)
                dweights_ref[slot, lanes] = dweights
                tops_ref[pl.ds(pl.multiple_of(index * 8, 8), 8), lanes] = new_top
                decay = jnp.exp2(top - new_top)
                following.append(
                    (
                        new_top,
                        total * decay + jnp.sum(terms, axis=0),
                        mixed * decay
                        + jnp.sum(terms * dweights.reshape(tile // 8, 8, group), axis=0),
                    )
                )
            return tuple(following)

        zero = jnp.zeros((8, group), jnp.float32)
        empty = (jnp.full_like(zero, masked_value), zero, zero)
        sums = lax.fori_loop(0, count, sums_step, (empty,) * len(groups))
        tops, total, mixed = (jnp.concatenate(part, axis=1) for part in zip(*sums))
        top = jnp.max(tops, axis=0, keepdims=True)
        decay = jnp.exp2(tops - top)
        inverse = 1.0 / jnp.sum(total * decay, axis=0, keepdims=True)
        delta = jnp.sum(mixed * decay, axis=0, keepdims=True) * inverse

        def grads_step(index, carry):
            _, rows, slot = tile_rows(index)
            tops = tops_ref[pl.ds(pl.multiple_of(index * 8, 8), 8), :]
            factor = jnp.exp2(tops - top) * inverse
            weights = (
                terms_ref[slot, :].reshape(tile // 8, 8, cols) * factor[None]
            ).reshape(tile, cols)
            dlogits = (weights * (dweights_ref[slot, :] - delta)).astype(jnp.bfloat16)
            for lane_block in range(cols // head_width):
                dlogits_ref[half, lane_block, slot, :] = dlogits[
                    :, lane_block * head_width : (lane_block + 1) * head_width
                ]
            acc_ref[1, rows, :] += jnp.dot(
                weights.astype(jnp.bfloat16),
                stack_ref[half, 1],
                preferred_element_type=jnp.float32,
            )
            acc_ref[0, rows, :] += jnp.dot(
                dlogits, stack_ref[half, 0], preferred_element_type=jnp.float32
            )
            return carry

        lax.fori_loop(0, count, grads_step, 0)

    for piece, *place in staged_moves(
        ctx_count, dp_count, inner, part_rows, ctx_index, dp_index
    ):
        key_rows, value_rows, ordered = rows_of(*place)
        dkv_refs[piece][key_rows, :] = (scale * acc_ref[0, ordered, :]).astype(jnp.bfloat16)
        dkv_refs[piece][value_rows, :] = acc_ref[1, ordered, :].astype(jnp.bfloat16)


def query_kernel(
    ctx_count,
    tile,
    tiles_ref,
    keys_ref,
    dlogits_ref,
    passed_ref,
    dq_ref,
    same_ref,
    sum_ref,
):
    tok_rows = dq_ref.shape[0]
    head_width = keys_ref.shape[1]
    span_rows = tok_rows // 2
    scale = head_width ** (-0.5)
    same_ref[...] = passed_ref[...]
    for half in range(2):
        end = span_first(half, ctx_count, span_rows) + span_rows
        sum_ref[...] = jnp.zeros_like(sum_ref)

        def query_step(index, carry):
            rows = pl.ds(pl.multiple_of(end - index * tile, span_rows), tile)
            slot = pl.ds(pl.multiple_of(index * tile, tile), tile)
            dlogits = jnp.concatenate(
                [dlogits_ref[half, block, slot, :] for block in range(dlogits_ref.shape[1])], axis=1
            )
            sum_ref[...] += jnp.dot(
                keys_ref[rows, :].T, dlogits, preferred_element_type=jnp.float32
            )
            return carry

        lax.fori_loop(0, tile_count(tiles_ref, half), query_step, 0)
        grads = (scale * sum_ref[...]).T.astype(jnp.bfloat16)
        for head in range(dq_ref.shape[1] // head_width):
            dq_ref[
                pl.ds(half * span_rows, span_rows), pl.ds(head * head_width, head_width)
            ] = grads[head * span_rows : (head + 1) * span_rows]


def prepare(ctx_count, tile, doc_lengths, queries, out_grads, head_width, line):
    tok_rows, width = queries.shape
    cols = width // head_width * (tok_rows // 2)
    unmoved = [
        pltpu.with_memory_space_constraint(argument, pltpu.HBM)
        for argument in (doc_lengths, queries, out_grads)
    ]
    return pl.pallas_call(
        functools.partial(prepare_kernel, ctx_count, tile),
        out_shape=(
            jax.ShapeDtypeStruct((2, 2, cols, head_width), jnp.bfloat16),
            jax.ShapeDtypeStruct((2, 2, head_width, cols), jnp.bfloat16),
            jax.ShapeDtypeStruct((2, 1, cols), jnp.int32),
            jax.ShapeDtypeStruct((2, 8, 128), jnp.float32),
            jax.ShapeDtypeStruct((2, tile + ctx_count * tok_rows, head_width), jnp.float32),
            jax.ShapeDtypeStruct(line.shape, line.dtype),
        ),
        in_specs=[hbm, hbm, hbm, vmem],
        out_specs=[vmem] * 6,
        scratch_shapes=[
            pltpu.VMEM((2, tok_rows, width), jnp.bfloat16),
            pltpu.SMEM(doc_lengths.shape, jnp.int32),
            pltpu.SemaphoreType.DMA((3,)),
        ],
        compiler_params=pltpu.CompilerParams(vmem_limit_bytes=4 * 1024 * 1024),
    )(*unmoved, line)


def attend(ctx_count, dp_count, inner, tile, moves, tiles, starts, stacked, flipped, zeros, pieces):
    cols, head_width = stacked.shape[2:]
    seq = dp_count * inner * pieces[0].shape[0] // 2
    slots = -(-seq // tile)
    results = pl.pallas_call(
        functools.partial(attend_kernel, ctx_count, dp_count, inner, tile, moves),
        out_shape=[
            jax.ShapeDtypeStruct((tile + seq, head_width), jnp.bfloat16),
            jax.ShapeDtypeStruct(
                (2, cols // head_width, slots * tile, head_width), jnp.bfloat16
            ),
            jax.ShapeDtypeStruct(zeros.shape, zeros.dtype),
        ]
        + [jax.ShapeDtypeStruct(piece.shape, jnp.bfloat16) for piece in pieces],
        in_specs=[vmem] * (5 + len(pieces)),
        out_specs=[vmem] * (3 + len(pieces)),
        scratch_shapes=[
            pltpu.VMEM((tile + seq, head_width), jnp.bfloat16),
            pltpu.VMEM((slots * tile, cols), jnp.float32),
            pltpu.VMEM((slots * tile, cols), jnp.float32),
            pltpu.VMEM((8 * slots, cols), jnp.float32),
        ],
        input_output_aliases={4: 2},
        compiler_params=pltpu.CompilerParams(vmem_limit_bytes=32 * 1024 * 1024),
    )(tiles, starts, stacked, flipped, zeros, *pieces)
    return results[0], results[1], results[3:]


def query_side(ctx_count, tile, tiles, keys_ordered, dlogits, passed, tok_rows):
    head_width = keys_ordered.shape[1]
    cols = dlogits.shape[1] * head_width
    return pl.pallas_call(
        functools.partial(query_kernel, ctx_count, tile),
        out_shape=(
            jax.ShapeDtypeStruct(
                (tok_rows, cols // (tok_rows // 2) * head_width), jnp.bfloat16
            ),
            jax.ShapeDtypeStruct(passed.shape, passed.dtype),
        ),
        in_specs=[vmem] * 4,
        out_specs=(vmem, vmem),
        scratch_shapes=[
            pltpu.VMEM((head_width, cols), jnp.float32),
        ],
        compiler_params=pltpu.CompilerParams(vmem_limit_bytes=8 * 1024 * 1024),
    )(tiles, keys_ordered, dlogits, passed)


def swap(value, axis, offset):
    pairs = [(index, index ^ offset) for index in range(lax.axis_size(axis))]
    return lax.ppermute(value, axis, pairs)


def total_of(terms):
    return sum(term.astype(jnp.float32) for term in terms).astype(jnp.bfloat16)


def staged_line(keys, values, inner, part_rows):
    head_width = keys.shape[1]
    outer = lax.axis_size("ctx") // inner
    start = lax.axis_index("dp") * part_rows
    own_keys = lax.dynamic_slice_in_dim(keys, start, part_rows, 0)
    own_values = lax.dynamic_slice_in_dim(values, start, part_rows, 0)
    zero = jnp.zeros((), keys.dtype)
    own = jnp.where(
        lax.broadcasted_iota(jnp.int32, (2 * part_rows, head_width), 0) < part_rows,
        lax.pad(own_keys, zero, ((0, part_rows, 0), (0, 0, 0))),
        lax.pad(own_values, zero, ((part_rows, 0, 0), (0, 0, 0))),
    )
    others = [swap(own, "ctx", step * inner) for step in range(1, outer)]
    return jnp.concatenate([own] + others, axis=0)


def paired_line(keys, values, inner, part_rows):
    head_width = keys.shape[1]
    lowest = jnp.array(-jnp.inf, keys.dtype)
    halves = (2, 1, part_rows, head_width)
    own = jnp.maximum(
        lax.pad(keys.reshape(halves), lowest, ((0, 0, 0), (0, 1, 0), (0, 0, 0), (0, 0, 0))),
        lax.pad(values.reshape(halves), lowest, ((0, 0, 0), (1, 0, 0), (0, 0, 0), (0, 0, 0))),
    ).reshape(4 * part_rows, head_width)
    rows = 2 * part_rows
    own_half = lax.dynamic_slice_in_dim(own, lax.axis_index("dp") * rows, rows, 0)
    pairs = [
        (2 * ctx + dp, 2 * (ctx ^ ((3 if dp else 1) * inner)) + dp)
        for ctx in range(lax.axis_size("ctx"))
        for dp in range(2)
    ]
    whole = lax.ppermute(own, ("ctx", "dp"), pairs)
    return jnp.concatenate([own_half, swap(own_half, "ctx", 2 * inner), whole], axis=0)


def body(queries, keys, values, out_grads, doc_lengths):
    ctx_count = lax.axis_size("ctx")
    dp_count = lax.axis_size("dp")
    inner = math.gcd(4, ctx_count)
    outer = ctx_count // inner
    tok_rows, head_width = keys.shape
    part_rows = tok_rows // dp_count
    tile = math.gcd(256, ctx_count * tok_rows)
    if outer == 4 and dp_count == 2:
        line = paired_line(keys, values, inner, part_rows)
        moves = functools.partial(paired_moves, inner, part_rows)
    else:
        line = staged_line(keys, values, inner, part_rows)
        moves = functools.partial(staged_moves, ctx_count, dp_count, inner, part_rows)
    plane = [line] + [swap(line, "ctx", offset) for offset in range(1, inner)]
    stacked, flipped, starts, tiles, zeros, plane[0] = prepare(
        ctx_count, tile, doc_lengths, queries, out_grads, head_width, line
    )
    pieces = plane + [
        swap(piece, "dp", offset) for offset in range(1, dp_count) for piece in plane
    ]
    keys_ordered, dlogits, parts = attend(
        ctx_count, dp_count, inner, tile, moves, tiles, starts, stacked, flipped, zeros, pieces
    )
    plane_sums = [
        total_of(
            [parts[offset]]
            + [swap(parts[far * inner + offset], "dp", far) for far in range(1, dp_count)]
        )
        for offset in range(inner)
    ]
    query_grads, plane_sums[0] = query_side(
        ctx_count, tile, tiles, keys_ordered, dlogits, plane_sums[0], tok_rows
    )
    line_sum = total_of(
        [plane_sums[0]] + [swap(plane_sums[offset], "ctx", offset) for offset in reversed(range(1, inner))]
    )
    blocks = jnp.split(line_sum, outer, axis=0)
    kv_grads = total_of(
        [blocks[0]] + [swap(blocks[block], "ctx", block * inner) for block in send_order(outer)]
    )
    return (query_grads, kv_grads[:part_rows], kv_grads[part_rows:])


def solution(mesh):
    return jax.shard_map(
        body,
        mesh=mesh,
        in_specs=(P("ctx", "dp"), P("ctx", None), P("ctx", None), P("ctx", "dp"), P()),
        out_specs=(P("ctx", "dp"), P(("ctx", "dp"), None), P(("ctx", "dp"), None)),
        check_vma=False,
    )
```

```python
import functools
import math

import jax
import jax.numpy as jnp
from jax import lax
from jax.experimental import pallas as pl
from jax.experimental.pallas import tpu as pltpu
from jax.sharding import PartitionSpec as P

masked_value = -1e30

vmem = pl.BlockSpec(memory_space=pltpu.VMEM)
smem = pl.BlockSpec(memory_space=pltpu.SMEM)
hbm = pl.BlockSpec(memory_space=pltpu.HBM)


def row_position(ctx_index, start, ctx_count, rows, span_rows):
    low = ctx_index * span_rows + start
    high = (2 * ctx_count - 1 - ctx_index) * span_rows + start - span_rows
    return pl.multiple_of(jnp.where(start < span_rows, low, high), rows)


def span_first(half, ctx_count, span_rows):
    ctx_index = lax.axis_index("ctx")
    return (ctx_index if half == 0 else 2 * ctx_count - 1 - ctx_index) * span_rows


def tile_count(tiles_ref, half):
    return jnp.max(tiles_ref[half]).astype(jnp.int32)


def prepare_kernel(
    ctx_count,
    tile,
    lengths_hbm,
    q_hbm,
    g_hbm,
    line_ref,
    stack_ref,
    flip_ref,
    starts_ref,
    tiles_ref,
    zero_ref,
    same_ref,
    raw_ref,
    lengths_ref,
    sems,
):
    tok_rows = q_hbm.shape[0]
    head_width = stack_ref.shape[3]
    cols = stack_ref.shape[2]
    span_rows = tok_rows // 2
    copies = [
        pltpu.make_async_copy(source, raw_ref.at[slot], sems.at[slot])
        for slot, source in enumerate((q_hbm, g_hbm))
    ]
    for copy in copies:
        copy.start()
    lengths_copy = pltpu.make_async_copy(lengths_hbm, lengths_ref, sems.at[2])
    lengths_copy.start()
    same_ref[...] = line_ref[...]
    zero_ref[...] = jnp.zeros_like(zero_ref)
    lengths_copy.wait()
    for half in range(2):
        first = span_first(half, ctx_count, span_rows)
        query_pos = first + lax.rem(
            lax.broadcasted_iota(jnp.int32, (1, cols), 1), jnp.int32(span_rows)
        )
        doc_start = jnp.zeros((1, cols), jnp.int32)
        first_key = jnp.int32(0)
        end = jnp.int32(0)
        for doc in range(lengths_ref.shape[0]):
            end = end + lengths_ref[doc]
            doc_start = jnp.where(query_pos >= end, end, doc_start)
            first_key = jnp.where(first >= end, end, first_key)
        starts_ref[half] = doc_start
        count = (first + span_rows - first_key + tile - 1) // tile
        tiles_ref[half] = jnp.full(tiles_ref.shape[1:], count.astype(jnp.float32))
    for slot, copy in enumerate(copies):
        copy.wait()
        for half in range(2):
            for head in range(q_hbm.shape[1] // head_width):
                stack_ref[half, slot, pl.ds(head * span_rows, span_rows), :] = raw_ref[
                    slot,
                    pl.ds(half * span_rows, span_rows),
                    pl.ds(head * head_width, head_width),
                ]
            flip_ref[half, slot] = stack_ref[half, slot].T


def staged_moves(ctx_count, dp_count, inner, part_rows, ctx_index, dp_index):
    for piece in range(dp_count * inner):
        for block in range(ctx_count // inner):
            owner = ctx_index ^ (piece % inner) ^ (block * inner)
            start = (dp_index ^ (piece // inner)) * part_rows
            yield piece, 2 * block * part_rows, owner, start


def paired_moves(inner, part_rows, ctx_index, dp_index):
    for side in range(2):
        holder = dp_index ^ side
        for offset in range(inner):
            piece, near = side * inner + offset, ctx_index ^ offset
            whole = near ^ jnp.where(holder == 1, 3 * inner, inner)
            yield piece, 0, near, holder * part_rows
            yield piece, 2 * part_rows, near ^ (2 * inner), holder * part_rows
            yield piece, 4 * part_rows, whole, 0
            yield piece, 6 * part_rows, whole, part_rows


def send_order(outer):
    return (3, 1, 2) if outer == 4 else tuple(reversed(range(1, outer)))


def attend_kernel(
    ctx_count, dp_count, inner, tile, moves, tiles_ref, starts_ref, stack_ref, flip_ref, _, *refs
):
    piece_count = dp_count * inner
    kv_refs = refs[:piece_count]
    refs = refs[piece_count:]
    keys_ref, dlogits_ref, acc_ref = refs[:3]
    dkv_refs = refs[3 : piece_count + 3]
    values_ref, terms_ref, dweights_ref, tops_ref, stats_ref = refs[piece_count + 3 :]
    cols, head_width = stack_ref.shape[2:]
    tok_rows = (keys_ref.shape[0] - tile) // ctx_count
    part_rows = tok_rows // dp_count
    span_rows = tok_rows // 2
    scale = head_width ** (-0.5)
    ctx_index = lax.axis_index("ctx")
    dp_index = lax.axis_index("dp")

    def rows_of(row, owner, start):
        position = row_position(owner, start, ctx_count, part_rows, span_rows)
        return (
            pl.ds(row, part_rows),
            pl.ds(row + part_rows, part_rows),
            pl.ds(tile + position, part_rows),
        )

    dead = jnp.zeros((tile, head_width), jnp.bfloat16)
    keys_ref[:tile, :] = dead
    values_ref[:tile, :] = dead
    for piece, *place in moves(ctx_index, dp_index):
        key_rows, value_rows, ordered = rows_of(*place)
        keys_ref[ordered, :] = kv_refs[piece][key_rows, :]
        values_ref[ordered, :] = kv_refs[piece][value_rows, :]
    group = min(256, cols)
    groups = [slice(start, start + group) for start in range(0, cols, group)]
    counts = [tile_count(tiles_ref, half) for half in range(2)]
    firsts = [span_first(half, ctx_count, span_rows) for half in range(2)]
    offset_in_span = lax.rem(
        lax.broadcasted_iota(jnp.int32, (1, group), 1), jnp.int32(span_rows)
    )
    for half in range(2):
        stats_ref[half, 0:1, :] = jnp.full((1, cols), masked_value, jnp.float32)
        stats_ref[half, 1:3, :] = jnp.zeros((2, cols), jnp.float32)

    def tile_place(step):
        half = (step >= counts[0]).astype(jnp.int32)
        index = step - half * counts[0]
        first = jnp.where(half == 1, firsts[1], firsts[0])
        position = first + span_rows - (index + 1) * tile
        rows = pl.ds(pl.multiple_of(tile + position, span_rows), tile)
        slot = pl.ds(pl.multiple_of(step * tile, tile), tile)
        return half, index, first, position, rows, slot

    def sums_step(step, carry):
        half, _, first, position, rows, slot = tile_place(step)
        key_block, value_block = keys_ref[rows, :], values_ref[rows, :]
        all_logits = [
            jnp.dot(key_block, flip_ref[half, 0, :, lanes], preferred_element_type=jnp.float32)
            for lanes in groups
        ]
        all_dweights = [
            jnp.dot(value_block, flip_ref[half, 1, :, lanes], preferred_element_type=jnp.float32)
            for lanes in groups
        ]
        for lanes, logits, dweights in zip(groups, all_logits, all_dweights):
            top = stats_ref[half, 0:1, lanes]
            key_pos = lax.broadcasted_iota(jnp.int32, logits.shape, 0)
            live = (key_pos >= starts_ref[half, :, lanes] - position) & (
                key_pos <= offset_in_span + (first - position)
            )
            logits = jnp.where(live, logits * (scale * math.log2(math.e)), masked_value)
            new_top = jnp.maximum(top, jnp.max(logits, axis=0, keepdims=True))
            terms = jnp.exp2(logits - new_top)
            terms_ref[slot, lanes] = terms
            dweights_ref[slot, lanes] = dweights
            tops_ref[pl.ds(step, 1), lanes] = new_top
            decay = jnp.exp2(top - new_top)
            stats_ref[half, 0:1, lanes] = new_top
            stats_ref[half, 1:2, lanes] = stats_ref[half, 1:2, lanes] * decay + jnp.sum(
                terms, axis=0, keepdims=True
            )
            stats_ref[half, 2:3, lanes] = stats_ref[half, 2:3, lanes] * decay + jnp.sum(
                terms * dweights, axis=0, keepdims=True
            )
        return carry

    lax.fori_loop(0, counts[0] + counts[1], sums_step, 0)
    for half in range(2):
        inverse = 1.0 / stats_ref[half, 1:2, :]
        stats_ref[half, 1:2, :] = inverse
        stats_ref[half, 2:3, :] = stats_ref[half, 2:3, :] * inverse

    def grads_step(step, carry):
        half, index, _, _, rows, slot = tile_place(step)
        top, inverse, delta = (stats_ref[half, row : row + 1, :] for row in range(3))
        factor = jnp.exp2(tops_ref[pl.ds(step, 1), :] - top) * inverse
        weights = terms_ref[slot, :] * factor
        dlogits = (weights * (dweights_ref[slot, :] - delta)).astype(jnp.bfloat16)
        kept = pl.ds(pl.multiple_of(index * tile, tile), tile)
        for lane_block in range(cols // head_width):
            dlogits_ref[half, lane_block, kept, :] = dlogits[
                :, lane_block * head_width : (lane_block + 1) * head_width
            ]
        acc_ref[1, rows, :] += jnp.dot(
            weights.astype(jnp.bfloat16), stack_ref[half, 1], preferred_element_type=jnp.float32
        )
        acc_ref[0, rows, :] += jnp.dot(
            dlogits, stack_ref[half, 0], preferred_element_type=jnp.float32
        )
        return carry

    lax.fori_loop(0, counts[0] + counts[1], grads_step, 0)

    for piece, *place in staged_moves(
        ctx_count, dp_count, inner, part_rows, ctx_index, dp_index
    ):
        key_rows, value_rows, ordered = rows_of(*place)
        dkv_refs[piece][key_rows, :] = (scale * acc_ref[0, ordered, :]).astype(jnp.bfloat16)
        dkv_refs[piece][value_rows, :] = acc_ref[1, ordered, :].astype(jnp.bfloat16)


def query_kernel(
    ctx_count,
    tile,
    tiles_ref,
    keys_ref,
    dlogits_ref,
    passed_ref,
    dq_ref,
    same_ref,
    sum_ref,
):
    tok_rows = dq_ref.shape[0]
    head_width = keys_ref.shape[1]
    span_rows = tok_rows // 2
    scale = head_width ** (-0.5)
    same_ref[...] = passed_ref[...]
    for half in range(2):
        end = span_first(half, ctx_count, span_rows) + span_rows
        sum_ref[...] = jnp.zeros_like(sum_ref)

        def query_step(index, carry):
            rows = pl.ds(pl.multiple_of(end - index * tile, span_rows), tile)
            slot = pl.ds(pl.multiple_of(index * tile, tile), tile)
            dlogits = jnp.concatenate(
                [dlogits_ref[half, block, slot, :] for block in range(dlogits_ref.shape[1])], axis=1
            )
            sum_ref[...] += jnp.dot(
                keys_ref[rows, :].T, dlogits, preferred_element_type=jnp.float32
            )
            return carry

        lax.fori_loop(0, tile_count(tiles_ref, half), query_step, 0)
        grads = (scale * sum_ref[...]).T.astype(jnp.bfloat16)
        for head in range(dq_ref.shape[1] // head_width):
            dq_ref[
                pl.ds(half * span_rows, span_rows), pl.ds(head * head_width, head_width)
            ] = grads[head * span_rows : (head + 1) * span_rows]


def prepare(ctx_count, tile, doc_lengths, queries, out_grads, head_width, line):
    tok_rows, width = queries.shape
    cols = width // head_width * (tok_rows // 2)
    unmoved = [
        pltpu.with_memory_space_constraint(argument, pltpu.HBM)
        for argument in (doc_lengths, queries, out_grads)
    ]
    return pl.pallas_call(
        functools.partial(prepare_kernel, ctx_count, tile),
        out_shape=(
            jax.ShapeDtypeStruct((2, 2, cols, head_width), jnp.bfloat16),
            jax.ShapeDtypeStruct((2, 2, head_width, cols), jnp.bfloat16),
            jax.ShapeDtypeStruct((2, 1, cols), jnp.int32),
            jax.ShapeDtypeStruct((2, 8, 128), jnp.float32),
            jax.ShapeDtypeStruct((2, tile + ctx_count * tok_rows, head_width), jnp.float32),
            jax.ShapeDtypeStruct(line.shape, line.dtype),
        ),
        in_specs=[hbm, hbm, hbm, vmem],
        out_specs=[vmem] * 6,
        scratch_shapes=[
            pltpu.VMEM((2, tok_rows, width), jnp.bfloat16),
            pltpu.SMEM(doc_lengths.shape, jnp.int32),
            pltpu.SemaphoreType.DMA((3,)),
        ],
        compiler_params=pltpu.CompilerParams(vmem_limit_bytes=4 * 1024 * 1024),
    )(*unmoved, line)


def attend(ctx_count, dp_count, inner, tile, moves, tiles, starts, stacked, flipped, zeros, pieces):
    cols, head_width = stacked.shape[2:]
    seq = dp_count * inner * pieces[0].shape[0] // 2
    slots = -(-seq // tile)
    steps = slots + -(-(seq // 2) // tile)
    results = pl.pallas_call(
        functools.partial(attend_kernel, ctx_count, dp_count, inner, tile, moves),
        out_shape=[
            jax.ShapeDtypeStruct((tile + seq, head_width), jnp.bfloat16),
            jax.ShapeDtypeStruct(
                (2, cols // head_width, slots * tile, head_width), jnp.bfloat16
            ),
            jax.ShapeDtypeStruct(zeros.shape, zeros.dtype),
        ]
        + [jax.ShapeDtypeStruct(piece.shape, jnp.bfloat16) for piece in pieces],
        in_specs=[vmem] * (5 + len(pieces)),
        out_specs=[vmem] * (3 + len(pieces)),
        scratch_shapes=[
            pltpu.VMEM((tile + seq, head_width), jnp.bfloat16),
            pltpu.VMEM((steps * tile, cols), jnp.float32),
            pltpu.VMEM((steps * tile, cols), jnp.float32),
            pltpu.VMEM((steps, cols), jnp.float32),
            pltpu.VMEM((2, 8, cols), jnp.float32),
        ],
        input_output_aliases={4: 2},
        compiler_params=pltpu.CompilerParams(vmem_limit_bytes=32 * 1024 * 1024),
    )(tiles, starts, stacked, flipped, zeros, *pieces)
    return results[0], results[1], results[3:]


def query_side(ctx_count, tile, tiles, keys_ordered, dlogits, passed, tok_rows):
    head_width = keys_ordered.shape[1]
    cols = dlogits.shape[1] * head_width
    return pl.pallas_call(
        functools.partial(query_kernel, ctx_count, tile),
        out_shape=(
            jax.ShapeDtypeStruct(
                (tok_rows, cols // (tok_rows // 2) * head_width), jnp.bfloat16
            ),
            jax.ShapeDtypeStruct(passed.shape, passed.dtype),
        ),
        in_specs=[vmem] * 4,
        out_specs=(vmem, vmem),
        scratch_shapes=[
            pltpu.VMEM((head_width, cols), jnp.float32),
        ],
        compiler_params=pltpu.CompilerParams(vmem_limit_bytes=8 * 1024 * 1024),
    )(tiles, keys_ordered, dlogits, passed)


def swap(value, axis, offset):
    pairs = [(index, index ^ offset) for index in range(lax.axis_size(axis))]
    return lax.ppermute(value, axis, pairs)


def total_of(terms):
    return sum(term.astype(jnp.float32) for term in terms).astype(jnp.bfloat16)


def staged_line(keys, values, inner, part_rows):
    head_width = keys.shape[1]
    outer = lax.axis_size("ctx") // inner
    start = lax.axis_index("dp") * part_rows
    own_keys = lax.dynamic_slice_in_dim(keys, start, part_rows, 0)
    own_values = lax.dynamic_slice_in_dim(values, start, part_rows, 0)
    zero = jnp.zeros((), keys.dtype)
    own = jnp.where(
        lax.broadcasted_iota(jnp.int32, (2 * part_rows, head_width), 0) < part_rows,
        lax.pad(own_keys, zero, ((0, part_rows, 0), (0, 0, 0))),
        lax.pad(own_values, zero, ((part_rows, 0, 0), (0, 0, 0))),
    )
    others = [swap(own, "ctx", step * inner) for step in range(1, outer)]
    return jnp.concatenate([own] + others, axis=0)


def paired_line(keys, values, inner, part_rows):
    head_width = keys.shape[1]
    lowest = jnp.array(-jnp.inf, keys.dtype)
    halves = (2, 1, part_rows, head_width)
    own = jnp.maximum(
        lax.pad(keys.reshape(halves), lowest, ((0, 0, 0), (0, 1, 0), (0, 0, 0), (0, 0, 0))),
        lax.pad(values.reshape(halves), lowest, ((0, 0, 0), (1, 0, 0), (0, 0, 0), (0, 0, 0))),
    ).reshape(4 * part_rows, head_width)
    rows = 2 * part_rows
    own_half = lax.dynamic_slice_in_dim(own, lax.axis_index("dp") * rows, rows, 0)
    pairs = [
        (2 * ctx + dp, 2 * (ctx ^ ((3 if dp else 1) * inner)) + dp)
        for ctx in range(lax.axis_size("ctx"))
        for dp in range(2)
    ]
    whole = lax.ppermute(own, ("ctx", "dp"), pairs)
    return jnp.concatenate([own_half, swap(own_half, "ctx", 2 * inner), whole], axis=0)


def body(queries, keys, values, out_grads, doc_lengths):
    ctx_count = lax.axis_size("ctx")
    dp_count = lax.axis_size("dp")
    inner = math.gcd(4, ctx_count)
    outer = ctx_count // inner
    tok_rows, head_width = keys.shape
    part_rows = tok_rows // dp_count
    tile = math.gcd(512, ctx_count * tok_rows)
    if outer == 4 and dp_count == 2:
        line = paired_line(keys, values, inner, part_rows)
        moves = functools.partial(paired_moves, inner, part_rows)
    else:
        line = staged_line(keys, values, inner, part_rows)
        moves = functools.partial(staged_moves, ctx_count, dp_count, inner, part_rows)
    plane = [line] + [swap(line, "ctx", offset) for offset in range(1, inner)]
    stacked, flipped, starts, tiles, zeros, plane[0] = prepare(
        ctx_count, tile, doc_lengths, queries, out_grads, head_width, line
    )
    pieces = plane + [
        swap(piece, "dp", offset) for offset in range(1, dp_count) for piece in plane
    ]
    keys_ordered, dlogits, parts = attend(
        ctx_count, dp_count, inner, tile, moves, tiles, starts, stacked, flipped, zeros, pieces
    )
    plane_sums = [
        total_of(
            [parts[offset]]
            + [swap(parts[far * inner + offset], "dp", far) for far in range(1, dp_count)]
        )
        for offset in range(inner)
    ]
    query_grads, plane_sums[0] = query_side(
        ctx_count, tile, tiles, keys_ordered, dlogits, plane_sums[0], tok_rows
    )
    line_sum = total_of(
        [plane_sums[0]] + [swap(plane_sums[offset], "ctx", offset) for offset in reversed(range(1, inner))]
    )
    blocks = jnp.split(line_sum, outer, axis=0)
    kv_grads = total_of(
        [blocks[0]] + [swap(blocks[block], "ctx", block * inner) for block in send_order(outer)]
    )
    return (query_grads, kv_grads[:part_rows], kv_grads[part_rows:])


def solution(mesh):
    return jax.shard_map(
        body,
        mesh=mesh,
        in_specs=(P("ctx", "dp"), P("ctx", None), P("ctx", None), P("ctx", "dp"), P()),
        out_specs=(P("ctx", "dp"), P(("ctx", "dp"), None), P(("ctx", "dp"), None)),
        check_vma=False,
    )
```

```python
import functools
import math

import jax
import jax.numpy as jnp
from jax import lax
from jax.experimental import pallas as pl
from jax.experimental.pallas import tpu as pltpu
from jax.sharding import PartitionSpec as P

masked_value = -1e30

vmem = pl.BlockSpec(memory_space=pltpu.VMEM)
smem = pl.BlockSpec(memory_space=pltpu.SMEM)
hbm = pl.BlockSpec(memory_space=pltpu.HBM)


def row_position(ctx_index, start, ctx_count, rows, span_rows):
    low = ctx_index * span_rows + start
    high = (2 * ctx_count - 1 - ctx_index) * span_rows + start - span_rows
    return pl.multiple_of(jnp.where(start < span_rows, low, high), rows)


def span_first(half, ctx_count, span_rows):
    ctx_index = lax.axis_index("ctx")
    return (ctx_index if half == 0 else 2 * ctx_count - 1 - ctx_index) * span_rows


def tile_count(tiles_ref, half):
    return jnp.max(tiles_ref[half]).astype(jnp.int32)


def prepare_kernel(
    ctx_count,
    tile,
    lengths_hbm,
    q_hbm,
    g_hbm,
    line_ref,
    stack_ref,
    flip_ref,
    starts_ref,
    tiles_ref,
    zero_ref,
    same_ref,
    raw_ref,
    lengths_ref,
    sems,
):
    tok_rows = q_hbm.shape[0]
    head_width = stack_ref.shape[3]
    cols = stack_ref.shape[2]
    span_rows = tok_rows // 2
    copies = [
        pltpu.make_async_copy(source, raw_ref.at[slot], sems.at[slot])
        for slot, source in enumerate((q_hbm, g_hbm))
    ]
    for copy in copies:
        copy.start()
    lengths_copy = pltpu.make_async_copy(lengths_hbm, lengths_ref, sems.at[2])
    lengths_copy.start()
    same_ref[...] = line_ref[...]
    zero_ref[...] = jnp.zeros_like(zero_ref)
    lengths_copy.wait()
    for half in range(2):
        first = span_first(half, ctx_count, span_rows)
        query_pos = first + lax.rem(
            lax.broadcasted_iota(jnp.int32, (1, cols), 1), jnp.int32(span_rows)
        )
        doc_start = jnp.zeros((1, cols), jnp.int32)
        first_key = jnp.int32(0)
        end = jnp.int32(0)
        for doc in range(lengths_ref.shape[0]):
            end = end + lengths_ref[doc]
            doc_start = jnp.where(query_pos >= end, end, doc_start)
            first_key = jnp.where(first >= end, end, first_key)
        starts_ref[half] = doc_start
        count = (first + span_rows - first_key + tile - 1) // tile
        tiles_ref[half] = jnp.full(tiles_ref.shape[1:], count.astype(jnp.float32))
    for slot, copy in enumerate(copies):
        copy.wait()
        for half in range(2):
            for head in range(q_hbm.shape[1] // head_width):
                stack_ref[half, slot, pl.ds(head * span_rows, span_rows), :] = raw_ref[
                    slot,
                    pl.ds(half * span_rows, span_rows),
                    pl.ds(head * head_width, head_width),
                ]
            flip_ref[half, slot] = stack_ref[half, slot].T


def staged_moves(ctx_count, dp_count, inner, part_rows, ctx_index, dp_index):
    for piece in range(dp_count * inner):
        for block in range(ctx_count // inner):
            owner = ctx_index ^ (piece % inner) ^ (block * inner)
            start = (dp_index ^ (piece // inner)) * part_rows
            yield piece, 2 * block * part_rows, owner, start


def paired_moves(inner, part_rows, ctx_index, dp_index):
    for side in range(2):
        holder = dp_index ^ side
        for offset in range(inner):
            piece, near = side * inner + offset, ctx_index ^ offset
            whole = near ^ jnp.where(holder == 1, 3 * inner, inner)
            yield piece, 0, near, holder * part_rows
            yield piece, 2 * part_rows, near ^ (2 * inner), holder * part_rows
            yield piece, 4 * part_rows, whole, 0
            yield piece, 6 * part_rows, whole, part_rows


def send_order(outer):
    return (3, 1, 2) if outer == 4 else tuple(reversed(range(1, outer)))


def attend_kernel(
    ctx_count, dp_count, inner, tile, moves, tiles_ref, starts_ref, stack_ref, flip_ref, _, *refs
):
    piece_count = dp_count * inner
    kv_refs = refs[:piece_count]
    refs = refs[piece_count:]
    keys_ref, dlogits_ref, acc_ref = refs[:3]
    dkv_refs = refs[3 : piece_count + 3]
    values_ref, terms_ref, dweights_ref, tops_ref = refs[piece_count + 3 :]
    cols, head_width = stack_ref.shape[2:]
    tok_rows = (keys_ref.shape[0] - tile) // ctx_count
    part_rows = tok_rows // dp_count
    span_rows = tok_rows // 2
    scale = head_width ** (-0.5)
    ctx_index = lax.axis_index("ctx")
    dp_index = lax.axis_index("dp")

    def rows_of(row, owner, start):
        position = row_position(owner, start, ctx_count, part_rows, span_rows)
        return (
            pl.ds(row, part_rows),
            pl.ds(row + part_rows, part_rows),
            pl.ds(tile + position, part_rows),
        )

    dead = jnp.zeros((tile, head_width), jnp.bfloat16)
    keys_ref[:tile, :] = dead
    values_ref[:tile, :] = dead
    for piece, *place in moves(ctx_index, dp_index):
        key_rows, value_rows, ordered = rows_of(*place)
        keys_ref[ordered, :] = kv_refs[piece][key_rows, :]
        values_ref[ordered, :] = kv_refs[piece][value_rows, :]
    group = min(512, cols)
    groups = [slice(start, start + group) for start in range(0, cols, group)]

    for half in range(2):
        first = span_first(half, ctx_count, span_rows)
        query_pos = first + lax.rem(
            lax.broadcasted_iota(jnp.int32, (1, group), 1), jnp.int32(span_rows)
        )
        doc_start = starts_ref[half]
        count = tile_count(tiles_ref, half)

        def tile_rows(index):
            position = first + span_rows - (index + 1) * tile
            rows = pl.ds(pl.multiple_of(tile + position, span_rows), tile)
            return position, rows, pl.ds(pl.multiple_of(index * tile, tile), tile)

        def sums_step(index, state):
            position, rows, slot = tile_rows(index)
            key_block, value_block = keys_ref[rows, :], values_ref[rows, :]
            all_logits = [
                jnp.dot(key_block, flip_ref[half, 0, :, lanes], preferred_element_type=jnp.float32)
                for lanes in groups
            ]
            all_dweights = [
                jnp.dot(
                    value_block, flip_ref[half, 1, :, lanes], preferred_element_type=jnp.float32
                )
                for lanes in groups
            ]
            following = []
            for lanes, logits, dweights, (top, total, mixed) in zip(
                groups, all_logits, all_dweights, state
            ):
                key_pos = lax.broadcasted_iota(jnp.int32, logits.shape, 0)
                live = (key_pos >= doc_start[:, lanes] - position) & (
                    key_pos <= query_pos - position
                )
                logits = jnp.where(live, logits * (scale * math.log2(math.e)), masked_value)
                new_top = jnp.maximum(top, jnp.max(logits, axis=0, keepdims=True))
                terms = jnp.exp2(logits - new_top)
                terms_ref[slot, lanes] = terms
                dweights_ref[slot, lanes] = dweights
                tops_ref[pl.ds(index, 1), lanes] = new_top
                decay = jnp.exp2(top - new_top)
                following.append(
                    (
                        new_top,
                        total * decay + jnp.sum(terms, axis=0, keepdims=True),
                        mixed * decay + jnp.sum(terms * dweights, axis=0, keepdims=True),
                    )
                )
            return tuple(following)

        zero = jnp.zeros((1, group), jnp.float32)
        empty = (jnp.full_like(zero, masked_value), zero, zero)
        sums = lax.fori_loop(0, count, sums_step, (empty,) * len(groups))
        top, total, mixed = (jnp.concatenate(part, axis=1) for part in zip(*sums))
        inverse = 1.0 / total
        delta = mixed * inverse

        def grads_step(index, carry):
            _, rows, slot = tile_rows(index)
            factor = jnp.exp2(tops_ref[pl.ds(index, 1), :] - top) * inverse
            weights = terms_ref[slot, :] * factor
            dlogits = (weights * (dweights_ref[slot, :] - delta)).astype(jnp.bfloat16)
            for lane_block in range(cols // head_width):
                dlogits_ref[half, lane_block, slot, :] = dlogits[
                    :, lane_block * head_width : (lane_block + 1) * head_width
                ]
            acc_ref[1, rows, :] += jnp.dot(
                weights.astype(jnp.bfloat16),
                stack_ref[half, 1],
                preferred_element_type=jnp.float32,
            )
            acc_ref[0, rows, :] += jnp.dot(
                dlogits, stack_ref[half, 0], preferred_element_type=jnp.float32
            )
            return carry

        lax.fori_loop(0, count, grads_step, 0)

    for piece, *place in staged_moves(
        ctx_count, dp_count, inner, part_rows, ctx_index, dp_index
    ):
        key_rows, value_rows, ordered = rows_of(*place)
        dkv_refs[piece][key_rows, :] = (scale * acc_ref[0, ordered, :]).astype(jnp.bfloat16)
        dkv_refs[piece][value_rows, :] = acc_ref[1, ordered, :].astype(jnp.bfloat16)


def query_kernel(
    ctx_count,
    tile,
    tiles_ref,
    keys_ref,
    dlogits_ref,
    passed_ref,
    dq_ref,
    same_ref,
    sum_ref,
):
    tok_rows = dq_ref.shape[0]
    head_width = keys_ref.shape[1]
    span_rows = tok_rows // 2
    scale = head_width ** (-0.5)
    same_ref[...] = passed_ref[...]
    for half in range(2):
        end = span_first(half, ctx_count, span_rows) + span_rows
        sum_ref[...] = jnp.zeros_like(sum_ref)

        def query_step(index, carry):
            rows = pl.ds(pl.multiple_of(end - index * tile, span_rows), tile)
            slot = pl.ds(pl.multiple_of(index * tile, tile), tile)
            dlogits = jnp.concatenate(
                [dlogits_ref[half, block, slot, :] for block in range(dlogits_ref.shape[1])], axis=1
            )
            sum_ref[...] += jnp.dot(
                keys_ref[rows, :].T, dlogits, preferred_element_type=jnp.float32
            )
            return carry

        lax.fori_loop(0, tile_count(tiles_ref, half), query_step, 0)
        grads = (scale * sum_ref[...]).T.astype(jnp.bfloat16)
        for head in range(dq_ref.shape[1] // head_width):
            dq_ref[
                pl.ds(half * span_rows, span_rows), pl.ds(head * head_width, head_width)
            ] = grads[head * span_rows : (head + 1) * span_rows]


def prepare(ctx_count, tile, doc_lengths, queries, out_grads, head_width, line):
    tok_rows, width = queries.shape
    cols = width // head_width * (tok_rows // 2)
    unmoved = [
        pltpu.with_memory_space_constraint(argument, pltpu.HBM)
        for argument in (doc_lengths, queries, out_grads)
    ]
    return pl.pallas_call(
        functools.partial(prepare_kernel, ctx_count, tile),
        out_shape=(
            jax.ShapeDtypeStruct((2, 2, cols, head_width), jnp.bfloat16),
            jax.ShapeDtypeStruct((2, 2, head_width, cols), jnp.bfloat16),
            jax.ShapeDtypeStruct((2, 1, cols), jnp.int32),
            jax.ShapeDtypeStruct((2, 8, 128), jnp.float32),
            jax.ShapeDtypeStruct((2, tile + ctx_count * tok_rows, head_width), jnp.float32),
            jax.ShapeDtypeStruct(line.shape, line.dtype),
        ),
        in_specs=[hbm, hbm, hbm, vmem],
        out_specs=[vmem] * 6,
        scratch_shapes=[
            pltpu.VMEM((2, tok_rows, width), jnp.bfloat16),
            pltpu.SMEM(doc_lengths.shape, jnp.int32),
            pltpu.SemaphoreType.DMA((3,)),
        ],
        compiler_params=pltpu.CompilerParams(vmem_limit_bytes=4 * 1024 * 1024),
    )(*unmoved, line)


def attend(ctx_count, dp_count, inner, tile, moves, tiles, starts, stacked, flipped, zeros, pieces):
    cols, head_width = stacked.shape[2:]
    seq = dp_count * inner * pieces[0].shape[0] // 2
    slots = -(-seq // tile)
    results = pl.pallas_call(
        functools.partial(attend_kernel, ctx_count, dp_count, inner, tile, moves),
        out_shape=[
            jax.ShapeDtypeStruct((tile + seq, head_width), jnp.bfloat16),
            jax.ShapeDtypeStruct(
                (2, cols // head_width, slots * tile, head_width), jnp.bfloat16
            ),
            jax.ShapeDtypeStruct(zeros.shape, zeros.dtype),
        ]
        + [jax.ShapeDtypeStruct(piece.shape, jnp.bfloat16) for piece in pieces],
        in_specs=[vmem] * (5 + len(pieces)),
        out_specs=[vmem] * (3 + len(pieces)),
        scratch_shapes=[
            pltpu.VMEM((tile + seq, head_width), jnp.bfloat16),
            pltpu.VMEM((slots * tile, cols), jnp.float32),
            pltpu.VMEM((slots * tile, cols), jnp.float32),
            pltpu.VMEM((slots, cols), jnp.float32),
        ],
        input_output_aliases={4: 2},
        compiler_params=pltpu.CompilerParams(vmem_limit_bytes=32 * 1024 * 1024),
    )(tiles, starts, stacked, flipped, zeros, *pieces)
    return results[0], results[1], results[3:]


def query_side(ctx_count, tile, tiles, keys_ordered, dlogits, passed, tok_rows):
    head_width = keys_ordered.shape[1]
    cols = dlogits.shape[1] * head_width
    return pl.pallas_call(
        functools.partial(query_kernel, ctx_count, tile),
        out_shape=(
            jax.ShapeDtypeStruct(
                (tok_rows, cols // (tok_rows // 2) * head_width), jnp.bfloat16
            ),
            jax.ShapeDtypeStruct(passed.shape, passed.dtype),
        ),
        in_specs=[vmem] * 4,
        out_specs=(vmem, vmem),
        scratch_shapes=[
            pltpu.VMEM((head_width, cols), jnp.float32),
        ],
        compiler_params=pltpu.CompilerParams(vmem_limit_bytes=8 * 1024 * 1024),
    )(tiles, keys_ordered, dlogits, passed)


def swap(value, axis, offset):
    pairs = [(index, index ^ offset) for index in range(lax.axis_size(axis))]
    return lax.ppermute(value, axis, pairs)


def total_of(terms):
    return sum(term.astype(jnp.float32) for term in terms).astype(jnp.bfloat16)


def staged_line(keys, values, inner, part_rows):
    head_width = keys.shape[1]
    outer = lax.axis_size("ctx") // inner
    start = lax.axis_index("dp") * part_rows
    own_keys = lax.dynamic_slice_in_dim(keys, start, part_rows, 0)
    own_values = lax.dynamic_slice_in_dim(values, start, part_rows, 0)
    zero = jnp.zeros((), keys.dtype)
    own = jnp.where(
        lax.broadcasted_iota(jnp.int32, (2 * part_rows, head_width), 0) < part_rows,
        lax.pad(own_keys, zero, ((0, part_rows, 0), (0, 0, 0))),
        lax.pad(own_values, zero, ((part_rows, 0, 0), (0, 0, 0))),
    )
    others = [swap(own, "ctx", step * inner) for step in range(1, outer)]
    return jnp.concatenate([own] + others, axis=0)


def paired_line(keys, values, inner, part_rows):
    head_width = keys.shape[1]
    lowest = jnp.array(-jnp.inf, keys.dtype)
    halves = (2, 1, part_rows, head_width)
    own = jnp.maximum(
        lax.pad(keys.reshape(halves), lowest, ((0, 0, 0), (0, 1, 0), (0, 0, 0), (0, 0, 0))),
        lax.pad(values.reshape(halves), lowest, ((0, 0, 0), (1, 0, 0), (0, 0, 0), (0, 0, 0))),
    ).reshape(4 * part_rows, head_width)
    rows = 2 * part_rows
    own_half = lax.dynamic_slice_in_dim(own, lax.axis_index("dp") * rows, rows, 0)
    pairs = [
        (2 * ctx + dp, 2 * (ctx ^ ((3 if dp else 1) * inner)) + dp)
        for ctx in range(lax.axis_size("ctx"))
        for dp in range(2)
    ]
    whole = lax.ppermute(own, ("ctx", "dp"), pairs)
    return jnp.concatenate([own_half, swap(own_half, "ctx", 2 * inner), whole], axis=0)


def body(queries, keys, values, out_grads, doc_lengths):
    ctx_count = lax.axis_size("ctx")
    dp_count = lax.axis_size("dp")
    inner = math.gcd(4, ctx_count)
    outer = ctx_count // inner
    tok_rows, head_width = keys.shape
    part_rows = tok_rows // dp_count
    tile = math.gcd(256, ctx_count * tok_rows)
    if outer == 4 and dp_count == 2:
        line = paired_line(keys, values, inner, part_rows)
        moves = functools.partial(paired_moves, inner, part_rows)
    else:
        line = staged_line(keys, values, inner, part_rows)
        moves = functools.partial(staged_moves, ctx_count, dp_count, inner, part_rows)
    plane = [line] + [swap(line, "ctx", offset) for offset in range(1, inner)]
    stacked, flipped, starts, tiles, zeros, plane[0] = prepare(
        ctx_count, tile, doc_lengths, queries, out_grads, head_width, line
    )
    pieces = plane + [
        swap(piece, "dp", offset) for offset in range(1, dp_count) for piece in plane
    ]
    keys_ordered, dlogits, parts = attend(
        ctx_count, dp_count, inner, tile, moves, tiles, starts, stacked, flipped, zeros, pieces
    )
    plane_sums = [
        total_of(
            [parts[offset]]
            + [swap(parts[far * inner + offset], "dp", far) for far in range(1, dp_count)]
        )
        for offset in range(inner)
    ]
    query_grads, plane_sums[0] = query_side(
        ctx_count, tile, tiles, keys_ordered, dlogits, plane_sums[0], tok_rows
    )
    line_sum = total_of(
        [plane_sums[0]] + [swap(plane_sums[offset], "ctx", offset) for offset in reversed(range(1, inner))]
    )
    blocks = jnp.split(line_sum, outer, axis=0)
    kv_grads = total_of(
        [blocks[0]] + [swap(blocks[block], "ctx", block * inner) for block in send_order(outer)]
    )
    return (query_grads, kv_grads[:part_rows], kv_grads[part_rows:])


def solution(mesh):
    return jax.shard_map(
        body,
        mesh=mesh,
        in_specs=(P("ctx", "dp"), P("ctx", None), P("ctx", None), P("ctx", "dp"), P()),
        out_specs=(P("ctx", "dp"), P(("ctx", "dp"), None), P(("ctx", "dp"), None)),
        check_vma=False,
    )
```

```python
import functools
import math

import jax
import jax.numpy as jnp
from jax import lax
from jax.experimental import pallas as pl
from jax.experimental.pallas import tpu as pltpu
from jax.sharding import PartitionSpec as P

masked_value = -1e30

vmem = pl.BlockSpec(memory_space=pltpu.VMEM)
smem = pl.BlockSpec(memory_space=pltpu.SMEM)
hbm = pl.BlockSpec(memory_space=pltpu.HBM)


def row_position(ctx_index, start, ctx_count, rows, span_rows):
    low = ctx_index * span_rows + start
    high = (2 * ctx_count - 1 - ctx_index) * span_rows + start - span_rows
    return pl.multiple_of(jnp.where(start < span_rows, low, high), rows)


def span_first(half, ctx_count, span_rows):
    ctx_index = lax.axis_index("ctx")
    return (ctx_index if half == 0 else 2 * ctx_count - 1 - ctx_index) * span_rows


def tile_count(tiles_ref, half):
    return jnp.max(tiles_ref[half]).astype(jnp.int32)


def prepare_kernel(
    ctx_count,
    tile,
    lengths_hbm,
    q_hbm,
    g_hbm,
    line_ref,
    stack_ref,
    flip_ref,
    starts_ref,
    tiles_ref,
    zero_ref,
    same_ref,
    raw_ref,
    lengths_ref,
    sems,
):
    tok_rows = q_hbm.shape[0]
    head_width = stack_ref.shape[3]
    cols = stack_ref.shape[2]
    span_rows = tok_rows // 2
    copies = [
        pltpu.make_async_copy(source, raw_ref.at[slot], sems.at[slot])
        for slot, source in enumerate((q_hbm, g_hbm))
    ]
    for copy in copies:
        copy.start()
    lengths_copy = pltpu.make_async_copy(lengths_hbm, lengths_ref, sems.at[2])
    lengths_copy.start()
    same_ref[...] = line_ref[...]
    zero_ref[...] = jnp.zeros_like(zero_ref)
    lengths_copy.wait()
    for half in range(2):
        first = span_first(half, ctx_count, span_rows)
        query_pos = first + lax.rem(
            lax.broadcasted_iota(jnp.int32, (1, cols), 1), jnp.int32(span_rows)
        )
        doc_start = jnp.zeros((1, cols), jnp.int32)
        first_key = jnp.int32(0)
        end = jnp.int32(0)
        for doc in range(lengths_ref.shape[0]):
            end = end + lengths_ref[doc]
            doc_start = jnp.where(query_pos >= end, end, doc_start)
            first_key = jnp.where(first >= end, end, first_key)
        starts_ref[half] = doc_start
        count = (first + span_rows - first_key + tile - 1) // tile
        tiles_ref[half] = jnp.full(tiles_ref.shape[1:], count.astype(jnp.float32))
    for slot, copy in enumerate(copies):
        copy.wait()
        for half in range(2):
            for head in range(q_hbm.shape[1] // head_width):
                stack_ref[half, slot, pl.ds(head * span_rows, span_rows), :] = raw_ref[
                    slot,
                    pl.ds(half * span_rows, span_rows),
                    pl.ds(head * head_width, head_width),
                ]
            flip_ref[half, slot] = stack_ref[half, slot].T


def staged_moves(ctx_count, dp_count, inner, part_rows, ctx_index, dp_index):
    for piece in range(dp_count * inner):
        for block in range(ctx_count // inner):
            owner = ctx_index ^ (piece % inner) ^ (block * inner)
            start = (dp_index ^ (piece // inner)) * part_rows
            yield piece, 2 * block * part_rows, owner, start


def paired_moves(inner, part_rows, ctx_index, dp_index):
    for side in range(2):
        holder = dp_index ^ side
        for offset in range(inner):
            piece, near = side * inner + offset, ctx_index ^ offset
            whole = near ^ jnp.where(holder == 1, 3 * inner, inner)
            yield piece, 0, near, holder * part_rows
            yield piece, 2 * part_rows, near ^ (2 * inner), holder * part_rows
            yield piece, 4 * part_rows, whole, 0
            yield piece, 6 * part_rows, whole, part_rows


def send_order(outer):
    return (3, 1, 2) if outer == 4 else tuple(reversed(range(1, outer)))


def attend_kernel(
    ctx_count, dp_count, inner, tile, moves, tiles_ref, starts_ref, stack_ref, flip_ref, _, *refs
):
    piece_count = dp_count * inner
    kv_refs = refs[:piece_count]
    refs = refs[piece_count:]
    keys_ref, dlogits_ref, acc_ref = refs[:3]
    dkv_refs = refs[3 : piece_count + 3]
    values_ref, terms_ref, dweights_ref, tops_ref = refs[piece_count + 3 :]
    cols, head_width = stack_ref.shape[2:]
    tok_rows = (keys_ref.shape[0] - tile) // ctx_count
    part_rows = tok_rows // dp_count
    span_rows = tok_rows // 2
    scale = head_width ** (-0.5)
    ctx_index = lax.axis_index("ctx")
    dp_index = lax.axis_index("dp")

    def rows_of(row, owner, start):
        position = row_position(owner, start, ctx_count, part_rows, span_rows)
        return (
            pl.ds(row, part_rows),
            pl.ds(row + part_rows, part_rows),
            pl.ds(tile + position, part_rows),
        )

    dead = jnp.zeros((tile, head_width), jnp.bfloat16)
    keys_ref[:tile, :] = dead
    values_ref[:tile, :] = dead
    for piece, *place in moves(ctx_index, dp_index):
        key_rows, value_rows, ordered = rows_of(*place)
        keys_ref[ordered, :] = kv_refs[piece][key_rows, :]
        values_ref[ordered, :] = kv_refs[piece][value_rows, :]
    group = min(128, cols)
    groups = [slice(start, start + group) for start in range(0, cols, group)]

    for half in range(2):
        first = span_first(half, ctx_count, span_rows)
        query_pos = first + lax.rem(
            lax.broadcasted_iota(jnp.int32, (1, group), 1), jnp.int32(span_rows)
        )
        doc_start = starts_ref[half]
        count = tile_count(tiles_ref, half)

        def tile_rows(index):
            position = first + span_rows - (index + 1) * tile
            rows = pl.ds(pl.multiple_of(tile + position, span_rows), tile)
            return position, rows, pl.ds(pl.multiple_of(index * tile, tile), tile)

        def sums_step(index, state):
            position, rows, slot = tile_rows(index)
            key_block, value_block = keys_ref[rows, :], values_ref[rows, :]
            all_logits = [
                jnp.dot(key_block, flip_ref[half, 0, :, lanes], preferred_element_type=jnp.float32)
                for lanes in groups
            ]
            all_dweights = [
                jnp.dot(
                    value_block, flip_ref[half, 1, :, lanes], preferred_element_type=jnp.float32
                )
                for lanes in groups
            ]
            following = []
            for lanes, logits, dweights, (top, total, mixed) in zip(
                groups, all_logits, all_dweights, state
            ):
                key_pos = lax.broadcasted_iota(jnp.int32, logits.shape, 0)
                live = (key_pos >= doc_start[:, lanes] - position) & (
                    key_pos <= query_pos - position
                )
                logits = jnp.where(live, logits * (scale * math.log2(math.e)), masked_value)
                new_top = jnp.maximum(top, jnp.max(logits, axis=0, keepdims=True))
                terms = jnp.exp2(logits - new_top)
                terms_ref[slot, lanes] = terms
                dweights_ref[slot, lanes] = dweights
                decay = jnp.exp2(top - new_top)
                following.append(
                    (
                        new_top,
                        total * decay + jnp.sum(terms, axis=0, keepdims=True),
                        mixed * decay + jnp.sum(terms * dweights, axis=0, keepdims=True),
                    )
                )
            tops_ref[pl.ds(index, 1), :] = jnp.concatenate([top for top, _, _ in following], axis=1)
            return tuple(following)

        zero = jnp.zeros((1, group), jnp.float32)
        empty = (jnp.full_like(zero, masked_value), zero, zero)
        sums = lax.fori_loop(0, count, sums_step, (empty,) * len(groups))
        top, total, mixed = (jnp.concatenate(part, axis=1) for part in zip(*sums))
        inverse = 1.0 / total
        delta = mixed * inverse

        def grads_step(index, carry):
            _, rows, slot = tile_rows(index)
            factor = jnp.exp2(tops_ref[pl.ds(index, 1), :] - top) * inverse
            weights = terms_ref[slot, :] * factor
            dlogits = (weights * (dweights_ref[slot, :] - delta)).astype(jnp.bfloat16)
            for lane_block in range(cols // head_width):
                dlogits_ref[half, lane_block, slot, :] = dlogits[
                    :, lane_block * head_width : (lane_block + 1) * head_width
                ]
            acc_ref[1, rows, :] += jnp.dot(
                weights.astype(jnp.bfloat16),
                stack_ref[half, 1],
                preferred_element_type=jnp.float32,
            )
            acc_ref[0, rows, :] += jnp.dot(
                dlogits, stack_ref[half, 0], preferred_element_type=jnp.float32
            )
            return carry

        lax.fori_loop(0, count, grads_step, 0)

    for piece, *place in staged_moves(
        ctx_count, dp_count, inner, part_rows, ctx_index, dp_index
    ):
        key_rows, value_rows, ordered = rows_of(*place)
        dkv_refs[piece][key_rows, :] = (scale * acc_ref[0, ordered, :]).astype(jnp.bfloat16)
        dkv_refs[piece][value_rows, :] = acc_ref[1, ordered, :].astype(jnp.bfloat16)


def query_kernel(
    ctx_count,
    tile,
    tiles_ref,
    keys_ref,
    dlogits_ref,
    passed_ref,
    dq_ref,
    same_ref,
    sum_ref,
):
    tok_rows = dq_ref.shape[0]
    head_width = keys_ref.shape[1]
    span_rows = tok_rows // 2
    scale = head_width ** (-0.5)
    same_ref[...] = passed_ref[...]
    for half in range(2):
        end = span_first(half, ctx_count, span_rows) + span_rows
        sum_ref[...] = jnp.zeros_like(sum_ref)

        def query_step(index, carry):
            rows = pl.ds(pl.multiple_of(end - index * tile, span_rows), tile)
            slot = pl.ds(pl.multiple_of(index * tile, tile), tile)
            dlogits = jnp.concatenate(
                [dlogits_ref[half, block, slot, :] for block in range(dlogits_ref.shape[1])], axis=1
            )
            sum_ref[...] += jnp.dot(
                keys_ref[rows, :].T, dlogits, preferred_element_type=jnp.float32
            )
            return carry

        lax.fori_loop(0, tile_count(tiles_ref, half), query_step, 0)
        grads = (scale * sum_ref[...]).T.astype(jnp.bfloat16)
        for head in range(dq_ref.shape[1] // head_width):
            dq_ref[
                pl.ds(half * span_rows, span_rows), pl.ds(head * head_width, head_width)
            ] = grads[head * span_rows : (head + 1) * span_rows]


def prepare(ctx_count, tile, doc_lengths, queries, out_grads, head_width, line):
    tok_rows, width = queries.shape
    cols = width // head_width * (tok_rows // 2)
    unmoved = [
        pltpu.with_memory_space_constraint(argument, pltpu.HBM)
        for argument in (doc_lengths, queries, out_grads)
    ]
    return pl.pallas_call(
        functools.partial(prepare_kernel, ctx_count, tile),
        out_shape=(
            jax.ShapeDtypeStruct((2, 2, cols, head_width), jnp.bfloat16),
            jax.ShapeDtypeStruct((2, 2, head_width, cols), jnp.bfloat16),
            jax.ShapeDtypeStruct((2, 1, cols), jnp.int32),
            jax.ShapeDtypeStruct((2, 8, 128), jnp.float32),
            jax.ShapeDtypeStruct((2, tile + ctx_count * tok_rows, head_width), jnp.float32),
            jax.ShapeDtypeStruct(line.shape, line.dtype),
        ),
        in_specs=[hbm, hbm, hbm, vmem],
        out_specs=[vmem] * 6,
        scratch_shapes=[
            pltpu.VMEM((2, tok_rows, width), jnp.bfloat16),
            pltpu.SMEM(doc_lengths.shape, jnp.int32),
            pltpu.SemaphoreType.DMA((3,)),
        ],
        compiler_params=pltpu.CompilerParams(vmem_limit_bytes=4 * 1024 * 1024),
    )(*unmoved, line)


def attend(ctx_count, dp_count, inner, tile, moves, tiles, starts, stacked, flipped, zeros, pieces):
    cols, head_width = stacked.shape[2:]
    seq = dp_count * inner * pieces[0].shape[0] // 2
    slots = -(-seq // tile)
    results = pl.pallas_call(
        functools.partial(attend_kernel, ctx_count, dp_count, inner, tile, moves),
        out_shape=[
            jax.ShapeDtypeStruct((tile + seq, head_width), jnp.bfloat16),
            jax.ShapeDtypeStruct(
                (2, cols // head_width, slots * tile, head_width), jnp.bfloat16
            ),
            jax.ShapeDtypeStruct(zeros.shape, zeros.dtype),
        ]
        + [jax.ShapeDtypeStruct(piece.shape, jnp.bfloat16) for piece in pieces],
        in_specs=[vmem] * (5 + len(pieces)),
        out_specs=[vmem] * (3 + len(pieces)),
        scratch_shapes=[
            pltpu.VMEM((tile + seq, head_width), jnp.bfloat16),
            pltpu.VMEM((slots * tile, cols), jnp.float32),
            pltpu.VMEM((slots * tile, cols), jnp.float32),
            pltpu.VMEM((slots, cols), jnp.float32),
        ],
        input_output_aliases={4: 2},
        compiler_params=pltpu.CompilerParams(vmem_limit_bytes=32 * 1024 * 1024),
    )(tiles, starts, stacked, flipped, zeros, *pieces)
    return results[0], results[1], results[3:]


def query_side(ctx_count, tile, tiles, keys_ordered, dlogits, passed, tok_rows):
    head_width = keys_ordered.shape[1]
    cols = dlogits.shape[1] * head_width
    return pl.pallas_call(
        functools.partial(query_kernel, ctx_count, tile),
        out_shape=(
            jax.ShapeDtypeStruct(
                (tok_rows, cols // (tok_rows // 2) * head_width), jnp.bfloat16
            ),
            jax.ShapeDtypeStruct(passed.shape, passed.dtype),
        ),
        in_specs=[vmem] * 4,
        out_specs=(vmem, vmem),
        scratch_shapes=[
            pltpu.VMEM((head_width, cols), jnp.float32),
        ],
        compiler_params=pltpu.CompilerParams(vmem_limit_bytes=8 * 1024 * 1024),
    )(tiles, keys_ordered, dlogits, passed)


def swap(value, axis, offset):
    pairs = [(index, index ^ offset) for index in range(lax.axis_size(axis))]
    return lax.ppermute(value, axis, pairs)


def total_of(terms):
    return sum(term.astype(jnp.float32) for term in terms).astype(jnp.bfloat16)


def staged_line(keys, values, inner, part_rows):
    head_width = keys.shape[1]
    outer = lax.axis_size("ctx") // inner
    start = lax.axis_index("dp") * part_rows
    own_keys = lax.dynamic_slice_in_dim(keys, start, part_rows, 0)
    own_values = lax.dynamic_slice_in_dim(values, start, part_rows, 0)
    zero = jnp.zeros((), keys.dtype)
    own = jnp.where(
        lax.broadcasted_iota(jnp.int32, (2 * part_rows, head_width), 0) < part_rows,
        lax.pad(own_keys, zero, ((0, part_rows, 0), (0, 0, 0))),
        lax.pad(own_values, zero, ((part_rows, 0, 0), (0, 0, 0))),
    )
    others = [swap(own, "ctx", step * inner) for step in range(1, outer)]
    return jnp.concatenate([own] + others, axis=0)


def paired_line(keys, values, inner, part_rows):
    head_width = keys.shape[1]
    lowest = jnp.array(-jnp.inf, keys.dtype)
    halves = (2, 1, part_rows, head_width)
    own = jnp.maximum(
        lax.pad(keys.reshape(halves), lowest, ((0, 0, 0), (0, 1, 0), (0, 0, 0), (0, 0, 0))),
        lax.pad(values.reshape(halves), lowest, ((0, 0, 0), (1, 0, 0), (0, 0, 0), (0, 0, 0))),
    ).reshape(4 * part_rows, head_width)
    rows = 2 * part_rows
    own_half = lax.dynamic_slice_in_dim(own, lax.axis_index("dp") * rows, rows, 0)
    pairs = [
        (2 * ctx + dp, 2 * (ctx ^ ((3 if dp else 1) * inner)) + dp)
        for ctx in range(lax.axis_size("ctx"))
        for dp in range(2)
    ]
    whole = lax.ppermute(own, ("ctx", "dp"), pairs)
    return jnp.concatenate([own_half, swap(own_half, "ctx", 2 * inner), whole], axis=0)


def body(queries, keys, values, out_grads, doc_lengths):
    ctx_count = lax.axis_size("ctx")
    dp_count = lax.axis_size("dp")
    inner = math.gcd(4, ctx_count)
    outer = ctx_count // inner
    tok_rows, head_width = keys.shape
    part_rows = tok_rows // dp_count
    tile = math.gcd(256, ctx_count * tok_rows)
    if outer == 4 and dp_count == 2:
        line = paired_line(keys, values, inner, part_rows)
        moves = functools.partial(paired_moves, inner, part_rows)
    else:
        line = staged_line(keys, values, inner, part_rows)
        moves = functools.partial(staged_moves, ctx_count, dp_count, inner, part_rows)
    plane = [line] + [swap(line, "ctx", offset) for offset in range(1, inner)]
    stacked, flipped, starts, tiles, zeros, plane[0] = prepare(
        ctx_count, tile, doc_lengths, queries, out_grads, head_width, line
    )
    pieces = plane + [
        swap(piece, "dp", offset) for offset in range(1, dp_count) for piece in plane
    ]
    keys_ordered, dlogits, parts = attend(
        ctx_count, dp_count, inner, tile, moves, tiles, starts, stacked, flipped, zeros, pieces
    )
    plane_sums = [
        total_of(
            [parts[offset]]
            + [swap(parts[far * inner + offset], "dp", far) for far in range(1, dp_count)]
        )
        for offset in range(inner)
    ]
    query_grads, plane_sums[0] = query_side(
        ctx_count, tile, tiles, keys_ordered, dlogits, plane_sums[0], tok_rows
    )
    line_sum = total_of(
        [plane_sums[0]] + [swap(plane_sums[offset], "ctx", offset) for offset in reversed(range(1, inner))]
    )
    blocks = jnp.split(line_sum, outer, axis=0)
    kv_grads = total_of(
        [blocks[0]] + [swap(blocks[block], "ctx", block * inner) for block in send_order(outer)]
    )
    return (query_grads, kv_grads[:part_rows], kv_grads[part_rows:])


def solution(mesh):
    return jax.shard_map(
        body,
        mesh=mesh,
        in_specs=(P("ctx", "dp"), P("ctx", None), P("ctx", None), P("ctx", "dp"), P()),
        out_specs=(P("ctx", "dp"), P(("ctx", "dp"), None), P(("ctx", "dp"), None)),
        check_vma=False,
    )
```
